256 devices in a mesh: section: 2 (over core), tp: 16 (over x, y), dp: 8 (over z).
Axes of the slice: x: 4, y: 4, z: 8, core: 2. Of those that a mesh axis runs over, the one named last changes fastest.
Arguments:
- x_prefill: bfloat16 [4096, 8192], P(('section', 'dp'), 'tp'), as said below
- x_decode: bfloat16 [3, 1024, 8192], P(None, ('section', 'dp'), 'tp'), as said below
- w_query: bfloat16 [8192, 8192], P(('section', 'dp'), 'tp'), may hold values from -0.0625 to 0.0625
- w_keyval: bfloat16 [8192, 2048], P(('section', 'dp'), 'tp'), may hold values from -0.0625 to 0.0625
- w_out: bfloat16 [8192, 8192], P('tp', ('section', 'dp')), may hold values from -0.0625 to 0.0625
- cache_pool: bfloat16 [16, 256, 128, 256], P('tp', ('section', 'dp')), as said below
- placement: int32 [32, 2], replicated, may hold values from 0 to 31, as said below
- page_table: int32 [1024, 8], P(('section', 'dp')), may hold values from 0 to 31, as said below
- cache_len: int32 [1024], P(('section', 'dp')), may hold values from 1 to 1024
Outputs:
- prefill_out: bfloat16 [4096, 8192], P(('section', 'dp'), 'tp')
- decode_out: bfloat16 [3, 1024, 8192], P(None, ('section', 'dp'), 'tp')
The draws below stay inside these ranges and needn't reach their ends.
Inputs may be any that keep to these rules, and one draw needn't show every extreme that they name: `placement`: no two rows name the same group and slot id; column 0 is a group below 16, column 1 a slot id below 32. `page_table`: column j of every row names a slot id whose lane, id // 16, equals j % 2; requests may share pages. `x_prefill`: entries are real numbers of moderate size. `x_decode`: entries are real numbers of moderate size. `cache_pool`: entries are real numbers of moderate size.
All inputs are finite; a program needn't handle non-finite values.
Results may differ from the reference program's by a relative error of at most 0.03.
Values may be sent and summed in bfloat16 or wider, within the bound.
No kernel may reach another device: no remote copies, remote signals or barrier semaphores. Data moves between devices by JAX's collectives and lax.ppermute only.
A program may use at most 128 MiB of HBM per device.

```python
import math
import jax
import jax.numpy as jnp
from jax import lax

D = 8192
QH = 64
KVH = 8
HD = 128
PAGE = 128
STEPS = 3
MAXP = 8
REQ_DEV = 64
POOL_DEV = 16
NG = 16
SEQ = 4096
NBLK = 32
REQ = 1024
KV_DEV = 1
KVP = 2
GS = 8
KVW = 256
POOL_ROWS = 256
N_TP = 16


def draw_x_prefill(key, part):
    key = jax.random.fold_in(key, 11)
    values = jax.random.normal(key, (SEQ, D), jnp.float32)
    return values.astype(jnp.bfloat16)


def draw_x_decode(key, part):
    key = jax.random.fold_in(key, 12)
    values = jax.random.normal(key, (STEPS, REQ, D), jnp.float32)
    return values.astype(jnp.bfloat16)


def draw_cache_pool(key, part):
    key = jax.random.fold_in(key, 13)
    values = jax.random.normal(key, (N_TP, POOL_ROWS, PAGE, KVW), jnp.float32)
    return values.astype(jnp.bfloat16)


def draw_placement(key, part):
    key = jax.random.fold_in(key, 21)
    chosen = jax.random.permutation(key, NG * KVP * POOL_DEV)[:NBLK]
    owner = chosen // (KVP * POOL_DEV)
    target = chosen % (KVP * POOL_DEV)
    return jnp.stack([owner, target], axis=1).astype(jnp.int32)


def draw_page_table(key, part):
    key = jax.random.fold_in(key, 22)
    slots = jax.random.randint(key, (REQ, MAXP), 0, POOL_DEV)
    lanes = jnp.arange(MAXP) % KVP
    return (lanes[None, :] * POOL_DEV + slots).astype(jnp.int32)


def draw_cache_len(key, part):
    key = jax.random.fold_in(key, 23)
    lengths = jax.random.randint(key, (REQ,), 1, MAXP * PAGE + 1)
    return lengths.at[0].set(MAXP * PAGE).astype(jnp.int32)


def block_scale(stream_key, shape, cuts, smallest, top_value):
    level, own = 1.0, jax.random.fold_in(stream_key, 6)
    for dim, blocks in cuts:
        draws = jnp.exp(jax.random.uniform(jax.random.fold_in(own, dim), (blocks,), jnp.float32, smallest / len(cuts), top_value / len(cuts)))
        level = level * jnp.repeat(draws, shape[dim] // blocks).reshape([-1 if axis == dim else 1 for axis in range(len(shape))])
    return level


def scatter_about(rng, dims, spread, limit, split=(), held_as=jnp.bfloat16):
    level = block_scale(rng, dims, split, -0.22, 0.18) if split else 1.0
    result = jax.random.normal(rng, dims, jnp.float32) * spread * level
    return jnp.minimum(jnp.maximum(result, -limit), limit).astype(held_as)


def setup_inputs(seed: int = 0) -> dict:
    keys = jax.random.split(jax.random.key(seed), 10)
    x_prefill = draw_x_prefill(jax.random.fold_in(keys[9], 71), 0)
    x_decode = draw_x_decode(jax.random.fold_in(keys[9], 71), 0)
    w_query = scatter_about(keys[2], (D, QH * HD), D ** -0.5, 0.0625, ((0, 16), (1, 16)))
    w_keyval = scatter_about(keys[3], (D, 2 * KVH * HD), D ** -0.5, 0.0625, ((0, 16), (1, 16)))
    w_out = scatter_about(keys[4], (QH * HD, D), (QH * HD) ** -0.5, 0.0625, ((0, 16), (1, 16)))
    cache_pool = draw_cache_pool(jax.random.fold_in(keys[9], 71), 0)
    placement = draw_placement(jax.random.fold_in(keys[9], 71), 0)
    page_table = draw_page_table(jax.random.fold_in(keys[9], 71), 0)
    cache_len = draw_cache_len(jax.random.fold_in(keys[9], 71), 0)
    return {"x_prefill": x_prefill, "x_decode": x_decode, "w_query": w_query, "w_keyval": w_keyval, "w_out": w_out, "cache_pool": cache_pool, "placement": placement, "page_table": page_table, "cache_len": cache_len}


NEG = -1e+30

def prefill_attention(query, keyval, scale):
    queries = query.reshape(SEQ, KVH, GS, HD)
    pairs = keyval.reshape(SEQ, KVH, 2, HD)
    block = math.gcd(SEQ, 512)

    def per_head(head):
        q_head = lax.dynamic_index_in_dim(queries, head, 1, keepdims=False).astype(jnp.float32)
        kv_head = lax.dynamic_index_in_dim(pairs, head, 1, keepdims=False).astype(jnp.float32)
        k_head = kv_head[:, 0]
        v_head = kv_head[:, 1]

        def per_block(index):
            start = index * block
            rows = lax.dynamic_slice_in_dim(q_head, start, block, 0)
            scores = jnp.einsum('qgd,kd->qgk', rows, k_head) * scale
            qpos = start + jnp.arange(block, dtype=jnp.int32)
            kpos = jnp.arange(SEQ, dtype=jnp.int32)
            causal = (kpos[None, :] <= qpos[:, None])[:, None, :]
            scores = jnp.where(causal, scores, NEG)
            top = lax.optimization_barrier(jnp.max(scores, axis=-1, keepdims=True))
            probs = jnp.exp(scores - top) * causal
            total = lax.optimization_barrier(jnp.sum(probs, axis=-1, keepdims=True))
            out = jnp.einsum('qgk,kd->qgd', probs, v_head) / total
            return out.astype(jnp.bfloat16)
        outs = lax.map(per_block, jnp.arange(SEQ // block, dtype=jnp.int32))
        return outs.reshape(SEQ, GS, HD)
    heads = lax.map(per_head, jnp.arange(KVH, dtype=jnp.int32))
    return jnp.transpose(heads, (1, 0, 2, 3)).reshape(SEQ, QH * HD)

def handoff(keyval, cache_pool, placement):
    groups = N_TP // KVP
    blocks = keyval.reshape(NBLK, PAGE, groups, KVW)
    owner = placement[:, 0]
    target = placement[:, 1]
    lane = target // POOL_DEV
    row = owner * POOL_DEV + target % POOL_DEV
    pages = []
    for shard in range(N_TP):
        where_to = jnp.where(lane == shard % KVP, row, POOL_ROWS)
        pages.append(cache_pool[shard].at[where_to].set(blocks[:, :, shard // KVP], mode='drop'))
    return jnp.stack(pages)

def decode_attention(q_dec, kv_dec, pool, page_table, cache_len, scale):
    groups = N_TP // KVP
    queries = q_dec.reshape(STEPS, REQ, groups, KV_DEV, GS, HD)
    fresh = kv_dec.reshape(STEPS, REQ, groups, KV_DEV, 2, HD)
    rblock = math.gcd(REQ, 64)
    lanes = jnp.arange(MAXP, dtype=jnp.int32) % KVP
    step_ids = jnp.arange(STEPS, dtype=jnp.int32)
    new_mask = (step_ids[None, :] <= step_ids[:, None])[:, None, None, None, :]

    def per_group(group):
        cache_group = lax.dynamic_slice_in_dim(pool, group * KVP, KVP, 0)
        q_group = lax.dynamic_index_in_dim(queries, group, 2, keepdims=False)
        kv_group = lax.dynamic_index_in_dim(fresh, group, 2, keepdims=False)

        def per_block(index):
            start = index * rblock
            rows = start + jnp.arange(rblock, dtype=jnp.int32)
            table = lax.dynamic_slice_in_dim(page_table, start, rblock, 0)
            lengths = lax.dynamic_slice_in_dim(cache_len, start, rblock, 0)
            slot_rows = (rows // REQ_DEV)[:, None] * POOL_DEV + table % POOL_DEV
            pages = cache_group[lanes[None, :], slot_rows]
            pages = pages.reshape(rblock, MAXP * PAGE, KV_DEV, 2, HD).astype(jnp.float32)
            q_rows = lax.dynamic_slice_in_dim(q_group, start, rblock, 1).astype(jnp.float32)
            new_rows = lax.dynamic_slice_in_dim(kv_group, start, rblock, 1).astype(jnp.float32)
            pos = jnp.arange(MAXP * PAGE, dtype=jnp.int32)
            cache_mask = (pos[None, :] < lengths[:, None])[None, :, None, None, :]
            score_cache = jnp.einsum('srabd,rkad->srabk', q_rows, pages[:, :, :, 0]) * scale
            score_new = jnp.einsum('srabd,trad->srabt', q_rows, new_rows[:, :, :, 0]) * scale
            score_cache = jnp.where(cache_mask, score_cache, NEG)
            score_new = jnp.where(new_mask, score_new, NEG)
            top = jnp.maximum(lax.optimization_barrier(jnp.max(score_cache, axis=-1)), lax.optimization_barrier(jnp.max(score_new, axis=-1)))[..., None]
            prob_cache = jnp.exp(score_cache - top) * cache_mask
            prob_new = jnp.exp(score_new - top) * new_mask
            total = lax.optimization_barrier(jnp.sum(prob_cache, axis=-1)) + lax.optimization_barrier(jnp.sum(prob_new, axis=-1))
            out = jnp.einsum('srabk,rkad->srabd', prob_cache, pages[:, :, :, 1])
            out = out + jnp.einsum('srabt,trad->srabd', prob_new, new_rows[:, :, :, 1])
            return (out / total[..., None]).astype(jnp.bfloat16)
        outs = lax.map(per_block, jnp.arange(REQ // rblock, dtype=jnp.int32))
        return jnp.transpose(outs, (1, 0, 2, 3, 4, 5)).reshape(STEPS, REQ, KV_DEV, GS, HD)
    heads = lax.map(per_group, jnp.arange(groups, dtype=jnp.int32))
    return jnp.transpose(heads, (1, 2, 0, 3, 4, 5)).reshape(STEPS * REQ, QH * HD)

def reference(x_prefill, x_decode, w_query, w_keyval, w_out, cache_pool, placement, page_table, cache_len):
    scale = 1.0 / math.sqrt(HD)
    query = jnp.dot(x_prefill, w_query, preferred_element_type=jnp.float32).astype(jnp.bfloat16)
    keyval = jnp.dot(x_prefill, w_keyval, preferred_element_type=jnp.float32).astype(jnp.bfloat16)
    prefill_out = prefill_attention(query, keyval, scale)
    pool = handoff(keyval, cache_pool, placement)
    rows = x_decode.reshape(STEPS * REQ, D)
    q_dec = jnp.dot(rows, w_query, preferred_element_type=jnp.float32).astype(jnp.bfloat16)
    kv_dec = jnp.dot(rows, w_keyval, preferred_element_type=jnp.float32).astype(jnp.bfloat16)
    attention = decode_attention(q_dec, kv_dec, pool, page_table, cache_len, scale)
    width = QH * HD // N_TP
    summed = jnp.zeros((STEPS * REQ, D), jnp.float32)
    for shard in range(N_TP):
        part = jnp.dot(attention[:, shard * width:(shard + 1) * width], w_out[shard * width:(shard + 1) * width], preferred_element_type=jnp.float32)
        summed = summed + lax.optimization_barrier(part.astype(jnp.bfloat16)).astype(jnp.float32)
    decode_out = summed.astype(jnp.bfloat16).reshape(STEPS, REQ, D)
    return (prefill_out, decode_out)
```

```python
import math

import jax
import jax.numpy as jnp
from jax import lax
from jax.experimental import pallas as pl
from jax.experimental.pallas import tpu as pltpu
from jax.sharding import PartitionSpec as P

HD = 128
PAGE = 128
NEG = -1e30
SCALE = 1.0 / math.sqrt(HD)
VMEM_LIMIT = 48 * 1024 * 1024

ST = ("section", "tp")


def tp_perm(dx, dy, by_section):
    pairs = []
    for s in range(2):
        d = -1 if (by_section and s == 1) else 1
        for x in range(4):
            for y in range(4):
                to = ((x + d * dx) % 4) * 4 + (y + d * dy) % 4
                pairs.append((s * 16 + x * 4 + y, s * 16 + to))
    return pairs


RING_X = tp_perm(1, 0, True)
RING_Y = tp_perm(0, 1, True)
SWAP = [(0, 1), (1, 0)]
LANE = [(t, t ^ 1) for t in range(16)]
UP = [(z, (z + 1) % 8) for z in range(8)]
DOWN = [(z, (z - 1) % 8) for z in range(8)]


def gather_tp(first, second):
    a, b = [first], [second]
    for _ in range(3):
        a.append(lax.ppermute(a[-1], ST, RING_Y))
        b.append(lax.ppermute(b[-1], ST, RING_X))
    a, b = [jnp.stack(a)], [jnp.stack(b)]
    for _ in range(3):
        a.append(lax.ppermute(a[-1], ST, RING_X))
        b.append(lax.ppermute(b[-1], ST, RING_Y))
    return a + b


def gather_groups(value):
    up, down = [value], [value]
    for _ in range(3):
        up.append(lax.ppermute(up[-1], "dp", UP))
        down.append(lax.ppermute(down[-1], "dp", DOWN))
    up.append(lax.ppermute(up[-1], "dp", UP))
    own = jnp.stack(up + [down[3], down[2], down[1]])
    return own, lax.ppermute(own, "section", SWAP)


def project_kernel(order, *refs):
    a, b, w, out, held, sems = refs[:4], refs[4:8], refs[8], refs[9], refs[10], refs[11]
    copies = []
    for n in range(16):
        copy = pltpu.make_async_copy(w.at[order[n]], held.at[n], sems.at[n])
        copy.start()
        copies.append(copy)
    total = None
    for n in range(16):
        i, j = n // 4, n % 4
        rows = jnp.concatenate([a[i][j], b[j][i]], axis=0)
        copies[n].wait()
        part = jnp.dot(rows, held[n], preferred_element_type=jnp.float32)
        total = part if total is None else total + part
    out[...] = total.astype(out.dtype)


def project(order, blocks, w):
    rows = blocks[0].shape[1] + blocks[4].shape[1]
    depth, cols = w.shape[1:]
    vmem = pl.BlockSpec(memory_space=pltpu.VMEM)
    return pl.pallas_call(
        project_kernel,
        out_shape=jax.ShapeDtypeStruct((rows, cols), jnp.bfloat16),
        in_specs=[pl.BlockSpec(memory_space=pltpu.SMEM)]
        + [vmem] * 8
        + [pl.BlockSpec(memory_space=pl.ANY)],
        out_specs=vmem,
        scratch_shapes=[
            pltpu.VMEM((16, depth, cols), jnp.bfloat16),
            pltpu.SemaphoreType.DMA((16,)),
        ],
        compiler_params=pltpu.CompilerParams(vmem_limit_bytes=VMEM_LIMIT),
        cost_estimate=pl.CostEstimate(
            flops=2 * rows * 16 * depth * cols,
            bytes_accessed=2 * 16 * depth * (rows + cols),
            transcendentals=0,
        ),
        name="project",
    )(order, *blocks, w)


def dot_t(a, b):
    return lax.dot_general(a, b, (((1,), (1,)), ((), ())), preferred_element_type=jnp.float32)


def block_place(info, group):
    section, plane = lax.div(group, 8), lax.rem(group, 8)
    return jnp.where(section == info[1], 0, 8) + lax.rem(info[2] - plane + 8, 8)


def prefill_kernel(info, q, kv_own, kv_other, out, qs, ms, ls, acc):
    tokens = q.shape[0]
    heads = q.shape[1] // HD
    for h in range(heads):
        qs[h * tokens : (h + 1) * tokens, :] = q[:, h * HD : (h + 1) * HD]
    group = info[0]
    rows = heads * tokens

    def step(kv, place, diagonal):
        scores = dot_t(qs[...], kv[place, 0]) * SCALE
        if diagonal:
            row = lax.broadcasted_iota(jnp.int32, (heads, tokens, tokens), 1)
            col = lax.broadcasted_iota(jnp.int32, (heads, tokens, tokens), 2)
            scores = jnp.where((col <= row).reshape(rows, tokens), scores, NEG)
            top = jnp.max(scores, axis=-1, keepdims=True)
            probs = jnp.exp(scores - top)
            ms[...] = top
            ls[...] = jnp.sum(probs, axis=-1, keepdims=True)
            acc[...] = jnp.dot(
                probs.astype(jnp.bfloat16), kv[place, 1], preferred_element_type=jnp.float32
            )
        else:
            old = ms[...]
            top = jnp.maximum(old, jnp.max(scores, axis=-1, keepdims=True))
            probs = jnp.exp(scores - top)
            keep = jnp.exp(old - top)
            ms[...] = top
            ls[...] = ls[...] * keep + jnp.sum(probs, axis=-1, keepdims=True)
            acc[...] = acc[...] * keep + jnp.dot(
                probs.astype(jnp.bfloat16), kv[place, 1], preferred_element_type=jnp.float32
            )

    step(kv_own, 0, True)

    @pl.loop(0, group)
    def _(other):
        section, plane = lax.div(other, 8), lax.rem(other, 8)
        place = lax.rem(info[2] - plane + 8, 8)

        @pl.when(section == info[1])
        def _():
            step(kv_own, place, False)

        @pl.when(section != info[1])
        def _():
            step(kv_other, place, False)

    result = acc[...] / ls[...]
    for h in range(heads):
        out[:, h * HD : (h + 1) * HD] = result[h * tokens : (h + 1) * tokens].astype(out.dtype)


def prefill_attention(info, q, kv_own, kv_other):
    tokens, cols = q.shape
    rows = tokens * (cols // HD)
    vmem = pl.BlockSpec(memory_space=pltpu.VMEM)
    return pl.pallas_call(
        prefill_kernel,
        out_shape=jax.ShapeDtypeStruct(q.shape, jnp.bfloat16),
        in_specs=[pl.BlockSpec(memory_space=pltpu.SMEM)] + [vmem] * 3,
        out_specs=vmem,
        scratch_shapes=[
            pltpu.VMEM((rows, HD), jnp.bfloat16),
            pltpu.VMEM((rows, 1), jnp.float32),
            pltpu.VMEM((rows, 1), jnp.float32),
            pltpu.VMEM((rows, HD), jnp.float32),
        ],
        compiler_params=pltpu.CompilerParams(vmem_limit_bytes=VMEM_LIMIT),
        cost_estimate=pl.CostEstimate(
            flops=4 * rows * 4096 * HD, bytes_accessed=3 << 20, transcendentals=rows * 4096
        ),
        name="prefill_attention",
    )(info, q, kv_own, kv_other)


def decode_kernel(
    info, placement, q, keys, values, table, lens, mine, other, kv_own, kv_other, out, ks, vs, bias
):
    slots = mine.shape[0]
    requests, pages = table.shape
    steps = q.shape[0] // requests
    heads = q.shape[1] // HD
    lane = info[3]
    for pool, first in ((mine, lane * slots), (other, (1 - lane) * slots)):
        for i in range(slots):
            ks[first + i] = pool[i, :, :HD]
            vs[first + i] = pool[i, :, HD:]

    @pl.loop(0, placement.shape[0])
    def _(block):
        @pl.when(placement[block, 0] == info[0])
        def _():
            target = placement[block, 1]
            group, half = lax.div(block, 2), lax.rem(block, 2)
            section, plane = lax.div(group, 8), lax.rem(group, 8)
            place = lax.rem(info[2] - plane + 8, 8)
            rows = pl.ds(pl.multiple_of(half * PAGE, PAGE), PAGE)

            @pl.when(section == info[1])
            def _():
                ks[target] = kv_own[place, 0, rows, :]
                vs[target] = kv_own[place, 1, rows, :]

            @pl.when(section != info[1])
            def _():
                ks[target] = kv_other[place, 0, rows, :]
                vs[target] = kv_other[place, 1, rows, :]

    offset = lax.broadcasted_iota(jnp.int32, (requests, PAGE), 1)
    length = jnp.broadcast_to(lens[...], (requests, PAGE))
    named = []
    for j in range(pages):
        slot = jnp.broadcast_to(table[:, j : j + 1], (requests, PAGE))
        named.append(jnp.where(offset + j * PAGE < length, slot, -1))
    for slot in range(2 * slots):
        count = jnp.zeros((requests, PAGE), jnp.float32)
        for j in range(slot // slots, pages, 2):
            count = count + jnp.where(named[j] == slot, 1.0, 0.0)
        bias[:, slot * PAGE : (slot + 1) * PAGE] = jnp.where(
            count > 0, jnp.log(jnp.maximum(count, 1.0)), NEG
        )

    chunk = 8
    for step in range(steps):
        q_rows = q[step * requests : (step + 1) * requests, :]
        stacked = jnp.concatenate([q_rows[:, h * HD : (h + 1) * HD] for h in range(heads)], axis=0)
        wide = stacked.astype(jnp.float32).reshape(heads, requests, HD)
        fresh = []
        for t in range(step + 1):
            key = keys[t * requests : (t + 1) * requests, :].astype(jnp.float32)
            fresh.append(jnp.sum(wide * key[None], axis=-1, keepdims=True) * SCALE)
        top = fresh[0]
        for score in fresh[1:]:
            top = jnp.maximum(top, score)
        total = jnp.zeros((heads, requests, 1), jnp.float32)
        weighted = jnp.zeros((heads, requests, HD), jnp.float32)
        for t, score in enumerate(fresh):
            prob = jnp.exp(score - top)
            value = values[t * requests : (t + 1) * requests, :].astype(jnp.float32)
            total = total + prob
            weighted = weighted + prob * value[None]
        for first in range(0, 2 * slots, chunk):
            width = chunk * PAGE
            k = ks[first : first + chunk].reshape(width, HD)
            v = vs[first : first + chunk].reshape(width, HD)
            scores = dot_t(stacked, k).reshape(heads, requests, width) * SCALE
            scores = scores + bias[:, first * PAGE : first * PAGE + width][None]
            new_top = jnp.maximum(top, jnp.max(scores, axis=-1, keepdims=True))
            probs = jnp.exp(scores - new_top)
            keep = jnp.exp(top - new_top)
            total = total * keep + jnp.sum(probs, axis=-1, keepdims=True)
            update = jnp.dot(
                probs.reshape(heads * requests, width).astype(jnp.bfloat16),
                v,
                preferred_element_type=jnp.float32,
            )
            weighted = weighted * keep + update.reshape(heads, requests, HD)
            top = new_top
        result = (weighted / total).astype(out.dtype)
        for h in range(heads):
            out[step * requests : (step + 1) * requests, h * HD : (h + 1) * HD] = result[h]


def decode_attention(info, placement, q, keys, values, table, lens, mine, other, kv_own, kv_other):
    slots = mine.shape[0]
    requests = table.shape[0]
    vmem = pl.BlockSpec(memory_space=pltpu.VMEM)
    smem = pl.BlockSpec(memory_space=pltpu.SMEM)
    return pl.pallas_call(
        decode_kernel,
        out_shape=jax.ShapeDtypeStruct(q.shape, jnp.bfloat16),
        in_specs=[smem, smem] + [vmem] * 9,
        out_specs=vmem,
        scratch_shapes=[
            pltpu.VMEM((2 * slots, PAGE, HD), jnp.bfloat16),
            pltpu.VMEM((2 * slots, PAGE, HD), jnp.bfloat16),
            pltpu.VMEM((requests, 2 * slots * PAGE), jnp.float32),
        ],
        compiler_params=pltpu.CompilerParams(vmem_limit_bytes=VMEM_LIMIT),
        cost_estimate=pl.CostEstimate(
            flops=4 * 768 * 4096 * HD, bytes_accessed=5 << 20, transcendentals=768 * 4096
        ),
        name="decode_attention",
    )(info, placement, q, keys, values, table, lens, mine, other, kv_own, kv_other)


def add_up(parts):
    total = parts[0].astype(jnp.float32)
    for part in parts[1:]:
        total = total + part.astype(jnp.float32)
    return total.astype(jnp.bfloat16)


def scatter_tp(summands, x, y):
    rows, cols = summands.shape
    width = cols // 16
    half = rows // 2
    first = summands[:half].reshape(half, 4, 4, width)
    second = summands[half:].reshape(half, 4, 4, width)

    def phase(value, axis, at, along):
        def part(k):
            return lax.dynamic_index_in_dim(value, lax.rem(at + k, 4), axis, keepdims=False)

        parts = [part(0)]
        for k in (2, 1, 3):
            pairs = tp_perm(k, 0, False) if along == "x" else tp_perm(0, k, False)
            parts.append(lax.ppermute(part(k), ST, pairs))
        return parts

    first, second = phase(first, 1, x, "x"), phase(second, 2, y, "y")
    first, second = add_up(first), add_up(second)
    first, second = phase(first, 1, y, "y"), phase(second, 1, x, "x")
    return jnp.concatenate([add_up(first), add_up(second)], axis=0)


def on_device(
    x_prefill, x_decode, w_query, w_keyval, w_out, cache_pool, placement, page_table, cache_len
):
    tokens = x_prefill.shape[0]
    steps, requests, width = x_decode.shape
    section, tp, plane = lax.axis_index("section"), lax.axis_index("tp"), lax.axis_index("dp")
    x, y = lax.div(tp, 4), lax.rem(tp, 4)
    lane = lax.rem(tp, 2)
    group = section * 8 + plane
    info = jnp.stack([group, section, plane, lane]).astype(jnp.int32)
    turn = jnp.where(section == 0, 1, -1)
    steps_of = jnp.arange(16, dtype=jnp.int32)
    order = lax.rem(x - turn * (steps_of // 4) + 4, 4) * 4 + lax.rem(
        y - turn * (steps_of % 4) + 4, 4
    )
    kv_order = jnp.where(order // 8 == section, 0, 8) + lax.rem(plane - order % 8 + 8, 8)

    wq_all = lax.all_gather(w_query, ("section", "dp"), axis=0, tiled=False)
    wo_all = lax.all_gather(w_out, ("section", "dp"), axis=1, tiled=True)

    wkv_all = jnp.concatenate(gather_groups(w_keyval), axis=0)
    half = tokens // 2
    x_pre = gather_tp(x_prefill[:half], x_prefill[half:])
    kv_mine = project(kv_order, x_pre, wkv_all)
    kv_theirs = lax.ppermute(kv_mine, "tp", LANE)
    kv_pair = jnp.stack(
        [jnp.where(lane == 0, kv_mine, kv_theirs), jnp.where(lane == 0, kv_theirs, kv_mine)]
    )
    kv_own, kv_other = gather_groups(kv_pair)

    rows = x_decode.reshape(steps * requests, width)
    half = rows.shape[0] // 2
    x_dec = gather_tp(rows[:half], rows[half:])
    new_mine = project(kv_order, x_dec, wkv_all)
    new_theirs = lax.ppermute(new_mine, "tp", LANE)
    keys = jnp.where(lane == 0, new_mine, new_theirs)
    values = jnp.where(lane == 0, new_theirs, new_mine)
    mine = cache_pool[0]
    other = lax.ppermute(mine, "tp", LANE)

    q_dec = project(order, x_dec, wq_all)
    attention = decode_attention(
        info,
        placement,
        q_dec,
        keys,
        values,
        page_table,
        cache_len[:, None],
        mine,
        other,
        kv_own,
        kv_other,
    )
    q_pre = project(order, x_pre, wq_all)
    prefill_out = prefill_attention(info, q_pre, kv_own, kv_other)
    projected = jnp.dot(attention, wo_all, preferred_element_type=jnp.float32).astype(jnp.bfloat16)
    decode_out = scatter_tp(projected, x, y).reshape(steps, requests, -1)
    return (prefill_out, decode_out)


def solution(mesh):
    return jax.shard_map(
        on_device,
        mesh=mesh,
        in_specs=(
            P(("section", "dp"), "tp"),
            P(None, ("section", "dp"), "tp"),
            P(("section", "dp"), "tp"),
            P(("section", "dp"), "tp"),
            P("tp", ("section", "dp")),
            P("tp", ("section", "dp"), None, None),
            P(),
            P(("section", "dp"), None),
            P(("section", "dp")),
        ),
        out_specs=(P(("section", "dp"), "tp"), P(None, ("section", "dp"), "tp")),
        check_vma=False,
    )
```

```python
import functools
import math

import jax
import jax.numpy as jnp
from jax import lax
from jax.experimental import pallas as pl
from jax.experimental.pallas import tpu as pltpu
from jax.sharding import PartitionSpec as P

HD = 128
PAGE = 128
NEG = -1e30
SCALE = 1.0 / math.sqrt(HD)
VMEM_LIMIT = 48 * 1024 * 1024

ALL = ("section", "tp", "dp")
ST = ("section", "tp")
SD = ("section", "dp")

SWAP = [(0, 1), (1, 0)]
LANE = [(t, t ^ 1) for t in range(16)]
SPIN = [(s * 8 + z, s * 8 + (z + 1 - 2 * s) % 8) for s in range(2) for z in range(8)]


def tp_perm(dx, dy):
    return [
        (x * 4 + y, (x + dx) % 4 * 4 + (y + dy) % 4) for x in range(4) for y in range(4)
    ]


def ring_perm(dx, dy):
    pairs = []
    for s in range(2):
        d = 1 - 2 * s
        pairs += [(s * 16 + a, s * 16 + b) for a, b in tp_perm(d * dx, d * dy)]
    return pairs


RING_X = ring_perm(1, 0)
RING_Y = ring_perm(0, 1)


def device(s, t, z):
    return s * 128 + t * 8 + z


def piece_of(c, y):
    return divmod((c + y) % 4, 2)


def to_rows(c):
    pairs = []
    for s in range(2):
        for t in range(16):
            other, high = piece_of(c, t % 4)
            for z in range(8):
                to = device(s ^ other, t, (z - t // 4 - 4 * high) % 8)
                pairs.append((device(s, t, z), to))
    return pairs


def to_columns(c):
    pairs = []
    for s in range(2):
        for t in range(16):
            other, high = piece_of(c, t % 4)
            for z in range(8):
                to = (s ^ other) * 8 + (z + t // 4 + 4 * high) % 8
                pairs.append((device(s, t, z), device(s, to, z)))
    return pairs


def gather_tp(first, second):
    a, b = [first], [second]
    for _ in range(3):
        a.append(lax.ppermute(a[-1], ST, RING_Y))
        b.append(lax.ppermute(b[-1], ST, RING_X))
    a, b = [jnp.stack(a)], [jnp.stack(b)]
    for _ in range(3):
        a.append(lax.ppermute(a[-1], ST, RING_X))
        b.append(lax.ppermute(b[-1], ST, RING_Y))
    return a + b


def gather_planes(value):
    mine = [jnp.stack([value, lax.ppermute(value, "section", SWAP)])]
    theirs = []
    for r in range(1, 5):
        mine.append(lax.ppermute(mine[-1], SD, SPIN))
        if r < 4:
            theirs.append(lax.ppermute(mine[-1], "section", SWAP))
    return mine + theirs


def placed(refs, section):
    for n, ref in enumerate(refs):
        r = n if n < 5 else n - 4
        up, down = (r, (8 - r) % 8) if n < 5 else (8 - r, r)
        below = jnp.where(section == 0, up, down)
        for e in range(2):
            yield ref.at[e], (e if n < 5 else 1 - e), below


def group_at(info, other, below):
    section = info[1] if other == 0 else 1 - info[1]
    return section * 8 + lax.rem(info[2] - below + 8, 8)


def specs(smem, vmem, anywhere=0):
    return (
        [pl.BlockSpec(memory_space=pltpu.SMEM)] * smem
        + [pl.BlockSpec(memory_space=pltpu.VMEM)] * vmem
        + [pl.BlockSpec(memory_space=pl.ANY)] * anywhere
    )


def params():
    return pltpu.CompilerParams(vmem_limit_bytes=VMEM_LIMIT)


def project_kernel(first, tokens, order, *refs):
    a, b, w, pre, dec, held, sems = refs[:4], refs[4:8], refs[8], *refs[9:]
    depth, cols = held.shape[1:]
    copies = []
    for n in range(16):
        source = w.at[order[n], :, first : first + cols]
        copy = pltpu.make_async_copy(source, held.at[n], sems.at[n])
        copy.start()
        copies.append(copy)
    total = None
    for i in range(4):
        rows = jnp.concatenate(
            [
                jnp.concatenate([a[i][j] for j in range(4)], axis=1),
                jnp.concatenate([b[j][i] for j in range(4)], axis=1),
            ],
            axis=0,
        )
        for j in range(4):
            copies[4 * i + j].wait()
        block = held[4 * i : 4 * i + 4].reshape(4 * depth, cols)
        part = jnp.dot(rows, block, preferred_element_type=jnp.float32)
        total = part if total is None else total + part
    result = total.astype(pre.dtype)
    half, each = tokens // 2, result.shape[0] // 2
    pre[:half, :] = result[:half]
    pre[half:, :] = result[each : each + half]
    dec[: each - half, :] = result[half:each]
    dec[each - half :, :] = result[each + half :]


def project(order, blocks, w, first, cols, tokens):
    rows = 2 * blocks[0].shape[1]
    depth = w.shape[1]
    return pl.pallas_call(
        functools.partial(project_kernel, first, tokens),
        out_shape=[
            jax.ShapeDtypeStruct((tokens, cols), jnp.bfloat16),
            jax.ShapeDtypeStruct((rows - tokens, cols), jnp.bfloat16),
        ],
        in_specs=specs(1, 8, 1),
        out_specs=specs(0, 2),
        scratch_shapes=[
            pltpu.VMEM((16, depth, cols), jnp.bfloat16),
            pltpu.SemaphoreType.DMA((16,)),
        ],
        compiler_params=params(),
        cost_estimate=pl.CostEstimate(
            flops=2 * rows * 16 * depth * cols,
            bytes_accessed=2 * 16 * depth * (rows + cols),
            transcendentals=0,
        ),
        name="project",
    )(order, *blocks, w)


def dot_t(a, b):
    return lax.dot_general(a, b, (((1,), (1,)), ((), ())), preferred_element_type=jnp.float32)


def lanes_max(value, top):
    for n in range(0, value.shape[-1], HD):
        top = jnp.maximum(top, value[..., n : n + HD])
    return top


def lanes_sum(value, total):
    for n in range(0, value.shape[-1], HD):
        total = total + value[..., n : n + HD]
    return total


def prefill_kernel(info, q, *refs):
    kv, out, qs, kvs, sc, mx, ls, acc = refs[:8], *refs[8:]
    tokens = q.shape[0]
    heads = q.shape[1] // HD
    group = info[0]
    for block, other, below in placed(kv, info[1]):
        kvs[group_at(info, other, below)] = block[...]
    for h in range(heads):
        qs[h] = q[:, h * HD : (h + 1) * HD]

    row = lax.broadcasted_iota(jnp.int32, (tokens, tokens), 0)
    col = lax.broadcasted_iota(jnp.int32, (tokens, tokens), 1)
    for h in range(heads):
        scores = jnp.where(col <= row, dot_t(qs[h], kvs[group, 0]), NEG)
        sc[group, h] = scores
        mx[h] = lanes_max(scores[:, HD:], scores[:, :HD])

    @pl.loop(0, group)
    def _(n):
        for h in range(heads):
            scores = dot_t(qs[h], kvs[n, 0])
            sc[n, h] = scores
            mx[h] = lanes_max(scores, mx[h])

    for h in range(heads):
        top = jnp.max(mx[h], axis=-1, keepdims=True) * SCALE
        mx[h] = jnp.broadcast_to(top, (tokens, HD))
        ls[h] = jnp.zeros((tokens, HD), jnp.float32)
        acc[h] = jnp.zeros((tokens, HD), jnp.float32)

    @pl.loop(0, group + 1)
    def _(n):
        for h in range(heads):
            top = jnp.concatenate([mx[h]] * (tokens // HD), axis=1)
            probs = jnp.exp(sc[n, h] * SCALE - top)
            ls[h] = lanes_sum(probs, ls[h])
            acc[h] += jnp.dot(
                probs.astype(jnp.bfloat16), kvs[n, 1], preferred_element_type=jnp.float32
            )

    for h in range(heads):
        total = jnp.sum(ls[h], axis=-1, keepdims=True)
        out[:, h * HD : (h + 1) * HD] = (acc[h] / total).astype(out.dtype)


def prefill_attention(info, q, kv):
    tokens, cols = q.shape
    heads = cols // HD
    return pl.pallas_call(
        prefill_kernel,
        out_shape=jax.ShapeDtypeStruct(q.shape, jnp.bfloat16),
        in_specs=specs(1, 9),
        out_specs=specs(0, 1)[0],
        scratch_shapes=[
            pltpu.VMEM((heads, tokens, HD), jnp.bfloat16),
            pltpu.VMEM((16, 2, tokens, HD), jnp.bfloat16),
            pltpu.VMEM((16, heads, tokens, tokens), jnp.float32),
            pltpu.VMEM((heads, tokens, HD), jnp.float32),
            pltpu.VMEM((heads, tokens, HD), jnp.float32),
            pltpu.VMEM((heads, tokens, HD), jnp.float32),
        ],
        compiler_params=params(),
        cost_estimate=pl.CostEstimate(
            flops=4 * 4096 * tokens * cols, bytes_accessed=3 << 20, transcendentals=4096 * 1024
        ),
        name="prefill_attention",
    )(info, q, *kv)


def decode_kernel(info, placement, q, keys, values, table, lens, mine, other, *refs):
    kv, outs, (ks, vs, bias, sc, res) = refs[:8], refs[8:12], refs[12:]
    slots = mine.shape[0]
    requests, pages = table.shape
    steps = q.shape[0] // requests
    heads = q.shape[1] // HD
    lane = info[3]
    for pool, first in ((mine, lane * slots), (other, (1 - lane) * slots)):
        for i in range(slots):
            ks[first + i] = pool[i, :, :HD]
            vs[first + i] = pool[i, :, HD:]

    for block, far, below in placed(kv, info[1]):
        group = group_at(info, far, below)
        for half in range(2):
            number = 2 * group + half

            @pl.when(placement[number, 0] == info[0])
            def _():
                target = placement[number, 1]
                ks[target] = block[0, half * PAGE : (half + 1) * PAGE, :]
                vs[target] = block[1, half * PAGE : (half + 1) * PAGE, :]

    offset = lax.broadcasted_iota(jnp.int32, (requests, PAGE), 1)
    length = jnp.broadcast_to(lens[...], (requests, PAGE))
    named = []
    for j in range(pages):
        slot = jnp.broadcast_to(table[:, j : j + 1], (requests, PAGE))
        named.append(jnp.where(offset + j * PAGE < length, slot, -1))
    for slot in range(2 * slots):
        count = jnp.zeros((requests, PAGE), jnp.float32)
        for j in range(slot // slots, pages, 2):
            count = count + jnp.where(named[j] == slot, 1.0, 0.0)
        bias[:, slot * PAGE : (slot + 1) * PAGE] = jnp.where(
            count > 0, jnp.log(jnp.maximum(count, 1.0)), NEG
        )

    chunk = 8
    width = chunk * PAGE
    for step in range(steps):
        q_rows = q[step * requests : (step + 1) * requests, :]
        stacked = jnp.concatenate([q_rows[:, h * HD : (h + 1) * HD] for h in range(heads)], axis=0)
        wide = stacked.astype(jnp.float32).reshape(heads, requests, HD)
        fresh = []
        for t in range(step + 1):
            key = keys[t * requests : (t + 1) * requests, :].astype(jnp.float32)
            fresh.append(jnp.sum(wide * key[None], axis=-1, keepdims=True) * SCALE)
        top = fresh[0]
        for score in fresh[1:]:
            top = jnp.maximum(top, score)
        lane_top = jnp.broadcast_to(top, (heads, requests, HD))
        for n in range(2 * slots // chunk):
            k = ks[n * chunk : (n + 1) * chunk].reshape(width, HD)
            scores = dot_t(stacked, k).reshape(heads, requests, width) * SCALE
            scores = scores + bias[:, n * width : (n + 1) * width][None]
            sc[n] = scores
            lane_top = lanes_max(scores, lane_top)
        top = jnp.max(lane_top, axis=-1, keepdims=True)
        total = jnp.zeros((heads, requests, 1), jnp.float32)
        weighted = jnp.zeros((heads, requests, HD), jnp.float32)
        for t, score in enumerate(fresh):
            prob = jnp.exp(score - top)
            value = values[t * requests : (t + 1) * requests, :].astype(jnp.float32)
            total = total + prob
            weighted = weighted + prob * value[None]
        wide_top = jnp.broadcast_to(top, (heads, requests, HD))
        lane_sum = jnp.zeros((heads, requests, HD), jnp.float32)
        for n in range(2 * slots // chunk):
            v = vs[n * chunk : (n + 1) * chunk].reshape(width, HD)
            probs = jnp.exp(sc[n] - jnp.concatenate([wide_top] * chunk, axis=-1))
            lane_sum = lanes_sum(probs, lane_sum)
            update = jnp.dot(
                probs.reshape(heads * requests, width).astype(jnp.bfloat16),
                v,
                preferred_element_type=jnp.float32,
            )
            weighted = weighted + update.reshape(heads, requests, HD)
        total = total + jnp.sum(lane_sum, axis=-1, keepdims=True)
        result = (weighted / total).astype(res.dtype)
        for h in range(heads):
            res[step * requests : (step + 1) * requests, h * HD : (h + 1) * HD] = result[h]

    part = outs[0].shape[0]
    for j in range(4):
        start = lax.rem(info[5] + j, 4) * part
        outs[j][...] = res[pl.ds(pl.multiple_of(start, 16), part), :]


def decode_attention(info, placement, q, keys, values, table, lens, mine, other, kv):
    slots = mine.shape[0]
    requests = table.shape[0]
    rows, cols = q.shape
    return pl.pallas_call(
        decode_kernel,
        out_shape=[jax.ShapeDtypeStruct((rows // 4, cols), jnp.bfloat16)] * 4,
        in_specs=specs(2, 15),
        out_specs=specs(0, 4),
        scratch_shapes=[
            pltpu.VMEM((2 * slots, PAGE, HD), jnp.bfloat16),
            pltpu.VMEM((2 * slots, PAGE, HD), jnp.bfloat16),
            pltpu.VMEM((requests, 2 * slots * PAGE), jnp.float32),
            pltpu.VMEM((2 * slots // 8, cols // HD, requests, 8 * PAGE), jnp.float32),
            pltpu.VMEM((rows, cols), jnp.bfloat16),
        ],
        compiler_params=params(),
        cost_estimate=pl.CostEstimate(
            flops=4 * 768 * 4096 * HD, bytes_accessed=5 << 20, transcendentals=768 * 4096
        ),
        name="decode_attention",
    )(info, placement, q, keys, values, table, lens, mine, other, *kv)


def output_kernel(info, *refs):
    rows_in, w, outs, held, weights = refs[:8], refs[8:12], refs[12:16], *refs[16:]
    depth = w[0].shape[0]
    for block, other, below in placed(rows_in, info[1]):
        held[other * 8 + below] = block[...]
    for j in range(4):
        weights[j * depth : (j + 1) * depth, :] = w[j][...]
    part = held.shape[1]
    for k in range(4):
        x = lax.rem(info[4] + k, 4)
        rows = jnp.concatenate([held[8 * o + x + 4 * h] for o in range(2) for h in range(2)], axis=0)
        result = jnp.dot(rows, weights[...], preferred_element_type=jnp.float32)
        for n in range(4):
            outs[k][n] = result[n * part : (n + 1) * part].astype(outs[k].dtype)


def output_projection(info, rows, w):
    _, part, depth = rows[0].shape
    cols = w[0].shape[1]
    return pl.pallas_call(
        output_kernel,
        out_shape=[jax.ShapeDtypeStruct((4, part, cols), jnp.bfloat16)] * 4,
        in_specs=specs(1, 12),
        out_specs=specs(0, 4),
        scratch_shapes=[
            pltpu.VMEM((16, part, depth), jnp.bfloat16),
            pltpu.VMEM((depth, cols), jnp.bfloat16),
        ],
        compiler_params=params(),
        cost_estimate=pl.CostEstimate(
            flops=32 * part * depth * cols, bytes_accessed=8 << 20, transcendentals=0
        ),
        name="output_projection",
    )(info, *rows, *w)


def sum_kernel(info, *refs):
    parts, outs = refs[:4], refs[4:]
    for c in range(4):
        n = lax.rem(info[5] + c, 4)
        total = parts[0][n].astype(jnp.float32)
        for part in parts[1:]:
            total = total + part[n].astype(jnp.float32)
        outs[c][...] = total.astype(outs[c].dtype)


def sum_parts(info, parts):
    _, part, cols = parts[0].shape
    return pl.pallas_call(
        sum_kernel,
        out_shape=[jax.ShapeDtypeStruct((part, cols), jnp.bfloat16)] * 4,
        in_specs=specs(1, 4),
        out_specs=specs(0, 4),
        compiler_params=params(),
        name="sum_parts",
    )(info, *parts)


def assemble_kernel(info, *refs):
    pieces, out = refs[:4], refs[4]
    part = pieces[0].shape[0]
    below = lax.rem(lax.rem(info[6], 8) - info[2] + 8, 8)
    other = jnp.where(lax.div(info[6], 8) == info[1], 0, 2)
    number = other + lax.div(below, 4)
    for c in range(4):
        start = lax.rem(number - c + 4, 4) * part
        out[pl.ds(pl.multiple_of(start, 16), part), :] = pieces[c][...]


def assemble(info, pieces):
    part, cols = pieces[0].shape
    return pl.pallas_call(
        assemble_kernel,
        out_shape=jax.ShapeDtypeStruct((4 * part, cols), jnp.bfloat16),
        in_specs=specs(1, 4),
        out_specs=specs(0, 1)[0],
        compiler_params=params(),
        name="assemble",
    )(info, *pieces)


def on_device(
    x_prefill, x_decode, w_query, w_keyval, w_out, cache_pool, placement, page_table, cache_len
):
    tokens = x_prefill.shape[0]
    steps, requests, width = x_decode.shape
    section, tp, plane = lax.axis_index("section"), lax.axis_index("tp"), lax.axis_index("dp")
    x, y = lax.div(tp, 4), lax.rem(tp, 4)
    lane = lax.rem(tp, 2)
    group = section * 8 + plane
    info = jnp.stack([group, section, plane, lane, x, y, tp]).astype(jnp.int32)
    turn = jnp.where(section == 0, 1, -1)
    count = jnp.arange(16, dtype=jnp.int32)
    order = lax.rem(x - turn * (count // 4) + 4, 4) * 4 + lax.rem(y - turn * (count % 4) + 4, 4)

    q_cols, kv_cols = w_query.shape[1], w_keyval.shape[1]
    w_all = lax.all_gather(jnp.concatenate([w_query, w_keyval], axis=1), SD, axis=0, tiled=False)

    rows = x_decode.reshape(steps * requests, width)
    half_p, half_d = tokens // 2, rows.shape[0] // 2
    blocks = gather_tp(
        jnp.concatenate([x_prefill[:half_p], rows[:half_d]], axis=0),
        jnp.concatenate([x_prefill[half_p:], rows[half_d:]], axis=0),
    )
    mine, w_out, *blocks = lax.optimization_barrier((cache_pool[0], w_out, *blocks))
    other = lax.ppermute(mine, "tp", LANE)
    wo = [w_out] + [lax.ppermute(w_out, "tp", tp_perm(0, j)) for j in range(1, 4)]

    kv_pre, kv_dec = project(order, blocks, w_all, q_cols, kv_cols, tokens)
    other_pre, other_dec = lax.ppermute((kv_pre, kv_dec), "tp", LANE)
    is_key = lane == 0
    kv = gather_planes(
        jnp.stack([jnp.where(is_key, kv_pre, other_pre), jnp.where(is_key, other_pre, kv_pre)])
    )
    keys = jnp.where(is_key, kv_dec, other_dec)
    values = jnp.where(is_key, other_dec, kv_dec)
    q_pre, q_dec = project(order, blocks, w_all, 0, q_cols, tokens)

    attention = decode_attention(
        info, placement, q_dec, keys, values, page_table, cache_len[:, None], mine, other, kv
    )
    split = [attention[0]] + [
        lax.ppermute(attention[j], "tp", tp_perm(0, j)) for j in range(1, 4)
    ]
    attended = gather_planes(jnp.concatenate(split, axis=1))
    prefill_out = prefill_attention(info, q_pre, kv)
    parts = output_projection(info, attended, wo)
    parts = [parts[0]] + [lax.ppermute(parts[k], "tp", tp_perm(k, 0)) for k in range(1, 4)]
    pieces = sum_parts(info, parts)
    pieces = [lax.ppermute(pieces[c], ALL, to_rows(c)) for c in range(4)]
    pieces = [lax.ppermute(pieces[c], ALL, to_columns(c)) for c in range(4)]
    decode_out = assemble(info, pieces).reshape(steps, requests, -1)
    return (prefill_out, decode_out)


def solution(mesh):
    return jax.shard_map(
        on_device,
        mesh=mesh,
        in_specs=(
            P(("section", "dp"), "tp"),
            P(None, ("section", "dp"), "tp"),
            P(("section", "dp"), "tp"),
            P(("section", "dp"), "tp"),
            P("tp", ("section", "dp")),
            P("tp", ("section", "dp"), None, None),
            P(),
            P(("section", "dp"), None),
            P(("section", "dp")),
        ),
        out_specs=(P(("section", "dp"), "tp"), P(None, ("section", "dp"), "tp")),
        check_vma=False,
    )
```

```python
import functools
import math

import jax
import jax.numpy as jnp
from jax import lax
from jax.experimental import pallas as pl
from jax.experimental.pallas import tpu as pltpu
from jax.sharding import PartitionSpec as P

HD = 128
PAGE = 128
NEG = -1e30
SCALE = 1.0 / math.sqrt(HD)
VMEM_LIMIT = 48 * 1024 * 1024

ST = ("section", "tp")
SD = ("section", "dp")

SWAP = [(0, 1), (1, 0)]
LANE = [(t, t ^ 1) for t in range(16)]
BOTH = [(t, t ^ 17) for t in range(32)]
SPIN = [(s * 8 + z, s * 8 + (z + 1 - 2 * s) % 8) for s in range(2) for z in range(8)]


def tp_perm(dx, dy):
    return [
        (x * 4 + y, (x + dx) % 4 * 4 + (y + dy) % 4) for x in range(4) for y in range(4)
    ]


def ring_perm(dx, dy):
    pairs = []
    for s in range(2):
        d = 1 - 2 * s
        pairs += [(s * 16 + a, s * 16 + b) for a, b in tp_perm(d * dx, d * dy)]
    return pairs


RING_X = ring_perm(1, 0)
RING_Y = ring_perm(0, 1)


def gather_tp(first, second):
    a, b = [first], [second]
    for _ in range(3):
        a.append(lax.ppermute(a[-1], ST, RING_Y))
        b.append(lax.ppermute(b[-1], ST, RING_X))
    a, b = [jnp.stack(a)], [jnp.stack(b)]
    for _ in range(3):
        a.append(lax.ppermute(a[-1], ST, RING_X))
        b.append(lax.ppermute(b[-1], ST, RING_Y))
    return a + b


def gather_planes(pair):
    mine = [pair]
    theirs = []
    for r in range(1, 5):
        mine.append(lax.ppermute(mine[-1], SD, SPIN))
        if r < 4:
            theirs.append(lax.ppermute(mine[-1], "section", SWAP))
    return mine + theirs


def placed(refs, section):
    for n, ref in enumerate(refs):
        r = n if n < 5 else n - 4
        up, down = (r, (8 - r) % 8) if n < 5 else (8 - r, r)
        below = jnp.where(section == 0, up, down)
        for e in range(2):
            yield ref.at[e], (e if n < 5 else 1 - e), below


def group_at(info, other, below):
    section = info[1] if other == 0 else 1 - info[1]
    return section * 8 + lax.rem(info[2] - below + 8, 8)


def specs(smem, vmem, anywhere=0):
    return (
        [pl.BlockSpec(memory_space=pltpu.SMEM)] * smem
        + [pl.BlockSpec(memory_space=pltpu.VMEM)] * vmem
        + [pl.BlockSpec(memory_space=pl.ANY)] * anywhere
    )


def params():
    return pltpu.CompilerParams(vmem_limit_bytes=VMEM_LIMIT)


def project_kernel(tokens, order, *refs):
    a, b, w, pre, dec, kv, held, sems = refs[:4], refs[4:8], refs[8], *refs[9:]
    depth, cols = held.shape[1:]
    q_cols = pre.shape[1]
    copies = []
    for n in range(16):
        copy = pltpu.make_async_copy(w.at[order[n]], held.at[n], sems.at[n])
        copy.start()
        copies.append(copy)
    total = None
    for i in range(4):
        rows = jnp.concatenate(
            [
                jnp.concatenate([a[i][j] for j in range(4)], axis=1),
                jnp.concatenate([b[j][i] for j in range(4)], axis=1),
            ],
            axis=0,
        )
        for j in range(4):
            copies[4 * i + j].wait()
        block = held[4 * i : 4 * i + 4].reshape(4 * depth, cols)
        part = jnp.dot(rows, block, preferred_element_type=jnp.float32)
        total = part if total is None else total + part
    result = total.astype(pre.dtype)
    half, each = tokens // 2, result.shape[0] // 2
    for first in range(2):
        start = first * each
        kept = result[start : start + half]
        rest = result[start + half : start + each]
        pre[first * half : (first + 1) * half, :] = kept[:, :q_cols]
        kv[first * half : (first + 1) * half, :] = kept[:, q_cols:]
        late = each - half
        dec[first * late : (first + 1) * late, :] = rest[:, :q_cols]
        kv[tokens + first * late : tokens + (first + 1) * late, :] = rest[:, q_cols:]


def project(order, blocks, w, q_cols, tokens):
    rows = 2 * blocks[0].shape[1]
    depth, cols = w.shape[1:]
    return pl.pallas_call(
        functools.partial(project_kernel, tokens),
        out_shape=[
            jax.ShapeDtypeStruct((tokens, q_cols), jnp.bfloat16),
            jax.ShapeDtypeStruct((rows - tokens, q_cols), jnp.bfloat16),
            jax.ShapeDtypeStruct((rows, cols - q_cols), jnp.bfloat16),
        ],
        in_specs=specs(1, 8, 1),
        out_specs=specs(0, 3),
        scratch_shapes=[
            pltpu.VMEM((16, depth, cols), jnp.bfloat16),
            pltpu.SemaphoreType.DMA((16,)),
        ],
        compiler_params=params(),
        cost_estimate=pl.CostEstimate(
            flops=2 * rows * 16 * depth * cols,
            bytes_accessed=2 * 16 * depth * (rows + cols),
            transcendentals=0,
        ),
        name="project",
    )(order, *blocks, w)


def dot_t(a, b):
    return lax.dot_general(a, b, (((1,), (1,)), ((), ())), preferred_element_type=jnp.float32)


def lanes_max(value, top):
    for n in range(0, value.shape[-1], HD):
        top = jnp.maximum(top, value[..., n : n + HD])
    return top


def lanes_sum(value, total):
    for n in range(0, value.shape[-1], HD):
        total = total + value[..., n : n + HD]
    return total


def prefill_kernel(info, q, *refs):
    kv, out, qs, kvs, sc, mx, ls, acc = refs[:8], *refs[8:]
    tokens = q.shape[0]
    heads = q.shape[1] // HD
    group = info[0]
    for block, other, below in placed(kv, info[1]):
        kvs[group_at(info, other, below)] = block[...]
    for h in range(heads):
        qs[h] = q[:, h * HD : (h + 1) * HD]

    row = lax.broadcasted_iota(jnp.int32, (tokens, tokens), 0)
    col = lax.broadcasted_iota(jnp.int32, (tokens, tokens), 1)
    for h in range(heads):
        scores = jnp.where(col <= row, dot_t(qs[h], kvs[group, 0]), NEG)
        sc[group, h] = scores
        mx[h] = lanes_max(scores[:, HD:], scores[:, :HD])

    @pl.loop(0, group)
    def _(n):
        for h in range(heads):
            scores = dot_t(qs[h], kvs[n, 0])
            sc[n, h] = scores
            mx[h] = lanes_max(scores, mx[h])

    for h in range(heads):
        top = jnp.max(mx[h], axis=-1, keepdims=True) * SCALE
        mx[h] = jnp.broadcast_to(top, (tokens, HD))
        ls[h] = jnp.zeros((tokens, HD), jnp.float32)
        acc[h] = jnp.zeros((tokens, HD), jnp.float32)

    @pl.loop(0, group + 1)
    def _(n):
        for h in range(heads):
            top = jnp.concatenate([mx[h]] * (tokens // HD), axis=1)
            probs = jnp.exp(sc[n, h] * SCALE - top)
            ls[h] = lanes_sum(probs, ls[h])
            acc[h] += jnp.dot(
                probs.astype(jnp.bfloat16), kvs[n, 1], preferred_element_type=jnp.float32
            )

    for h in range(heads):
        total = jnp.sum(ls[h], axis=-1, keepdims=True)
        out[:, h * HD : (h + 1) * HD] = (acc[h] / total).astype(out.dtype)


def prefill_attention(info, q, kv):
    tokens, cols = q.shape
    heads = cols // HD
    return pl.pallas_call(
        prefill_kernel,
        out_shape=jax.ShapeDtypeStruct(q.shape, jnp.bfloat16),
        in_specs=specs(1, 9),
        out_specs=specs(0, 1)[0],
        scratch_shapes=[
            pltpu.VMEM((heads, tokens, HD), jnp.bfloat16),
            pltpu.VMEM((16, 2, tokens, HD), jnp.bfloat16),
            pltpu.VMEM((16, heads, tokens, tokens), jnp.float32),
            pltpu.VMEM((heads, tokens, HD), jnp.float32),
            pltpu.VMEM((heads, tokens, HD), jnp.float32),
            pltpu.VMEM((heads, tokens, HD), jnp.float32),
        ],
        compiler_params=params(),
        cost_estimate=pl.CostEstimate(
            flops=4 * 4096 * tokens * cols, bytes_accessed=3 << 20, transcendentals=4096 * 1024
        ),
        name="prefill_attention",
    )(info, q, *kv)


def decode_kernel(info, placement, q, keys, values, table, lens, mine, other, *refs):
    kv, res, ks, vs, bias, sc = refs[:8], *refs[8:]
    slots = mine.shape[0]
    requests, pages = table.shape
    steps = q.shape[0] // requests
    heads = q.shape[1] // HD
    lane = info[3]
    for pool, first in ((mine, lane * slots), (other, (1 - lane) * slots)):
        for i in range(slots):
            ks[first + i] = pool[i, :, :HD]
            vs[first + i] = pool[i, :, HD:]

    for block, far, below in placed(kv, info[1]):
        group = group_at(info, far, below)
        for half in range(2):
            number = 2 * group + half

            @pl.when(placement[number, 0] == info[0])
            def _():
                target = placement[number, 1]
                ks[target] = block[0, half * PAGE : (half + 1) * PAGE, :]
                vs[target] = block[1, half * PAGE : (half + 1) * PAGE, :]

    offset = lax.broadcasted_iota(jnp.int32, (requests, PAGE), 1)
    length = jnp.broadcast_to(lens[...], (requests, PAGE))
    named = []
    for j in range(pages):
        slot = jnp.broadcast_to(table[:, j : j + 1], (requests, PAGE))
        named.append(jnp.where(offset + j * PAGE < length, slot, -1))
    for slot in range(2 * slots):
        count = jnp.zeros((requests, PAGE), jnp.float32)
        for j in range(slot // slots, pages, 2):
            count = count + jnp.where(named[j] == slot, 1.0, 0.0)
        bias[:, slot * PAGE : (slot + 1) * PAGE] = jnp.where(
            count > 0, jnp.log(jnp.maximum(count, 1.0)), NEG
        )

    chunk = 8
    width = chunk * PAGE
    for step in range(steps):
        q_rows = q[step * requests : (step + 1) * requests, :]
        stacked = jnp.concatenate([q_rows[:, h * HD : (h + 1) * HD] for h in range(heads)], axis=0)
        wide = stacked.astype(jnp.float32).reshape(heads, requests, HD)
        fresh = []
        for t in range(step + 1):
            key = keys[t * requests : (t + 1) * requests, :].astype(jnp.float32)
            fresh.append(jnp.sum(wide * key[None], axis=-1, keepdims=True) * SCALE)
        top = fresh[0]
        for score in fresh[1:]:
            top = jnp.maximum(top, score)
        lane_top = jnp.broadcast_to(top, (heads, requests, HD))
        for n in range(2 * slots // chunk):
            k = ks[n * chunk : (n + 1) * chunk].reshape(width, HD)
            scores = dot_t(stacked, k).reshape(heads, requests, width) * SCALE
            scores = scores + bias[:, n * width : (n + 1) * width][None]
            sc[n] = scores
            lane_top = lanes_max(scores, lane_top)
        top = jnp.max(lane_top, axis=-1, keepdims=True)
        total = jnp.zeros((heads, requests, 1), jnp.float32)
        weighted = jnp.zeros((heads, requests, HD), jnp.float32)
        for t, score in enumerate(fresh):
            prob = jnp.exp(score - top)
            value = values[t * requests : (t + 1) * requests, :].astype(jnp.float32)
            total = total + prob
            weighted = weighted + prob * value[None]
        wide_top = jnp.broadcast_to(top, (heads, requests, HD))
        lane_sum = jnp.zeros((heads, requests, HD), jnp.float32)
        for n in range(2 * slots // chunk):
            v = vs[n * chunk : (n + 1) * chunk].reshape(width, HD)
            probs = jnp.exp(sc[n] - jnp.concatenate([wide_top] * chunk, axis=-1))
            lane_sum = lanes_sum(probs, lane_sum)
            update = jnp.dot(
                probs.reshape(heads * requests, width).astype(jnp.bfloat16),
                v,
                preferred_element_type=jnp.float32,
            )
            weighted = weighted + update.reshape(heads, requests, HD)
        total = total + jnp.sum(lane_sum, axis=-1, keepdims=True)
        result = (weighted / total).astype(res.dtype)
        for h in range(heads):
            res[step * requests : (step + 1) * requests, h * HD : (h + 1) * HD] = result[h]


def decode_attention(info, placement, q, keys, values, table, lens, mine, other, kv):
    slots = mine.shape[0]
    requests = table.shape[0]
    cols = q.shape[1]
    return pl.pallas_call(
        decode_kernel,
        out_shape=jax.ShapeDtypeStruct(q.shape, jnp.bfloat16),
        in_specs=specs(2, 15),
        out_specs=specs(0, 1)[0],
        scratch_shapes=[
            pltpu.VMEM((2 * slots, PAGE, HD), jnp.bfloat16),
            pltpu.VMEM((2 * slots, PAGE, HD), jnp.bfloat16),
            pltpu.VMEM((requests, 2 * slots * PAGE), jnp.float32),
            pltpu.VMEM((2 * slots // 8, cols // HD, requests, 8 * PAGE), jnp.float32),
        ],
        compiler_params=params(),
        cost_estimate=pl.CostEstimate(
            flops=4 * 768 * 4096 * HD, bytes_accessed=5 << 20, transcendentals=768 * 4096
        ),
        name="decode_attention",
    )(info, placement, q, keys, values, table, lens, mine, other, *kv)


def output_kernel(info, rows, w, *refs):
    outs, (held, product, sems) = refs[:8], refs[8:]
    half = rows.shape[0] // 2
    copies = []
    for n in range(16):
        copy = pltpu.make_async_copy(w.at[n], held.at[n], sems.at[n])
        copy.start()
        copies.append(copy)
    for n in range(16):
        copies[n].wait()
        result = jnp.dot(rows[...], held[n], preferred_element_type=jnp.float32)
        product[n] = result.astype(product.dtype)
    for k in range(4):
        x, y = lax.rem(info[4] + k, 4), lax.rem(info[5] + k, 4)
        for n in range(4):
            outs[k][n] = product[4 * x + n, :half, :]
            outs[4 + k][n] = product[4 * n + y, half:, :]


def output_projection(info, rows, w):
    half, depth = rows.shape[0] // 2, rows.shape[1]
    cols = w.shape[2]
    return pl.pallas_call(
        output_kernel,
        out_shape=[jax.ShapeDtypeStruct((4, half, cols), jnp.bfloat16)] * 8,
        in_specs=specs(1, 1, 1),
        out_specs=specs(0, 8),
        scratch_shapes=[
            pltpu.VMEM((16, depth, cols), jnp.bfloat16),
            pltpu.VMEM((16, 2 * half, cols), jnp.bfloat16),
            pltpu.SemaphoreType.DMA((16,)),
        ],
        compiler_params=params(),
        cost_estimate=pl.CostEstimate(
            flops=64 * half * depth * cols, bytes_accessed=12 << 20, transcendentals=0
        ),
        name="output_projection",
    )(info, rows, w)


def first_sum_kernel(info, *refs):
    parts, outs = refs[:8], refs[8:]
    for side in range(2):
        for k in range(4):
            n = lax.rem(info[5 - side] + k, 4)
            total = parts[4 * side][n].astype(jnp.float32)
            for part in parts[4 * side + 1 : 4 * side + 4]:
                total = total + part[n].astype(jnp.float32)
            outs[4 * side + k][...] = total.astype(outs[k].dtype)


def first_sum(info, parts):
    _, half, cols = parts[0].shape
    return pl.pallas_call(
        first_sum_kernel,
        out_shape=[jax.ShapeDtypeStruct((half, cols), jnp.bfloat16)] * 8,
        in_specs=specs(1, 8),
        out_specs=specs(0, 8),
        compiler_params=params(),
        name="first_sum",
    )(info, *parts)


def second_sum_kernel(*refs):
    parts, out = refs[:8], refs[8]
    half = parts[0].shape[0]
    for side in range(2):
        total = parts[4 * side][...].astype(jnp.float32)
        for part in parts[4 * side + 1 : 4 * side + 4]:
            total = total + part[...].astype(jnp.float32)
        out[side * half : (side + 1) * half, :] = total.astype(out.dtype)


def second_sum(parts):
    half, cols = parts[0].shape
    return pl.pallas_call(
        second_sum_kernel,
        out_shape=jax.ShapeDtypeStruct((2 * half, cols), jnp.bfloat16),
        in_specs=specs(0, 8),
        out_specs=specs(0, 1)[0],
        compiler_params=params(),
        name="second_sum",
    )(*parts)


def send_parts(parts, first):
    sent = list(parts)
    for k in (2, 1, 3):
        sent[k] = lax.ppermute(parts[k], "tp", tp_perm(k, 0) if first else tp_perm(0, k))
        sent[4 + k] = lax.ppermute(parts[4 + k], "tp", tp_perm(0, k) if first else tp_perm(k, 0))
    return sent


def on_device(
    x_prefill, x_decode, w_query, w_keyval, w_out, cache_pool, placement, page_table, cache_len
):
    tokens = x_prefill.shape[0]
    steps, requests, width = x_decode.shape
    section, tp, plane = lax.axis_index("section"), lax.axis_index("tp"), lax.axis_index("dp")
    x, y = lax.div(tp, 4), lax.rem(tp, 4)
    lane = lax.rem(tp, 2)
    group = section * 8 + plane
    info = jnp.stack([group, section, plane, lane, x, y, tp]).astype(jnp.int32)
    turn = jnp.where(section == 0, 1, -1)
    count = jnp.arange(16, dtype=jnp.int32)
    order = lax.rem(x - turn * (count // 4) + 4, 4) * 4 + lax.rem(y - turn * (count % 4) + 4, 4)

    q_cols = w_query.shape[1]
    w_all = lax.all_gather(jnp.concatenate([w_query, w_keyval], axis=1), SD, axis=0, tiled=False)
    wo_all = lax.all_gather(w_out, SD, axis=0, tiled=False)

    rows = x_decode.reshape(steps * requests, width)
    half_p, half_d = tokens // 2, rows.shape[0] // 2
    blocks = gather_tp(
        jnp.concatenate([x_prefill[:half_p], rows[:half_d]], axis=0),
        jnp.concatenate([x_prefill[half_p:], rows[half_d:]], axis=0),
    )
    q_pre, q_dec, kv_mine = project(order, blocks, w_all, q_cols, tokens)
    kv_lane = lax.ppermute(kv_mine, "tp", LANE)
    kv_core = lax.ppermute(kv_mine[:tokens], "section", SWAP)
    kv_both = lax.ppermute(kv_mine[:tokens], ST, BOTH)
    mine, kv_lane, kv_core, kv_both = lax.optimization_barrier(
        (cache_pool[0], kv_lane, kv_core, kv_both)
    )
    other = lax.ppermute(mine, "tp", LANE)
    is_key = lane == 0
    near, far = (kv_mine[:tokens], kv_lane[:tokens]), (kv_core, kv_both)
    kv = gather_planes(
        jnp.stack(
            [
                jnp.stack([jnp.where(is_key, p, q), jnp.where(is_key, q, p)])
                for p, q in (near, far)
            ]
        )
    )
    keys = jnp.where(is_key, kv_mine[tokens:], kv_lane[tokens:])
    values = jnp.where(is_key, kv_lane[tokens:], kv_mine[tokens:])

    attention = decode_attention(
        info, placement, q_dec, keys, values, page_table, cache_len[:, None], mine, other, kv
    )
    parts = send_parts(output_projection(info, attention, wo_all), True)
    prefill_out = prefill_attention(info, q_pre, kv)
    prefill_out, *parts = lax.optimization_barrier((prefill_out, *parts))
    parts = send_parts(first_sum(info, parts), False)
    decode_out = second_sum(parts).reshape(steps, requests, -1)
    return (prefill_out, decode_out)


def solution(mesh):
    return jax.shard_map(
        on_device,
        mesh=mesh,
        in_specs=(
            P(("section", "dp"), "tp"),
            P(None, ("section", "dp"), "tp"),
            P(("section", "dp"), "tp"),
            P(("section", "dp"), "tp"),
            P("tp", ("section", "dp")),
            P("tp", ("section", "dp"), None, None),
            P(),
            P(("section", "dp"), None),
            P(("section", "dp")),
        ),
        out_specs=(P(("section", "dp"), "tp"), P(None, ("section", "dp"), "tp")),
        check_vma=False,
    )
```

```python
import functools
import math

import jax
import jax.numpy as jnp
from jax import lax
from jax.experimental import pallas as pl
from jax.experimental.pallas import tpu as pltpu
from jax.sharding import PartitionSpec as P

HD = 128
PAGE = 128
NEG = -1e30
SCALE = 1.0 / math.sqrt(HD)

ST = ("section", "tp")
SD = ("section", "dp")

SWAP = [(0, 1), (1, 0)]
LANE = [(t, t ^ 1) for t in range(16)]
BOTH = [(t, t ^ 17) for t in range(32)]
SPIN = [(s * 8 + z, s * 8 + (z + 1 - 2 * s) % 8) for s in range(2) for z in range(8)]


def tp_perm(dx, dy):
    return [
        (x * 4 + y, (x + dx) % 4 * 4 + (y + dy) % 4) for x in range(4) for y in range(4)
    ]


def ring_perm(dx, dy):
    pairs = []
    for s in range(2):
        d = 1 - 2 * s
        pairs += [(s * 16 + a, s * 16 + b) for a, b in tp_perm(d * dx, d * dy)]
    return pairs


RING_X = ring_perm(1, 0)
RING_Y = ring_perm(0, 1)


def gather_tp(first, second):
    a, b = [first], [second]
    for _ in range(3):
        a.append(lax.ppermute(a[-1], ST, RING_Y))
        b.append(lax.ppermute(b[-1], ST, RING_X))
    a, b = [jnp.stack(a)], [jnp.stack(b)]
    for _ in range(3):
        a.append(lax.ppermute(a[-1], ST, RING_X))
        b.append(lax.ppermute(b[-1], ST, RING_Y))
    return a + b


def gather_planes(pair, beside):
    mine = [pair]
    theirs = []
    for r in range(1, 5):
        mine.append(lax.ppermute(mine[-1], SD, SPIN))
        if r == 1:
            mine[1], *beside = lax.optimization_barrier((mine[1], *beside))
        if r < 4:
            theirs.append(lax.ppermute(mine[-1], "section", SWAP))
    return mine + theirs, beside


def placed(refs, section):
    for n, ref in enumerate(refs):
        r = n if n < 5 else n - 4
        up, down = (r, (8 - r) % 8) if n < 5 else (8 - r, r)
        below = jnp.where(section == 0, up, down)
        for e in range(2):
            yield ref.at[e], (e if n < 5 else 1 - e), below


def group_at(info, other, below):
    section = info[1] if other == 0 else 1 - info[1]
    return section * 8 + lax.rem(info[2] - below + 8, 8)


def specs(smem, vmem, anywhere=0):
    return (
        [pl.BlockSpec(memory_space=pltpu.SMEM)] * smem
        + [pl.BlockSpec(memory_space=pltpu.VMEM)] * vmem
        + [pl.BlockSpec(memory_space=pl.ANY)] * anywhere
    )


def params(mib):
    return pltpu.CompilerParams(vmem_limit_bytes=mib << 20)


def start_copies(w, held, sems, order=None):
    copies = []
    for n in range(16):
        copy = pltpu.make_async_copy(w.at[n if order is None else order[n]], held.at[n], sems.at[n])
        copy.start()
        copies.append(copy)
    return copies


def key_kernel(tokens, order, *refs):
    a, b, w, out, held, sems = refs[:4], refs[4:8], refs[8], *refs[9:]
    depth, cols = held.shape[1:]
    half = tokens // 2
    copies = start_copies(w.at[:, :, w.shape[2] - cols :], held, sems, order)
    total = None
    for i in range(4):
        rows = jnp.concatenate(
            [
                jnp.concatenate([a[i][j, :half, :] for j in range(4)], axis=1),
                jnp.concatenate([b[j][i, :half, :] for j in range(4)], axis=1),
            ],
            axis=0,
        )
        for j in range(4):
            copies[4 * i + j].wait()
        block = held[4 * i : 4 * i + 4].reshape(4 * depth, cols)
        part = jnp.dot(rows, block, preferred_element_type=jnp.float32)
        total = part if total is None else total + part
    out[...] = total.astype(out.dtype)


def project_keys(order, blocks, w, cols, tokens):
    depth = w.shape[1]
    return pl.pallas_call(
        functools.partial(key_kernel, tokens),
        out_shape=jax.ShapeDtypeStruct((tokens, cols), jnp.bfloat16),
        in_specs=specs(1, 8, 1),
        out_specs=specs(0, 1)[0],
        scratch_shapes=[
            pltpu.VMEM((16, depth, cols), jnp.bfloat16),
            pltpu.SemaphoreType.DMA((16,)),
        ],
        compiler_params=params(47),
        cost_estimate=pl.CostEstimate(
            flops=2 * tokens * 16 * depth * cols,
            bytes_accessed=2 * 16 * depth * (tokens + cols),
            transcendentals=0,
        ),
        name="project_keys",
    )(order, *blocks, w)


def project_kernel(tokens, order, *refs):
    a, b, w, pre, dec, kv, held, sems = refs[:4], refs[4:8], refs[8], *refs[9:]
    q_cols = pre.shape[1]
    half, each = tokens // 2, a[0].shape[1]
    late = each - half
    copies = start_copies(w, held, sems, order)
    total, total_kv = None, None
    for n in range(16):
        i, j = n // 4, n % 4
        rows = jnp.concatenate([a[i][j], b[j][i]], axis=0)
        rows_kv = jnp.concatenate([a[i][j, half:, :], b[j][i, half:, :]], axis=0)
        copies[n].wait()
        part = jnp.dot(rows, held[n, :, :q_cols], preferred_element_type=jnp.float32)
        part_kv = jnp.dot(rows_kv, held[n, :, q_cols:], preferred_element_type=jnp.float32)
        total = part if total is None else total + part
        total_kv = part_kv if total_kv is None else total_kv + part_kv
    kv[...] = total_kv.astype(kv.dtype)
    result = total.astype(pre.dtype)
    for first in range(2):
        start = first * each
        pre[first * half : (first + 1) * half, :] = result[start : start + half]
        dec[first * late : (first + 1) * late, :] = result[start + half : start + each]


def project(order, blocks, w, q_cols, tokens):
    rows = 2 * blocks[0].shape[1]
    depth, cols = w.shape[1:]
    return pl.pallas_call(
        functools.partial(project_kernel, tokens),
        out_shape=[
            jax.ShapeDtypeStruct((tokens, q_cols), jnp.bfloat16),
            jax.ShapeDtypeStruct((rows - tokens, q_cols), jnp.bfloat16),
            jax.ShapeDtypeStruct((rows - tokens, cols - q_cols), jnp.bfloat16),
        ],
        in_specs=specs(1, 8, 1),
        out_specs=specs(0, 3),
        scratch_shapes=[
            pltpu.VMEM((16, depth, cols), jnp.bfloat16),
            pltpu.SemaphoreType.DMA((16,)),
        ],
        compiler_params=params(47),
        cost_estimate=pl.CostEstimate(
            flops=2 * rows * 16 * depth * cols,
            bytes_accessed=2 * 16 * depth * (rows + cols),
            transcendentals=0,
        ),
        name="project",
    )(order, *blocks, w)


def dot_t(a, b):
    return lax.dot_general(a, b, (((1,), (1,)), ((), ())), preferred_element_type=jnp.float32)


def lanes_max(value, top):
    for n in range(0, value.shape[-1], HD):
        top = jnp.maximum(top, value[..., n : n + HD])
    return top


def lanes_sum(value, total):
    for n in range(0, value.shape[-1], HD):
        total = total + value[..., n : n + HD]
    return total


def prefill_kernel(info, q, *refs):
    kv, out, qs, kvs, sc, mx, ls, acc = refs[:8], *refs[8:]
    tokens = q.shape[0]
    heads = q.shape[1] // HD
    group = info[0]
    for block, other, below in placed(kv, info[1]):
        kvs[group_at(info, other, below)] = block[...]
    for h in range(heads):
        qs[h] = q[:, h * HD : (h + 1) * HD]

    row = lax.broadcasted_iota(jnp.int32, (tokens, tokens), 0)
    col = lax.broadcasted_iota(jnp.int32, (tokens, tokens), 1)
    for h in range(heads):
        scores = jnp.where(col <= row, dot_t(qs[h], kvs[group, 0]), NEG)
        sc[group, h] = scores
        mx[h] = lanes_max(scores[:, HD:], scores[:, :HD])

    @pl.loop(0, group)
    def _(n):
        for h in range(heads):
            scores = dot_t(qs[h], kvs[n, 0])
            sc[n, h] = scores
            mx[h] = lanes_max(scores, mx[h])

    for h in range(heads):
        top = jnp.max(mx[h], axis=-1, keepdims=True) * SCALE
        mx[h] = jnp.broadcast_to(top, (tokens, HD))
        ls[h] = jnp.zeros((tokens, HD), jnp.float32)
        acc[h] = jnp.zeros((tokens, HD), jnp.float32)

    @pl.loop(0, group + 1)
    def _(n):
        for h in range(heads):
            top = jnp.concatenate([mx[h]] * (tokens // HD), axis=1)
            probs = jnp.exp(sc[n, h] * SCALE - top)
            ls[h] = lanes_sum(probs, ls[h])
            acc[h] += jnp.dot(
                probs.astype(jnp.bfloat16), kvs[n, 1], preferred_element_type=jnp.float32
            )

    for h in range(heads):
        total = jnp.sum(ls[h], axis=-1, keepdims=True)
        out[:, h * HD : (h + 1) * HD] = (acc[h] / total).astype(out.dtype)


def prefill_attention(info, q, kv):
    tokens, cols = q.shape
    heads = cols // HD
    return pl.pallas_call(
        prefill_kernel,
        out_shape=jax.ShapeDtypeStruct(q.shape, jnp.bfloat16),
        in_specs=specs(1, 9),
        out_specs=specs(0, 1)[0],
        scratch_shapes=[
            pltpu.VMEM((heads, tokens, HD), jnp.bfloat16),
            pltpu.VMEM((16, 2, tokens, HD), jnp.bfloat16),
            pltpu.VMEM((16, heads, tokens, tokens), jnp.float32),
            pltpu.VMEM((heads, tokens, HD), jnp.float32),
            pltpu.VMEM((heads, tokens, HD), jnp.float32),
            pltpu.VMEM((heads, tokens, HD), jnp.float32),
        ],
        compiler_params=params(36),
        cost_estimate=pl.CostEstimate(
            flops=4 * 4096 * tokens * cols, bytes_accessed=3 << 20, transcendentals=4096 * 1024
        ),
        name="prefill_attention",
    )(info, q, *kv)


def decode_kernel(info, placement, q, keys, values, table, lens, mine, other, *refs):
    kv, res, ks, vs, bias, sc = refs[:8], *refs[8:]
    slots = mine.shape[0]
    requests, pages = table.shape
    steps = q.shape[0] // requests
    heads = q.shape[1] // HD
    lane = info[3]
    for pool, first in ((mine, lane * slots), (other, (1 - lane) * slots)):
        for i in range(slots):
            ks[first + i] = pool[i, :, :HD]
            vs[first + i] = pool[i, :, HD:]

    for block, far, below in placed(kv, info[1]):
        group = group_at(info, far, below)
        for half in range(2):
            number = 2 * group + half

            @pl.when(placement[number, 0] == info[0])
            def _():
                target = placement[number, 1]
                ks[target] = block[0, half * PAGE : (half + 1) * PAGE, :]
                vs[target] = block[1, half * PAGE : (half + 1) * PAGE, :]

    offset = lax.broadcasted_iota(jnp.int32, (requests, PAGE), 1)
    length = jnp.broadcast_to(lens[...], (requests, PAGE))
    named = []
    for j in range(pages):
        slot = jnp.broadcast_to(table[:, j : j + 1], (requests, PAGE))
        named.append(jnp.where(offset + j * PAGE < length, slot, -1))
    for slot in range(2 * slots):
        count = jnp.zeros((requests, PAGE), jnp.float32)
        for j in range(slot // slots, pages, 2):
            count = count + jnp.where(named[j] == slot, 1.0, 0.0)
        bias[:, slot * PAGE : (slot + 1) * PAGE] = jnp.where(
            count > 0, jnp.log(jnp.maximum(count, 1.0)), NEG
        )

    chunk = 8
    width = chunk * PAGE
    for step in range(steps):
        q_rows = q[step * requests : (step + 1) * requests, :]
        stacked = jnp.concatenate([q_rows[:, h * HD : (h + 1) * HD] for h in range(heads)], axis=0)
        wide = stacked.astype(jnp.float32).reshape(heads, requests, HD)
        fresh = []
        for t in range(step + 1):
            key = keys[t * requests : (t + 1) * requests, :].astype(jnp.float32)
            fresh.append(jnp.sum(wide * key[None], axis=-1, keepdims=True) * SCALE)
        top = fresh[0]
        for score in fresh[1:]:
            top = jnp.maximum(top, score)
        lane_top = jnp.broadcast_to(top, (heads, requests, HD))
        for n in range(2 * slots // chunk):
            k = ks[n * chunk : (n + 1) * chunk].reshape(width, HD)
            scores = dot_t(stacked, k).reshape(heads, requests, width) * SCALE
            scores = scores + bias[:, n * width : (n + 1) * width][None]
            sc[n] = scores
            lane_top = lanes_max(scores, lane_top)
        top = jnp.max(lane_top, axis=-1, keepdims=True)
        total = jnp.zeros((heads, requests, 1), jnp.float32)
        weighted = jnp.zeros((heads, requests, HD), jnp.float32)
        for t, score in enumerate(fresh):
            prob = jnp.exp(score - top)
            value = values[t * requests : (t + 1) * requests, :].astype(jnp.float32)
            total = total + prob
            weighted = weighted + prob * value[None]
        wide_top = jnp.broadcast_to(top, (heads, requests, HD))
        lane_sum = jnp.zeros((heads, requests, HD), jnp.float32)
        for n in range(2 * slots // chunk):
            v = vs[n * chunk : (n + 1) * chunk].reshape(width, HD)
            probs = jnp.exp(sc[n] - jnp.concatenate([wide_top] * chunk, axis=-1))
            lane_sum = lanes_sum(probs, lane_sum)
            update = jnp.dot(
                probs.reshape(heads * requests, width).astype(jnp.bfloat16),
                v,
                preferred_element_type=jnp.float32,
            )
            weighted = weighted + update.reshape(heads, requests, HD)
        total = total + jnp.sum(lane_sum, axis=-1, keepdims=True)
        result = (weighted / total).astype(res.dtype)
        for h in range(heads):
            res[step * requests : (step + 1) * requests, h * HD : (h + 1) * HD] = result[h]


def decode_attention(info, placement, q, keys, values, table, lens, mine, other, kv):
    slots = mine.shape[0]
    requests = table.shape[0]
    cols = q.shape[1]
    return pl.pallas_call(
        decode_kernel,
        out_shape=jax.ShapeDtypeStruct(q.shape, jnp.bfloat16),
        in_specs=specs(2, 15),
        out_specs=specs(0, 1)[0],
        scratch_shapes=[
            pltpu.VMEM((2 * slots, PAGE, HD), jnp.bfloat16),
            pltpu.VMEM((2 * slots, PAGE, HD), jnp.bfloat16),
            pltpu.VMEM((requests, 2 * slots * PAGE), jnp.float32),
            pltpu.VMEM((2 * slots // 8, cols // HD, requests, 8 * PAGE), jnp.float32),
        ],
        compiler_params=params(32),
        cost_estimate=pl.CostEstimate(
            flops=4 * 768 * 4096 * HD, bytes_accessed=5 << 20, transcendentals=768 * 4096
        ),
        name="decode_attention",
    )(info, placement, q, keys, values, table, lens, mine, other, *kv)


def output_kernel(info, rows, w, *refs):
    outs, (held, product, sems) = refs[:8], refs[8:]
    half = rows.shape[0] // 2
    copies = start_copies(w, held, sems)
    for n in range(16):
        copies[n].wait()
        result = jnp.dot(rows[...], held[n], preferred_element_type=jnp.float32)
        product[n] = result.astype(product.dtype)
    for k in range(4):
        x, y = lax.rem(info[4] + k, 4), lax.rem(info[5] + k, 4)
        for n in range(4):
            outs[k][n] = product[4 * x + n, :half, :]
            outs[4 + k][n] = product[4 * n + y, half:, :]


def output_projection(info, rows, w):
    half, depth = rows.shape[0] // 2, rows.shape[1]
    cols = w.shape[2]
    return pl.pallas_call(
        output_kernel,
        out_shape=[jax.ShapeDtypeStruct((4, half, cols), jnp.bfloat16)] * 8,
        in_specs=specs(1, 1, 1),
        out_specs=specs(0, 8),
        scratch_shapes=[
            pltpu.VMEM((16, depth, cols), jnp.bfloat16),
            pltpu.VMEM((16, 2 * half, cols), jnp.bfloat16),
            pltpu.SemaphoreType.DMA((16,)),
        ],
        compiler_params=params(50),
        cost_estimate=pl.CostEstimate(
            flops=64 * half * depth * cols, bytes_accessed=12 << 20, transcendentals=0
        ),
        name="output_projection",
    )(info, rows, w)


def first_sum_kernel(info, *refs):
    parts, outs = refs[:8], refs[8:]
    for side in range(2):
        for k in range(4):
            n = lax.rem(info[5 - side] + k, 4)
            total = parts[4 * side][n].astype(jnp.float32)
            for part in parts[4 * side + 1 : 4 * side + 4]:
                total = total + part[n].astype(jnp.float32)
            outs[4 * side + k][...] = total.astype(outs[k].dtype)


def first_sum(info, parts):
    _, half, cols = parts[0].shape
    return pl.pallas_call(
        first_sum_kernel,
        out_shape=[jax.ShapeDtypeStruct((half, cols), jnp.bfloat16)] * 8,
        in_specs=specs(1, 8),
        out_specs=specs(0, 8),
        compiler_params=params(16),
        name="first_sum",
    )(info, *parts)


def second_sum_kernel(*refs):
    parts, out = refs[:8], refs[8]
    half = parts[0].shape[0]
    for side in range(2):
        total = parts[4 * side][...].astype(jnp.float32)
        for part in parts[4 * side + 1 : 4 * side + 4]:
            total = total + part[...].astype(jnp.float32)
        out[side * half : (side + 1) * half, :] = total.astype(out.dtype)


def second_sum(parts):
    half, cols = parts[0].shape
    return pl.pallas_call(
        second_sum_kernel,
        out_shape=jax.ShapeDtypeStruct((2 * half, cols), jnp.bfloat16),
        in_specs=specs(0, 8),
        out_specs=specs(0, 1)[0],
        compiler_params=params(16),
        name="second_sum",
    )(*parts)


def send_parts(parts, first):
    sent = list(parts)
    for k in (2, 1, 3):
        sent[k] = lax.ppermute(parts[k], "tp", tp_perm(k, 0) if first else tp_perm(0, k))
        sent[4 + k] = lax.ppermute(parts[4 + k], "tp", tp_perm(0, k) if first else tp_perm(k, 0))
    return sent


def on_device(
    x_prefill, x_decode, w_query, w_keyval, w_out, cache_pool, placement, page_table, cache_len
):
    tokens = x_prefill.shape[0]
    steps, requests, width = x_decode.shape
    section, tp, plane = lax.axis_index("section"), lax.axis_index("tp"), lax.axis_index("dp")
    x, y = lax.div(tp, 4), lax.rem(tp, 4)
    lane = lax.rem(tp, 2)
    group = section * 8 + plane
    info = jnp.stack([group, section, plane, lane, x, y, tp]).astype(jnp.int32)
    turn = jnp.where(section == 0, 1, -1)
    count = jnp.arange(16, dtype=jnp.int32)
    order = lax.rem(x - turn * (count // 4) + 4, 4) * 4 + lax.rem(y - turn * (count % 4) + 4, 4)

    q_cols = w_query.shape[1]
    w_all = lax.all_gather(jnp.concatenate([w_query, w_keyval], axis=1), SD, axis=0, tiled=False)
    wo_all = lax.all_gather(w_out, SD, axis=0, tiled=False)

    rows = x_decode.reshape(steps * requests, width)
    half_p, half_d = tokens // 2, rows.shape[0] // 2
    blocks = gather_tp(
        jnp.concatenate([x_prefill[:half_p], rows[:half_d]], axis=0),
        jnp.concatenate([x_prefill[half_p:], rows[half_d:]], axis=0),
    )
    kv_mine = project_keys(order, blocks, w_all, w_keyval.shape[1], tokens)
    kv_lane = lax.ppermute(kv_mine, "tp", LANE)
    kv_core = lax.ppermute(kv_mine, "section", SWAP)
    kv_both = lax.ppermute(kv_mine, ST, BOTH)
    mine, kv_lane, kv_core, kv_both = lax.optimization_barrier(
        (cache_pool[0], kv_lane, kv_core, kv_both)
    )
    is_key = lane == 0
    pair = jnp.stack(
        [
            jnp.stack([jnp.where(is_key, p, q), jnp.where(is_key, q, p)])
            for p, q in ((kv_mine, kv_lane), (kv_core, kv_both))
        ]
    )
    kv, (q_pre, q_dec, new_mine) = gather_planes(pair, project(order, blocks, w_all, q_cols, tokens))
    new_lane = lax.ppermute(new_mine, "tp", LANE)
    other = lax.ppermute(mine, "tp", LANE)
    keys = jnp.where(is_key, new_mine, new_lane)
    values = jnp.where(is_key, new_lane, new_mine)

    attention = decode_attention(
        info, placement, q_dec, keys, values, page_table, cache_len[:, None], mine, other, kv
    )
    parts = send_parts(output_projection(info, attention, wo_all), True)
    prefill_out = prefill_attention(info, q_pre, kv)
    prefill_out, *parts = lax.optimization_barrier((prefill_out, *parts))
    parts = send_parts(first_sum(info, parts), False)
    decode_out = second_sum(parts).reshape(steps, requests, -1)
    return (prefill_out, decode_out)


def solution(mesh):
    return jax.shard_map(
        on_device,
        mesh=mesh,
        in_specs=(
            P(("section", "dp"), "tp"),
            P(None, ("section", "dp"), "tp"),
            P(("section", "dp"), "tp"),
            P(("section", "dp"), "tp"),
            P("tp", ("section", "dp")),
            P("tp", ("section", "dp"), None, None),
            P(),
            P(("section", "dp"), None),
            P(("section", "dp")),
        ),
        out_specs=(P(("section", "dp"), "tp"), P(None, ("section", "dp"), "tp")),
        check_vma=False,
    )
```

```python
import functools
import math

import jax
import jax.numpy as jnp
from jax import lax
from jax.experimental import pallas as pl
from jax.experimental.pallas import tpu as pltpu
from jax.sharding import PartitionSpec as P

HD = 128
PAGE = 128
NEG = -1e30
SCALE = 1.0 / math.sqrt(HD)

ST = ("section", "tp")
SD = ("section", "dp")

SWAP = [(0, 1), (1, 0)]
LANE = [(t, t ^ 1) for t in range(16)]
BOTH = [(t, t ^ 17) for t in range(32)]
SPIN = [(s * 8 + z, s * 8 + (z + 1 - 2 * s) % 8) for s in range(2) for z in range(8)]


def tp_perm(dx, dy):
    return [
        (x * 4 + y, (x + dx) % 4 * 4 + (y + dy) % 4) for x in range(4) for y in range(4)
    ]


def ring_perm(dx, dy):
    pairs = []
    for s in range(2):
        d = 1 - 2 * s
        pairs += [(s * 16 + a, s * 16 + b) for a, b in tp_perm(d * dx, d * dy)]
    return pairs


RING_X = ring_perm(1, 0)
RING_Y = ring_perm(0, 1)


def gather_tp(first, second, beside):
    a, b = [first], [second]
    for _ in range(3):
        a.append(lax.ppermute(a[-1], ST, RING_Y))
        b.append(lax.ppermute(b[-1], ST, RING_X))
    a, b, *beside = lax.optimization_barrier((jnp.stack(a), jnp.stack(b), *beside))
    a, b = [a], [b]
    for _ in range(3):
        a.append(lax.ppermute(a[-1], ST, RING_X))
        b.append(lax.ppermute(b[-1], ST, RING_Y))
    return a + b, beside


def gather_planes(pair, beside):
    mine = [pair]
    theirs = []
    for r in range(1, 5):
        mine.append(lax.ppermute(mine[-1], SD, SPIN))
        if r == 1:
            mine[1], *beside = lax.optimization_barrier((mine[1], *beside))
        if r < 4:
            theirs.append(lax.ppermute(mine[-1], "section", SWAP))
    return mine + theirs, beside


def placed(refs, section):
    for n, ref in enumerate(refs):
        r = n if n < 5 else n - 4
        up, down = (r, (8 - r) % 8) if n < 5 else (8 - r, r)
        below = jnp.where(section == 0, up, down)
        for e in range(2):
            yield ref.at[e], (e if n < 5 else 1 - e), below


def group_at(info, other, below):
    section = info[1] if other == 0 else 1 - info[1]
    return section * 8 + lax.rem(info[2] - below + 8, 8)


def specs(smem, vmem, anywhere=0):
    return (
        [pl.BlockSpec(memory_space=pltpu.SMEM)] * smem
        + [pl.BlockSpec(memory_space=pltpu.VMEM)] * vmem
        + [pl.BlockSpec(memory_space=pl.ANY)] * anywhere
    )


def params(mib):
    return pltpu.CompilerParams(vmem_limit_bytes=mib << 20)


def start_copies(w, held, sems, order=None):
    copies = []
    for n in range(16):
        copy = pltpu.make_async_copy(w.at[n if order is None else order[n]], held.at[n], sems.at[n])
        copy.start()
        copies.append(copy)
    return copies


def project_kernel(start, stop, first, order, *refs):
    a, b, w, outs, (held, sems) = refs[:4], refs[4:8], refs[8], refs[9:-2], refs[-2:]
    depth, cols = held.shape[1:]
    copies = start_copies(w.at[:, :, first : first + cols], held, sems, order)
    total = None
    for i in range(4):
        rows = jnp.concatenate(
            [
                jnp.concatenate([a[i][j, start:stop, :] for j in range(4)], axis=1),
                jnp.concatenate([b[j][i, start:stop, :] for j in range(4)], axis=1),
            ],
            axis=0,
        )
        for j in range(4):
            copies[4 * i + j].wait()
        block = held[4 * i : 4 * i + 4].reshape(4 * depth, cols)
        part = jnp.dot(rows, block, preferred_element_type=jnp.float32)
        total = part if total is None else total + part
    result = total.astype(outs[0].dtype)
    at = 0
    for out in outs:
        out[...] = result[:, at : at + out.shape[1]]
        at += out.shape[1]


def project(order, blocks, w, start, stop, first, widths):
    rows, cols, depth = 2 * (stop - start), sum(widths), w.shape[1]
    return pl.pallas_call(
        functools.partial(project_kernel, start, stop, first),
        out_shape=[jax.ShapeDtypeStruct((rows, width), jnp.bfloat16) for width in widths],
        in_specs=specs(1, 8, 1),
        out_specs=specs(0, len(widths)),
        scratch_shapes=[
            pltpu.VMEM((16, depth, cols), jnp.bfloat16),
            pltpu.SemaphoreType.DMA((16,)),
        ],
        compiler_params=params(47),
        cost_estimate=pl.CostEstimate(
            flops=2 * rows * 16 * depth * cols,
            bytes_accessed=2 * 16 * depth * (rows + cols),
            transcendentals=0,
        ),
        name="project",
    )(order, *blocks, w)


def dot_t(a, b):
    return lax.dot_general(a, b, (((1,), (1,)), ((), ())), preferred_element_type=jnp.float32)


def lanes_max(value, top):
    for n in range(0, value.shape[-1], HD):
        top = jnp.maximum(top, value[..., n : n + HD])
    return top


def lanes_sum(value, total):
    for n in range(0, value.shape[-1], HD):
        total = total + value[..., n : n + HD]
    return total


def prefill_kernel(info, q, *refs):
    kv, out, qs, kvs, sc, mx, ls, acc = refs[:8], *refs[8:]
    tokens = q.shape[0]
    heads = q.shape[1] // HD
    group = info[0]
    for block, other, below in placed(kv, info[1]):
        kvs[group_at(info, other, below)] = block[...]
    for h in range(heads):
        qs[h] = q[:, h * HD : (h + 1) * HD]

    row = lax.broadcasted_iota(jnp.int32, (tokens, tokens), 0)
    col = lax.broadcasted_iota(jnp.int32, (tokens, tokens), 1)
    for h in range(heads):
        scores = jnp.where(col <= row, dot_t(qs[h], kvs[group, 0]), NEG)
        sc[group, h] = scores
        mx[h] = lanes_max(scores[:, HD:], scores[:, :HD])

    @pl.loop(0, group)
    def _(n):
        for h in range(heads):
            scores = dot_t(qs[h], kvs[n, 0])
            sc[n, h] = scores
            mx[h] = lanes_max(scores, mx[h])

    for h in range(heads):
        top = jnp.max(mx[h], axis=-1, keepdims=True) * SCALE
        mx[h] = jnp.broadcast_to(top, (tokens, HD))
        ls[h] = jnp.zeros((tokens, HD), jnp.float32)
        acc[h] = jnp.zeros((tokens, HD), jnp.float32)

    @pl.loop(0, group + 1)
    def _(n):
        for h in range(heads):
            top = jnp.concatenate([mx[h]] * (tokens // HD), axis=1)
            probs = jnp.exp(sc[n, h] * SCALE - top)
            ls[h] = lanes_sum(probs, ls[h])
            acc[h] += jnp.dot(
                probs.astype(jnp.bfloat16), kvs[n, 1], preferred_element_type=jnp.float32
            )

    for h in range(heads):
        total = jnp.sum(ls[h], axis=-1, keepdims=True)
        out[:, h * HD : (h + 1) * HD] = (acc[h] / total).astype(out.dtype)


def prefill_attention(info, q, kv):
    tokens, cols = q.shape
    heads = cols // HD
    return pl.pallas_call(
        prefill_kernel,
        out_shape=jax.ShapeDtypeStruct(q.shape, jnp.bfloat16),
        in_specs=specs(1, 9),
        out_specs=specs(0, 1)[0],
        scratch_shapes=[
            pltpu.VMEM((heads, tokens, HD), jnp.bfloat16),
            pltpu.VMEM((16, 2, tokens, HD), jnp.bfloat16),
            pltpu.VMEM((16, heads, tokens, tokens), jnp.float32),
            pltpu.VMEM((heads, tokens, HD), jnp.float32),
            pltpu.VMEM((heads, tokens, HD), jnp.float32),
            pltpu.VMEM((heads, tokens, HD), jnp.float32),
        ],
        compiler_params=params(36),
        cost_estimate=pl.CostEstimate(
            flops=4 * 4096 * tokens * cols, bytes_accessed=3 << 20, transcendentals=4096 * 1024
        ),
        name="prefill_attention",
    )(info, q, *kv)


def decode_kernel(info, placement, q, keys, values, table, lens, mine, other, *refs):
    kv, res, ks, vs, bias, sc = refs[:8], *refs[8:]
    slots = mine.shape[0]
    requests, pages = table.shape
    steps = q.shape[0] // requests
    heads = q.shape[1] // HD
    lane = info[3]
    for pool, first in ((mine, lane * slots), (other, (1 - lane) * slots)):
        for i in range(slots):
            ks[first + i] = pool[i, :, :HD]
            vs[first + i] = pool[i, :, HD:]

    for block, far, below in placed(kv, info[1]):
        group = group_at(info, far, below)
        for half in range(2):
            number = 2 * group + half

            @pl.when(placement[number, 0] == info[0])
            def _():
                target = placement[number, 1]
                ks[target] = block[0, half * PAGE : (half + 1) * PAGE, :]
                vs[target] = block[1, half * PAGE : (half + 1) * PAGE, :]

    offset = lax.broadcasted_iota(jnp.int32, (requests, PAGE), 1)
    length = jnp.broadcast_to(lens[...], (requests, PAGE))
    named = []
    for j in range(pages):
        slot = jnp.broadcast_to(table[:, j : j + 1], (requests, PAGE))
        named.append(jnp.where(offset + j * PAGE < length, slot, -1))
    for slot in range(2 * slots):
        count = jnp.zeros((requests, PAGE), jnp.float32)
        for j in range(slot // slots, pages, 2):
            count = count + jnp.where(named[j] == slot, 1.0, 0.0)
        bias[:, slot * PAGE : (slot + 1) * PAGE] = jnp.where(
            count > 0, jnp.log(jnp.maximum(count, 1.0)), NEG
        )

    chunk = 8
    width = chunk * PAGE
    for step in range(steps):
        q_rows = q[step * requests : (step + 1) * requests, :]
        stacked = jnp.concatenate([q_rows[:, h * HD : (h + 1) * HD] for h in range(heads)], axis=0)
        wide = stacked.astype(jnp.float32).reshape(heads, requests, HD)
        fresh = []
        for t in range(step + 1):
            key = keys[t * requests : (t + 1) * requests, :].astype(jnp.float32)
            fresh.append(jnp.sum(wide * key[None], axis=-1, keepdims=True) * SCALE)
        top = fresh[0]
        for score in fresh[1:]:
            top = jnp.maximum(top, score)
        lane_top = jnp.broadcast_to(top, (heads, requests, HD))
        for n in range(2 * slots // chunk):
            k = ks[n * chunk : (n + 1) * chunk].reshape(width, HD)
            scores = dot_t(stacked, k).reshape(heads, requests, width) * SCALE
            scores = scores + bias[:, n * width : (n + 1) * width][None]
            sc[n] = scores
            lane_top = lanes_max(scores, lane_top)
        top = jnp.max(lane_top, axis=-1, keepdims=True)
        total = jnp.zeros((heads, requests, 1), jnp.float32)
        weighted = jnp.zeros((heads, requests, HD), jnp.float32)
        for t, score in enumerate(fresh):
            prob = jnp.exp(score - top)
            value = values[t * requests : (t + 1) * requests, :].astype(jnp.float32)
            total = total + prob
            weighted = weighted + prob * value[None]
        wide_top = jnp.broadcast_to(top, (heads, requests, HD))
        lane_sum = jnp.zeros((heads, requests, HD), jnp.float32)
        for n in range(2 * slots // chunk):
            v = vs[n * chunk : (n + 1) * chunk].reshape(width, HD)
            probs = jnp.exp(sc[n] - jnp.concatenate([wide_top] * chunk, axis=-1))
            lane_sum = lanes_sum(probs, lane_sum)
            update = jnp.dot(
                probs.reshape(heads * requests, width).astype(jnp.bfloat16),
                v,
                preferred_element_type=jnp.float32,
            )
            weighted = weighted + update.reshape(heads, requests, HD)
        total = total + jnp.sum(lane_sum, axis=-1, keepdims=True)
        result = (weighted / total).astype(res.dtype)
        for h in range(heads):
            res[step * requests : (step + 1) * requests, h * HD : (h + 1) * HD] = result[h]


def decode_attention(info, placement, q, keys, values, table, lens, mine, other, kv):
    slots = mine.shape[0]
    requests = table.shape[0]
    cols = q.shape[1]
    return pl.pallas_call(
        decode_kernel,
        out_shape=jax.ShapeDtypeStruct(q.shape, jnp.bfloat16),
        in_specs=specs(2, 15),
        out_specs=specs(0, 1)[0],
        scratch_shapes=[
            pltpu.VMEM((2 * slots, PAGE, HD), jnp.bfloat16),
            pltpu.VMEM((2 * slots, PAGE, HD), jnp.bfloat16),
            pltpu.VMEM((requests, 2 * slots * PAGE), jnp.float32),
            pltpu.VMEM((2 * slots // 8, cols // HD, requests, 8 * PAGE), jnp.float32),
        ],
        compiler_params=params(32),
        cost_estimate=pl.CostEstimate(
            flops=4 * 768 * 4096 * HD, bytes_accessed=5 << 20, transcendentals=768 * 4096
        ),
        name="decode_attention",
    )(info, placement, q, keys, values, table, lens, mine, other, *kv)


def output_kernel(info, *refs):
    rows, w, outs, held, sems = refs[:4], refs[4], refs[5:9], refs[9], refs[10]
    width = w.shape[2]
    copies = []
    for n in range(16):
        k, c = n // 4, n % 4
        block = w.at[lax.rem(info[4] + k, 4) * 4 + c]
        copy = pltpu.make_async_copy(
            block, held.at[k, :, c * width : (c + 1) * width], sems.at[n]
        )
        copy.start()
        copies.append(copy)
    wide = jnp.concatenate([row[...] for row in rows], axis=1)
    for k in range(4):
        for c in range(4):
            copies[4 * k + c].wait()
        result = jnp.dot(wide, held[k], preferred_element_type=jnp.float32)
        outs[k][...] = result.astype(outs[k].dtype)


def output_projection(info, rows, w):
    count, depth = rows[0].shape
    cols = 4 * w.shape[2]
    return pl.pallas_call(
        output_kernel,
        out_shape=[jax.ShapeDtypeStruct((count, cols), jnp.bfloat16)] * 4,
        in_specs=specs(1, 4, 1),
        out_specs=specs(0, 4),
        scratch_shapes=[
            pltpu.VMEM((4, 4 * depth, cols), jnp.bfloat16),
            pltpu.SemaphoreType.DMA((16,)),
        ],
        compiler_params=params(50),
        cost_estimate=pl.CostEstimate(
            flops=32 * count * depth * cols, bytes_accessed=10 << 20, transcendentals=0
        ),
        name="output_projection",
    )(info, *rows, w)


def quarter(info, k, width):
    return pl.ds(pl.multiple_of(lax.rem(info[5] + k, 4) * width, width), width)


def sum_kernel(info, *refs):
    parts, outs, held = refs[:4], refs[4:8], refs[8]
    total = parts[0][...].astype(jnp.float32)
    for part in parts[1:]:
        total = total + part[...].astype(jnp.float32)
    held[...] = total
    for k in range(4):
        outs[k][...] = held[:, quarter(info, k, outs[k].shape[1])].astype(outs[k].dtype)


def sum_parts(info, parts):
    rows, cols = parts[0].shape
    return pl.pallas_call(
        sum_kernel,
        out_shape=[jax.ShapeDtypeStruct((rows, cols // 4), jnp.bfloat16)] * 4,
        in_specs=specs(1, 4),
        out_specs=specs(0, 4),
        scratch_shapes=[pltpu.VMEM((rows, cols), jnp.float32)],
        compiler_params=params(16),
        name="sum_parts",
    )(info, *parts)


def assemble_kernel(info, *refs):
    pieces, out = refs[:4], refs[4]
    for k in range(4):
        out[:, quarter(info, 4 - k, pieces[k].shape[1])] = pieces[k][...]


def assemble(info, pieces):
    rows, cols = pieces[0].shape
    return pl.pallas_call(
        assemble_kernel,
        out_shape=jax.ShapeDtypeStruct((rows, 4 * cols), jnp.bfloat16),
        in_specs=specs(1, 4),
        out_specs=specs(0, 1)[0],
        compiler_params=params(16),
        name="assemble",
    )(info, *pieces)


def along(values, dx, dy):
    sent = list(values)
    for k in (2, 1, 3):
        sent[k] = lax.ppermute(values[k], "tp", tp_perm(k * dx, k * dy))
    return sent


def on_device(
    x_prefill, x_decode, w_query, w_keyval, w_out, cache_pool, placement, page_table, cache_len
):
    tokens = x_prefill.shape[0]
    steps, requests, width = x_decode.shape
    section, tp, plane = lax.axis_index("section"), lax.axis_index("tp"), lax.axis_index("dp")
    x, y = lax.div(tp, 4), lax.rem(tp, 4)
    lane = lax.rem(tp, 2)
    group = section * 8 + plane
    info = jnp.stack([group, section, plane, lane, x, y, tp]).astype(jnp.int32)
    turn = jnp.where(section == 0, 1, -1)
    count = jnp.arange(16, dtype=jnp.int32)
    order = lax.rem(x - turn * (count // 4) + 4, 4) * 4 + lax.rem(y - turn * (count % 4) + 4, 4)

    q_cols = w_query.shape[1]
    kv_cols = w_keyval.shape[1]
    w_all = lax.all_gather(jnp.concatenate([w_query, w_keyval], axis=1), SD, axis=0, tiled=False)

    part = w_out.shape[1] // 4
    w_cut = along(
        [lax.dynamic_slice_in_dim(w_out, lax.rem(y + k, 4) * part, part, 1) for k in range(4)], 0, 1
    )
    rows = x_decode.reshape(steps * requests, width)
    half_p, half_d = tokens // 2, rows.shape[0] // 2
    blocks, w_cut = gather_tp(
        jnp.concatenate([x_prefill[:half_p], rows[:half_d]], axis=0),
        jnp.concatenate([x_prefill[half_p:], rows[half_d:]], axis=0),
        w_cut,
    )
    (kv_mine,) = project(order, blocks, w_all, 0, half_p, q_cols, [kv_cols])
    kv_lane = lax.ppermute(kv_mine, "tp", LANE)
    kv_core = lax.ppermute(kv_mine, "section", SWAP)
    kv_both = lax.ppermute(kv_mine, ST, BOTH)
    mine, kv_lane, kv_core, kv_both = lax.optimization_barrier(
        (cache_pool[0], kv_lane, kv_core, kv_both)
    )
    is_key = lane == 0
    pair = jnp.stack(
        [
            jnp.stack([jnp.where(is_key, p, q), jnp.where(is_key, q, p)])
            for p, q in ((kv_mine, kv_lane), (kv_core, kv_both))
        ]
    )
    kv, (q_dec, new_mine, *w_cut) = gather_planes(
        pair,
        [*project(order, blocks, w_all, half_p, half_p + half_d, 0, [q_cols, kv_cols]), *w_cut],
    )
    wo_all = lax.all_gather(jnp.concatenate(w_cut, axis=0), SD, axis=0, tiled=False)
    new_lane = lax.ppermute(new_mine, "tp", LANE)
    other = lax.ppermute(mine, "tp", LANE)
    keys = jnp.where(is_key, new_mine, new_lane)
    values = jnp.where(is_key, new_lane, new_mine)

    attention = decode_attention(
        info, placement, q_dec, keys, values, page_table, cache_len[:, None], mine, other, kv
    )
    attended = along([attention] * 4, 0, 1)
    (q_pre,) = project(order, blocks, w_all, 0, half_p, 0, [q_cols])
    prefill_out = prefill_attention(info, q_pre, kv)
    prefill_out, *attended = lax.optimization_barrier((prefill_out, *attended))
    parts = along(output_projection(info, attended, wo_all), 1, 0)
    pieces = along(sum_parts(info, parts), 0, 1)
    decode_out = assemble(info, pieces).reshape(steps, requests, -1)
    return (prefill_out, decode_out)


def solution(mesh):
    return jax.shard_map(
        on_device,
        mesh=mesh,
        in_specs=(
            P(("section", "dp"), "tp"),
            P(None, ("section", "dp"), "tp"),
            P(("section", "dp"), "tp"),
            P(("section", "dp"), "tp"),
            P("tp", ("section", "dp")),
            P("tp", ("section", "dp"), None, None),
            P(),
            P(("section", "dp"), None),
            P(("section", "dp")),
        ),
        out_specs=(P(("section", "dp"), "tp"), P(None, ("section", "dp"), "tp")),
        check_vma=False,
    )
```

```python
import functools
import math

import jax
import jax.numpy as jnp
from jax import lax
from jax.experimental import pallas as pl
from jax.experimental.pallas import tpu as pltpu
from jax.sharding import PartitionSpec as P

HD = 128
PAGE = 128
NEG = -1e30
SCALE = 1.0 / math.sqrt(HD)

ST = ("section", "tp")
SD = ("section", "dp")

SWAP = [(0, 1), (1, 0)]
LANE = [(t, t ^ 1) for t in range(16)]
BOTH = [(t, t ^ 17) for t in range(32)]
SPIN = [
    [(s * 8 + z, s * 8 + (z + r - 2 * r * s) % 8) for s in range(2) for z in range(8)]
    for r in range(3)
]


def tp_perm(dx, dy):
    return [
        (x * 4 + y, (x + dx) % 4 * 4 + (y + dy) % 4) for x in range(4) for y in range(4)
    ]


def ring_perm(dx, dy):
    pairs = []
    for s in range(2):
        d = 1 - 2 * s
        pairs += [(s * 16 + a, s * 16 + b) for a, b in tp_perm(d * dx, d * dy)]
    return pairs


RING_X = ring_perm(1, 0)
RING_Y = ring_perm(0, 1)


def gather_tp(first, second, beside):
    a, b = [first], [second]
    for r in range(1, 4):
        a.append(lax.ppermute(first, ST, ring_perm(0, r)))
        b.append(lax.ppermute(second, ST, ring_perm(r, 0)))
    a, b, *beside = lax.optimization_barrier((jnp.stack(a), jnp.stack(b), *beside))
    a, b = [a], [b]
    for _ in range(3):
        a.append(lax.ppermute(a[-1], ST, RING_X))
        b.append(lax.ppermute(b[-1], ST, RING_Y))
    return a + b, beside


def gather_planes(pair, beside):
    mine = [pair, lax.ppermute(pair, SD, SPIN[1]), lax.ppermute(pair, SD, SPIN[2])]
    mine[1], mine[2], *beside = lax.optimization_barrier((mine[1], mine[2], *beside))
    mine += [lax.ppermute(mine[1], SD, SPIN[2]), lax.ppermute(mine[2], SD, SPIN[2])]
    return mine + [lax.ppermute(block, "section", SWAP) for block in mine[1:4]], beside


def placed(refs, section):
    for n, ref in enumerate(refs):
        r = n if n < 5 else n - 4
        up, down = (r, (8 - r) % 8) if n < 5 else (8 - r, r)
        below = jnp.where(section == 0, up, down)
        for e in range(2):
            yield ref.at[e], (e if n < 5 else 1 - e), below


def group_at(info, other, below):
    section = info[1] if other == 0 else 1 - info[1]
    return section * 8 + lax.rem(info[2] - below + 8, 8)


def specs(smem, vmem, anywhere=0):
    return (
        [pl.BlockSpec(memory_space=pltpu.SMEM)] * smem
        + [pl.BlockSpec(memory_space=pltpu.VMEM)] * vmem
        + [pl.BlockSpec(memory_space=pl.ANY)] * anywhere
    )


def params(mib):
    return pltpu.CompilerParams(vmem_limit_bytes=mib << 20)


def start_copies(w, held, sems, order=None):
    copies = []
    for n in range(16):
        copy = pltpu.make_async_copy(w.at[n if order is None else order[n]], held.at[n], sems.at[n])
        copy.start()
        copies.append(copy)
    return copies


def project_kernel(start, stop, first, order, *refs):
    a, b, w, outs, (held, sems) = refs[:4], refs[4:8], refs[8], refs[9:-2], refs[-2:]
    depth, cols = held.shape[1:]
    copies = start_copies(w.at[:, :, first : first + cols], held, sems, order)
    total = None
    for i in range(4):
        rows = jnp.concatenate(
            [
                jnp.concatenate([a[i][j, start:stop, :] for j in range(4)], axis=1),
                jnp.concatenate([b[j][i, start:stop, :] for j in range(4)], axis=1),
            ],
            axis=0,
        )
        for j in range(4):
            copies[4 * i + j].wait()
        block = held[4 * i : 4 * i + 4].reshape(4 * depth, cols)
        part = jnp.dot(rows, block, preferred_element_type=jnp.float32)
        total = part if total is None else total + part
    result = total.astype(outs[0].dtype)
    at = 0
    for out in outs:
        out[...] = result[:, at : at + out.shape[1]]
        at += out.shape[1]


def project(order, blocks, w, start, stop, first, widths):
    rows, cols, depth = 2 * (stop - start), sum(widths), w.shape[1]
    return pl.pallas_call(
        functools.partial(project_kernel, start, stop, first),
        out_shape=[jax.ShapeDtypeStruct((rows, width), jnp.bfloat16) for width in widths],
        in_specs=specs(1, 8, 1),
        out_specs=specs(0, len(widths)),
        scratch_shapes=[
            pltpu.VMEM((16, depth, cols), jnp.bfloat16),
            pltpu.SemaphoreType.DMA((16,)),
        ],
        compiler_params=params(47),
        cost_estimate=pl.CostEstimate(
            flops=2 * rows * 16 * depth * cols,
            bytes_accessed=2 * 16 * depth * (rows + cols),
            transcendentals=0,
        ),
        name="project",
    )(order, *blocks, w)


def dot_t(a, b):
    return lax.dot_general(a, b, (((1,), (1,)), ((), ())), preferred_element_type=jnp.float32)


def lanes_max(value, top):
    for n in range(0, value.shape[-1], HD):
        top = jnp.maximum(top, value[..., n : n + HD])
    return top


def lanes_sum(value, total):
    for n in range(0, value.shape[-1], HD):
        total = total + value[..., n : n + HD]
    return total


def prefill_kernel(info, q, *refs):
    kv, out, qs, kvs, sc, mx, ls, acc = refs[:8], *refs[8:]
    tokens = q.shape[0]
    heads = q.shape[1] // HD
    group = info[0]
    for block, other, below in placed(kv, info[1]):
        kvs[group_at(info, other, below)] = block[...]
    for h in range(heads):
        qs[h] = q[:, h * HD : (h + 1) * HD]

    row = lax.broadcasted_iota(jnp.int32, (tokens, tokens), 0)
    col = lax.broadcasted_iota(jnp.int32, (tokens, tokens), 1)
    for h in range(heads):
        scores = jnp.where(col <= row, dot_t(qs[h], kvs[group, 0]), NEG)
        sc[group, h] = scores
        mx[h] = lanes_max(scores[:, HD:], scores[:, :HD])

    @pl.loop(0, group)
    def _(n):
        for h in range(heads):
            scores = dot_t(qs[h], kvs[n, 0])
            sc[n, h] = scores
            mx[h] = lanes_max(scores, mx[h])

    for h in range(heads):
        top = jnp.max(mx[h], axis=-1, keepdims=True) * SCALE
        mx[h] = jnp.broadcast_to(top, (tokens, HD))
        ls[h] = jnp.zeros((tokens, HD), jnp.float32)
        acc[h] = jnp.zeros((tokens, HD), jnp.float32)

    @pl.loop(0, group + 1)
    def _(n):
        for h in range(heads):
            top = jnp.concatenate([mx[h]] * (tokens // HD), axis=1)
            probs = jnp.exp(sc[n, h] * SCALE - top)
            ls[h] = lanes_sum(probs, ls[h])
            acc[h] += jnp.dot(
                probs.astype(jnp.bfloat16), kvs[n, 1], preferred_element_type=jnp.float32
            )

    for h in range(heads):
        total = jnp.sum(ls[h], axis=-1, keepdims=True)
        out[:, h * HD : (h + 1) * HD] = (acc[h] / total).astype(out.dtype)


def prefill_attention(info, q, kv):
    tokens, cols = q.shape
    heads = cols // HD
    return pl.pallas_call(
        prefill_kernel,
        out_shape=jax.ShapeDtypeStruct(q.shape, jnp.bfloat16),
        in_specs=specs(1, 9),
        out_specs=specs(0, 1)[0],
        scratch_shapes=[
            pltpu.VMEM((heads, tokens, HD), jnp.bfloat16),
            pltpu.VMEM((16, 2, tokens, HD), jnp.bfloat16),
            pltpu.VMEM((16, heads, tokens, tokens), jnp.float32),
            pltpu.VMEM((heads, tokens, HD), jnp.float32),
            pltpu.VMEM((heads, tokens, HD), jnp.float32),
            pltpu.VMEM((heads, tokens, HD), jnp.float32),
        ],
        compiler_params=params(36),
        cost_estimate=pl.CostEstimate(
            flops=4 * 4096 * tokens * cols, bytes_accessed=3 << 20, transcendentals=4096 * 1024
        ),
        name="prefill_attention",
    )(info, q, *kv)


def decode_kernel(info, placement, q, keys, values, table, lens, mine, other, *refs):
    kv, res, ks, vs, bias, sc = refs[:8], *refs[8:]
    slots = mine.shape[0]
    requests, pages = table.shape
    steps = q.shape[0] // requests
    heads = q.shape[1] // HD
    lane = info[3]
    for pool, first in ((mine, lane * slots), (other, (1 - lane) * slots)):
        for i in range(slots):
            ks[first + i] = pool[i, :, :HD]
            vs[first + i] = pool[i, :, HD:]

    for block, far, below in placed(kv, info[1]):
        group = group_at(info, far, below)
        for half in range(2):
            number = 2 * group + half

            @pl.when(placement[number, 0] == info[0])
            def _():
                target = placement[number, 1]
                ks[target] = block[0, half * PAGE : (half + 1) * PAGE, :]
                vs[target] = block[1, half * PAGE : (half + 1) * PAGE, :]

    offset = lax.broadcasted_iota(jnp.int32, (requests, PAGE), 1)
    length = jnp.broadcast_to(lens[...], (requests, PAGE))
    named = []
    for j in range(pages):
        slot = jnp.broadcast_to(table[:, j : j + 1], (requests, PAGE))
        named.append(jnp.where(offset + j * PAGE < length, slot, -1))
    for slot in range(2 * slots):
        count = jnp.zeros((requests, PAGE), jnp.float32)
        for j in range(slot // slots, pages, 2):
            count = count + jnp.where(named[j] == slot, 1.0, 0.0)
        bias[:, slot * PAGE : (slot + 1) * PAGE] = jnp.where(
            count > 0, jnp.log(jnp.maximum(count, 1.0)), NEG
        )

    chunk = 8
    width = chunk * PAGE
    for step in range(steps):
        q_rows = q[step * requests : (step + 1) * requests, :]
        stacked = jnp.concatenate([q_rows[:, h * HD : (h + 1) * HD] for h in range(heads)], axis=0)
        wide = stacked.astype(jnp.float32).reshape(heads, requests, HD)
        fresh = []
        for t in range(step + 1):
            key = keys[t * requests : (t + 1) * requests, :].astype(jnp.float32)
            fresh.append(jnp.sum(wide * key[None], axis=-1, keepdims=True) * SCALE)
        top = fresh[0]
        for score in fresh[1:]:
            top = jnp.maximum(top, score)
        lane_top = jnp.broadcast_to(top, (heads, requests, HD))
        for n in range(2 * slots // chunk):
            k = ks[n * chunk : (n + 1) * chunk].reshape(width, HD)
            scores = dot_t(stacked, k).reshape(heads, requests, width) * SCALE
            scores = scores + bias[:, n * width : (n + 1) * width][None]
            sc[n] = scores
            lane_top = lanes_max(scores, lane_top)
        top = jnp.max(lane_top, axis=-1, keepdims=True)
        total = jnp.zeros((heads, requests, 1), jnp.float32)
        weighted = jnp.zeros((heads, requests, HD), jnp.float32)
        for t, score in enumerate(fresh):
            prob = jnp.exp(score - top)
            value = values[t * requests : (t + 1) * requests, :].astype(jnp.float32)
            total = total + prob
            weighted = weighted + prob * value[None]
        wide_top = jnp.broadcast_to(top, (heads, requests, HD))
        lane_sum = jnp.zeros((heads, requests, HD), jnp.float32)
        for n in range(2 * slots // chunk):
            v = vs[n * chunk : (n + 1) * chunk].reshape(width, HD)
            probs = jnp.exp(sc[n] - jnp.concatenate([wide_top] * chunk, axis=-1))
            lane_sum = lanes_sum(probs, lane_sum)
            update = jnp.dot(
                probs.reshape(heads * requests, width).astype(jnp.bfloat16),
                v,
                preferred_element_type=jnp.float32,
            )
            weighted = weighted + update.reshape(heads, requests, HD)
        total = total + jnp.sum(lane_sum, axis=-1, keepdims=True)
        result = (weighted / total).astype(res.dtype)
        for h in range(heads):
            res[step * requests : (step + 1) * requests, h * HD : (h + 1) * HD] = result[h]


def decode_attention(info, placement, q, keys, values, table, lens, mine, other, kv):
    slots = mine.shape[0]
    requests = table.shape[0]
    cols = q.shape[1]
    return pl.pallas_call(
        decode_kernel,
        out_shape=jax.ShapeDtypeStruct(q.shape, jnp.bfloat16),
        in_specs=specs(2, 15),
        out_specs=specs(0, 1)[0],
        scratch_shapes=[
            pltpu.VMEM((2 * slots, PAGE, HD), jnp.bfloat16),
            pltpu.VMEM((2 * slots, PAGE, HD), jnp.bfloat16),
            pltpu.VMEM((requests, 2 * slots * PAGE), jnp.float32),
            pltpu.VMEM((2 * slots // 8, cols // HD, requests, 8 * PAGE), jnp.float32),
        ],
        compiler_params=params(32),
        cost_estimate=pl.CostEstimate(
            flops=4 * 768 * 4096 * HD, bytes_accessed=5 << 20, transcendentals=768 * 4096
        ),
        name="decode_attention",
    )(info, placement, q, keys, values, table, lens, mine, other, *kv)


def output_kernel(k, info, *refs):
    rows, w, out, held, sems = refs[:4], refs[4], refs[5], refs[6], refs[7]
    width = w.shape[2]
    copies = []
    for c in range(4):
        block = w.at[lax.rem(info[4] + k, 4) * 4 + c]
        copy = pltpu.make_async_copy(block, held.at[:, c * width : (c + 1) * width], sems.at[c])
        copy.start()
        copies.append(copy)
    wide = jnp.concatenate([row[...] for row in rows], axis=1)
    for copy in copies:
        copy.wait()
    result = jnp.dot(wide, held[...], preferred_element_type=jnp.float32)
    out[...] = result.astype(out.dtype)


def output_projection(info, rows, w, k):
    count, depth = rows[0].shape
    cols = 4 * w.shape[2]
    return pl.pallas_call(
        functools.partial(output_kernel, k),
        out_shape=jax.ShapeDtypeStruct((count, cols), jnp.bfloat16),
        in_specs=specs(1, 4, 1),
        out_specs=specs(0, 1)[0],
        scratch_shapes=[
            pltpu.VMEM((4 * depth, cols), jnp.bfloat16),
            pltpu.SemaphoreType.DMA((4,)),
        ],
        compiler_params=params(50),
        cost_estimate=pl.CostEstimate(
            flops=8 * count * depth * cols, bytes_accessed=3 << 20, transcendentals=0
        ),
        name="output_projection",
    )(info, *rows, w)


def quarter(info, k, width):
    return pl.ds(pl.multiple_of(lax.rem(info[5] + k, 4) * width, width), width)


def sum_kernel(info, *refs):
    parts, outs, held = refs[:4], refs[4:8], refs[8]
    total = parts[0][...].astype(jnp.float32)
    for part in parts[1:]:
        total = total + part[...].astype(jnp.float32)
    held[...] = total
    for k in range(4):
        outs[k][...] = held[:, quarter(info, k, outs[k].shape[1])].astype(outs[k].dtype)


def sum_parts(info, parts):
    rows, cols = parts[0].shape
    return pl.pallas_call(
        sum_kernel,
        out_shape=[jax.ShapeDtypeStruct((rows, cols // 4), jnp.bfloat16)] * 4,
        in_specs=specs(1, 4),
        out_specs=specs(0, 4),
        scratch_shapes=[pltpu.VMEM((rows, cols), jnp.float32)],
        compiler_params=params(16),
        name="sum_parts",
    )(info, *parts)


def assemble_kernel(info, *refs):
    pieces, out = refs[:4], refs[4]
    for k in range(4):
        out[:, quarter(info, 4 - k, pieces[k].shape[1])] = pieces[k][...]


def assemble(info, pieces):
    rows, cols = pieces[0].shape
    return pl.pallas_call(
        assemble_kernel,
        out_shape=jax.ShapeDtypeStruct((rows, 4 * cols), jnp.bfloat16),
        in_specs=specs(1, 4),
        out_specs=specs(0, 1)[0],
        compiler_params=params(16),
        name="assemble",
    )(info, *pieces)


def along(values, dx, dy):
    sent = list(values)
    for k in (2, 1, 3):
        sent[k] = lax.ppermute(values[k], "tp", tp_perm(k * dx, k * dy))
    return sent


def on_device(
    x_prefill, x_decode, w_query, w_keyval, w_out, cache_pool, placement, page_table, cache_len
):
    tokens = x_prefill.shape[0]
    steps, requests, width = x_decode.shape
    section, tp, plane = lax.axis_index("section"), lax.axis_index("tp"), lax.axis_index("dp")
    x, y = lax.div(tp, 4), lax.rem(tp, 4)
    lane = lax.rem(tp, 2)
    group = section * 8 + plane
    info = jnp.stack([group, section, plane, lane, x, y, tp]).astype(jnp.int32)
    turn = jnp.where(section == 0, 1, -1)
    count = jnp.arange(16, dtype=jnp.int32)
    order = lax.rem(x - turn * (count // 4) + 4, 4) * 4 + lax.rem(y - turn * (count % 4) + 4, 4)

    q_cols = w_query.shape[1]
    kv_cols = w_keyval.shape[1]
    w_all = lax.all_gather(jnp.concatenate([w_query, w_keyval], axis=1), SD, axis=0, tiled=False)

    part = w_out.shape[1] // 4
    w_cut = along(
        [lax.dynamic_slice_in_dim(w_out, lax.rem(y + k, 4) * part, part, 1) for k in range(4)], 0, 1
    )
    rows = x_decode.reshape(steps * requests, width)
    half_p, half_d = tokens // 2, rows.shape[0] // 2
    blocks, w_cut = gather_tp(
        jnp.concatenate([x_prefill[:half_p], rows[:half_d]], axis=0),
        jnp.concatenate([x_prefill[half_p:], rows[half_d:]], axis=0),
        w_cut,
    )
    wo_all = lax.all_gather(jnp.concatenate(w_cut, axis=0), SD, axis=0, tiled=False)
    (kv_mine,) = project(order, blocks, w_all, 0, half_p, q_cols, [kv_cols])
    kv_lane = lax.ppermute(kv_mine, "tp", LANE)
    kv_core = lax.ppermute(kv_mine, "section", SWAP)
    kv_both = lax.ppermute(kv_mine, ST, BOTH)
    mine, kv_lane, kv_core, kv_both = lax.optimization_barrier(
        (cache_pool[0], kv_lane, kv_core, kv_both)
    )
    is_key = lane == 0
    pair = jnp.stack(
        [
            jnp.stack([jnp.where(is_key, p, q), jnp.where(is_key, q, p)])
            for p, q in ((kv_mine, kv_lane), (kv_core, kv_both))
        ]
    )
    kv, (q_dec, new_mine) = gather_planes(
        pair, project(order, blocks, w_all, half_p, half_p + half_d, 0, [q_cols, kv_cols])
    )
    new_lane = lax.ppermute(new_mine, "tp", LANE)
    other = lax.ppermute(mine, "tp", LANE)
    keys = jnp.where(is_key, new_mine, new_lane)
    values = jnp.where(is_key, new_lane, new_mine)

    attention = decode_attention(
        info, placement, q_dec, keys, values, page_table, cache_len[:, None], mine, other, kv
    )
    attended = along([attention] * 4, 0, 1)
    (q_pre,) = project(order, blocks, w_all, 0, half_p, 0, [q_cols])
    prefill_out = prefill_attention(info, q_pre, kv)
    prefill_out, *attended = lax.optimization_barrier((prefill_out, *attended))
    parts = along([output_projection(info, attended, wo_all, k) for k in range(4)], 1, 0)
    pieces = along(sum_parts(info, parts), 0, 1)
    decode_out = assemble(info, pieces).reshape(steps, requests, -1)
    return (prefill_out, decode_out)


def solution(mesh):
    return jax.shard_map(
        on_device,
        mesh=mesh,
        in_specs=(
            P(("section", "dp"), "tp"),
            P(None, ("section", "dp"), "tp"),
            P(("section", "dp"), "tp"),
            P(("section", "dp"), "tp"),
            P("tp", ("section", "dp")),
            P("tp", ("section", "dp"), None, None),
            P(),
            P(("section", "dp"), None),
            P(("section", "dp")),
        ),
        out_specs=(P(("section", "dp"), "tp"), P(None, ("section", "dp"), "tp")),
        check_vma=False,
    )
```

```python
import functools
import math

import jax
import jax.numpy as jnp
from jax import lax
from jax.experimental import pallas as pl
from jax.experimental.pallas import tpu as pltpu
from jax.sharding import PartitionSpec as P

HD = 128
PAGE = 128
NEG = -1e30
SCALE = 1.0 / math.sqrt(HD)
LOG2E = math.log2(math.e)

ST = ("section", "tp")
SD = ("section", "dp")

SWAP = [(0, 1), (1, 0)]
LANE = [(t, t ^ 1) for t in range(16)]
BOTH = [(t, t ^ 17) for t in range(32)]
SPIN = [
    [(s * 8 + z, s * 8 + (z + r - 2 * r * s) % 8) for s in range(2) for z in range(8)]
    for r in range(3)
]


def tp_perm(dx, dy):
    return [
        (x * 4 + y, (x + dx) % 4 * 4 + (y + dy) % 4) for x in range(4) for y in range(4)
    ]


def ring_perm(dx, dy):
    pairs = []
    for s in range(2):
        d = 1 - 2 * s
        pairs += [(s * 16 + a, s * 16 + b) for a, b in tp_perm(d * dx, d * dy)]
    return pairs


RING_X = ring_perm(1, 0)
RING_Y = ring_perm(0, 1)


def gather_tp(first, second, beside):
    a, b = [first], [second]
    for r in range(1, 4):
        a.append(lax.ppermute(first, ST, ring_perm(0, r)))
        b.append(lax.ppermute(second, ST, ring_perm(r, 0)))
    a, b = [jnp.stack(a)], [jnp.stack(b)]
    for r in range(3):
        a.append(lax.ppermute(a[-1], ST, RING_X))
        b.append(lax.ppermute(b[-1], ST, RING_Y))
        if r == 0:
            a[1], b[1], *beside = lax.optimization_barrier((a[1], b[1], *beside))
    return a + b, beside


def gather_planes(pair, beside):
    mine = [pair, lax.ppermute(pair, SD, SPIN[1]), lax.ppermute(pair, SD, SPIN[2])]
    mine[1], mine[2], *beside = lax.optimization_barrier((mine[1], mine[2], *beside))
    mine += [lax.ppermute(mine[1], SD, SPIN[2]), lax.ppermute(mine[2], SD, SPIN[2])]
    return mine + [lax.ppermute(block, "section", SWAP) for block in mine[1:4]], beside


def placed(refs, section):
    for n, ref in enumerate(refs):
        r = n if n < 5 else n - 4
        up, down = (r, (8 - r) % 8) if n < 5 else (8 - r, r)
        below = jnp.where(section == 0, up, down)
        for e in range(2):
            yield ref.at[e], (e if n < 5 else 1 - e), below


def group_at(info, other, below):
    section = info[1] if other == 0 else 1 - info[1]
    return section * 8 + lax.rem(info[2] - below + 8, 8)


def specs(smem, vmem, anywhere=0):
    return (
        [pl.BlockSpec(memory_space=pltpu.SMEM)] * smem
        + [pl.BlockSpec(memory_space=pltpu.VMEM)] * vmem
        + [pl.BlockSpec(memory_space=pl.ANY)] * anywhere
    )


def params(mib):
    return pltpu.CompilerParams(vmem_limit_bytes=mib << 20)


def start_copies(w, held, sems, order=None):
    copies = []
    for n in range(16):
        copy = pltpu.make_async_copy(w.at[n if order is None else order[n]], held.at[n], sems.at[n])
        copy.start()
        copies.append(copy)
    return copies


def key_kernel(tokens, order, *refs):
    a, b, w, out, held, sems = refs[:4], refs[4:8], refs[8], *refs[9:]
    depth, cols = held.shape[1:]
    half = tokens // 2
    copies = start_copies(w.at[:, :, w.shape[2] - cols :], held, sems, order)
    total = None
    for i in range(4):
        rows = jnp.concatenate(
            [
                jnp.concatenate([a[i][j, :half, :] for j in range(4)], axis=1),
                jnp.concatenate([b[j][i, :half, :] for j in range(4)], axis=1),
            ],
            axis=0,
        )
        for j in range(4):
            copies[4 * i + j].wait()
        block = held[4 * i : 4 * i + 4].reshape(4 * depth, cols)
        part = jnp.dot(rows, block, preferred_element_type=jnp.float32)
        total = part if total is None else total + part
    out[...] = total.astype(out.dtype)


def project_keys(order, blocks, w, cols, tokens):
    depth = w.shape[1]
    return pl.pallas_call(
        functools.partial(key_kernel, tokens),
        out_shape=jax.ShapeDtypeStruct((tokens, cols), jnp.bfloat16),
        in_specs=specs(1, 8, 1),
        out_specs=specs(0, 1)[0],
        scratch_shapes=[
            pltpu.VMEM((16, depth, cols), jnp.bfloat16),
            pltpu.SemaphoreType.DMA((16,)),
        ],
        compiler_params=params(47),
        cost_estimate=pl.CostEstimate(
            flops=2 * tokens * 16 * depth * cols,
            bytes_accessed=2 * 16 * depth * (tokens + cols),
            transcendentals=0,
        ),
        name="project_keys",
    )(order, *blocks, w)


def project_kernel(tokens, order, *refs):
    a, b, w, pre, dec, kv, held, sems = refs[:4], refs[4:8], refs[8], *refs[9:]
    q_cols = pre.shape[1]
    half, each = tokens // 2, a[0].shape[1]
    late = each - half
    copies = start_copies(w, held, sems, order)
    total, total_kv = None, None
    for n in range(16):
        i, j = n // 4, n % 4
        rows = jnp.concatenate([a[i][j], b[j][i]], axis=0)
        rows_kv = jnp.concatenate([a[i][j, half:, :], b[j][i, half:, :]], axis=0)
        copies[n].wait()
        part = jnp.dot(rows, held[n, :, :q_cols], preferred_element_type=jnp.float32)
        part_kv = jnp.dot(rows_kv, held[n, :, q_cols:], preferred_element_type=jnp.float32)
        total = part if total is None else total + part
        total_kv = part_kv if total_kv is None else total_kv + part_kv
    kv[...] = total_kv.astype(kv.dtype)
    result = total.astype(pre.dtype)
    for first in range(2):
        start = first * each
        pre[first * half : (first + 1) * half, :] = result[start : start + half]
        dec[first * late : (first + 1) * late, :] = result[start + half : start + each]


def project(order, blocks, w, q_cols, tokens):
    rows = 2 * blocks[0].shape[1]
    depth, cols = w.shape[1:]
    return pl.pallas_call(
        functools.partial(project_kernel, tokens),
        out_shape=[
            jax.ShapeDtypeStruct((tokens, q_cols), jnp.bfloat16),
            jax.ShapeDtypeStruct((rows - tokens, q_cols), jnp.bfloat16),
            jax.ShapeDtypeStruct((rows - tokens, cols - q_cols), jnp.bfloat16),
        ],
        in_specs=specs(1, 8, 1),
        out_specs=specs(0, 3),
        scratch_shapes=[
            pltpu.VMEM((16, depth, cols), jnp.bfloat16),
            pltpu.SemaphoreType.DMA((16,)),
        ],
        compiler_params=params(47),
        cost_estimate=pl.CostEstimate(
            flops=2 * rows * 16 * depth * cols,
            bytes_accessed=2 * 16 * depth * (rows + cols),
            transcendentals=0,
        ),
        name="project",
    )(order, *blocks, w)


def dot_t(a, b):
    return lax.dot_general(a, b, (((1,), (1,)), ((), ())), preferred_element_type=jnp.float32)


def lanes_max(value, top):
    for n in range(0, value.shape[-1], HD):
        top = jnp.maximum(top, value[..., n : n + HD])
    return top


def lanes_sum(value, total):
    for n in range(0, value.shape[-1], HD):
        total = total + value[..., n : n + HD]
    return total


def prefill_kernel(info, q, *refs):
    kv, out, qs, kvs, sc, mx, ls, acc = refs[:8], *refs[8:]
    tokens = q.shape[0]
    wide = kvs.shape[2]
    heads = q.shape[1] // HD
    last, late = lax.div(info[0], 2), lax.rem(info[0], 2) * tokens
    for block, other, below in placed(kv, info[1]):
        group = group_at(info, other, below)
        at = pl.ds(pl.multiple_of(lax.rem(group, 2) * tokens, tokens), tokens)
        for c in range(2):
            kvs[lax.div(group, 2), c, at, :] = block[c]
    for h in range(heads):
        qs[h] = q[:, h * HD : (h + 1) * HD]

    row = lax.broadcasted_iota(jnp.int32, (tokens, wide), 0)
    col = lax.broadcasted_iota(jnp.int32, (tokens, wide), 1)
    for h in range(heads):
        scores = jnp.where(col <= row + late, dot_t(qs[h], kvs[last, 0]), NEG)
        sc[last, h] = scores
        mx[h] = lanes_max(scores[:, HD:], scores[:, :HD])

    @pl.loop(0, last)
    def _(n):
        for h in range(heads):
            scores = dot_t(qs[h], kvs[n, 0])
            sc[n, h] = scores
            mx[h] = lanes_max(scores, mx[h])

    for h in range(heads):
        top = jnp.max(mx[h], axis=-1, keepdims=True) * (SCALE * LOG2E)
        mx[h] = jnp.broadcast_to(top, (tokens, HD))
        ls[h] = jnp.zeros((tokens, HD), jnp.float32)
        acc[h] = jnp.zeros((tokens, HD), jnp.float32)

    @pl.loop(0, last + 1)
    def _(n):
        for h in range(heads):
            top = jnp.concatenate([mx[h]] * (wide // HD), axis=1)
            probs = jnp.exp2(sc[n, h] * (SCALE * LOG2E) - top)
            ls[h] = lanes_sum(probs, ls[h])
            acc[h] += jnp.dot(
                probs.astype(jnp.bfloat16), kvs[n, 1], preferred_element_type=jnp.float32
            )

    for h in range(heads):
        total = jnp.sum(ls[h], axis=-1, keepdims=True)
        out[:, h * HD : (h + 1) * HD] = (acc[h] / total).astype(out.dtype)


def prefill_attention(info, q, kv):
    tokens, cols = q.shape
    heads = cols // HD
    return pl.pallas_call(
        prefill_kernel,
        out_shape=jax.ShapeDtypeStruct(q.shape, jnp.bfloat16),
        in_specs=specs(1, 9),
        out_specs=specs(0, 1)[0],
        scratch_shapes=[
            pltpu.VMEM((heads, tokens, HD), jnp.bfloat16),
            pltpu.VMEM((8, 2, 2 * tokens, HD), jnp.bfloat16),
            pltpu.VMEM((8, heads, tokens, 2 * tokens), jnp.float32),
            pltpu.VMEM((heads, tokens, HD), jnp.float32),
            pltpu.VMEM((heads, tokens, HD), jnp.float32),
            pltpu.VMEM((heads, tokens, HD), jnp.float32),
        ],
        compiler_params=params(36),
        cost_estimate=pl.CostEstimate(
            flops=4 * 4096 * tokens * cols, bytes_accessed=3 << 20, transcendentals=4096 * 1024
        ),
        name="prefill_attention",
    )(info, q, *kv)


def decode_kernel(info, placement, q, keys, values, table, lens, mine, other, *refs):
    kv, res, ks, vs, bias, sc = refs[:8], *refs[8:]
    slots = mine.shape[0]
    requests, pages = table.shape
    steps = q.shape[0] // requests
    heads = q.shape[1] // HD
    lane = info[3]
    for pool, first in ((mine, lane * slots), (other, (1 - lane) * slots)):
        for i in range(slots):
            ks[first + i] = pool[i, :, :HD]
            vs[first + i] = pool[i, :, HD:]

    for block, far, below in placed(kv, info[1]):
        group = group_at(info, far, below)
        for half in range(2):
            number = 2 * group + half

            @pl.when(placement[number, 0] == info[0])
            def _():
                target = placement[number, 1]
                ks[target] = block[0, half * PAGE : (half + 1) * PAGE, :]
                vs[target] = block[1, half * PAGE : (half + 1) * PAGE, :]

    offset = lax.broadcasted_iota(jnp.int32, (requests, PAGE), 1)
    length = jnp.broadcast_to(lens[...], (requests, PAGE))
    named = []
    for j in range(pages):
        slot = jnp.broadcast_to(table[:, j : j + 1], (requests, PAGE))
        named.append(jnp.where(offset + j * PAGE < length, slot, -1))
    for slot in range(2 * slots):
        count = jnp.zeros((requests, PAGE), jnp.float32)
        for j in range(slot // slots, pages, 2):
            count = count + jnp.where(named[j] == slot, 1.0, 0.0)
        bias[:, slot * PAGE : (slot + 1) * PAGE] = jnp.where(
            count > 0, jnp.log2(jnp.maximum(count, 1.0)), NEG
        )

    chunk = 8
    width = chunk * PAGE
    for step in range(steps):
        q_rows = q[step * requests : (step + 1) * requests, :]
        stacked = jnp.concatenate([q_rows[:, h * HD : (h + 1) * HD] for h in range(heads)], axis=0)
        wide = stacked.astype(jnp.float32).reshape(heads, requests, HD)
        fresh = []
        for t in range(step + 1):
            key = keys[t * requests : (t + 1) * requests, :].astype(jnp.float32)
            fresh.append(jnp.sum(wide * key[None], axis=-1, keepdims=True) * (SCALE * LOG2E))
        top = fresh[0]
        for score in fresh[1:]:
            top = jnp.maximum(top, score)
        lane_top = jnp.broadcast_to(top, (heads, requests, HD))
        for n in range(2 * slots // chunk):
            k = ks[n * chunk : (n + 1) * chunk].reshape(width, HD)
            scores = dot_t(stacked, k).reshape(heads, requests, width) * (SCALE * LOG2E)
            scores = scores + bias[:, n * width : (n + 1) * width][None]
            sc[n] = scores
            lane_top = lanes_max(scores, lane_top)
        top = jnp.max(lane_top, axis=-1, keepdims=True)
        total = jnp.zeros((heads, requests, 1), jnp.float32)
        weighted = jnp.zeros((heads, requests, HD), jnp.float32)
        for t, score in enumerate(fresh):
            prob = jnp.exp2(score - top)
            value = values[t * requests : (t + 1) * requests, :].astype(jnp.float32)
            total = total + prob
            weighted = weighted + prob * value[None]
        wide_top = jnp.broadcast_to(top, (heads, requests, HD))
        lane_sum = jnp.zeros((heads, requests, HD), jnp.float32)
        for n in range(2 * slots // chunk):
            v = vs[n * chunk : (n + 1) * chunk].reshape(width, HD)
            probs = jnp.exp2(sc[n] - jnp.concatenate([wide_top] * chunk, axis=-1))
            lane_sum = lanes_sum(probs, lane_sum)
            update = jnp.dot(
                probs.reshape(heads * requests, width).astype(jnp.bfloat16),
                v,
                preferred_element_type=jnp.float32,
            )
            weighted = weighted + update.reshape(heads, requests, HD)
        total = total + jnp.sum(lane_sum, axis=-1, keepdims=True)
        result = (weighted / total).astype(res.dtype)
        for h in range(heads):
            res[step * requests : (step + 1) * requests, h * HD : (h + 1) * HD] = result[h]


def decode_attention(info, placement, q, keys, values, table, lens, mine, other, kv):
    slots = mine.shape[0]
    requests = table.shape[0]
    cols = q.shape[1]
    return pl.pallas_call(
        decode_kernel,
        out_shape=jax.ShapeDtypeStruct(q.shape, jnp.bfloat16),
        in_specs=specs(2, 15),
        out_specs=specs(0, 1)[0],
        scratch_shapes=[
            pltpu.VMEM((2 * slots, PAGE, HD), jnp.bfloat16),
            pltpu.VMEM((2 * slots, PAGE, HD), jnp.bfloat16),
            pltpu.VMEM((requests, 2 * slots * PAGE), jnp.float32),
            pltpu.VMEM((2 * slots // 8, cols // HD, requests, 8 * PAGE), jnp.float32),
        ],
        compiler_params=params(32),
        cost_estimate=pl.CostEstimate(
            flops=4 * 768 * 4096 * HD, bytes_accessed=5 << 20, transcendentals=768 * 4096
        ),
        name="decode_attention",
    )(info, placement, q, keys, values, table, lens, mine, other, *kv)


def output_kernel(info, *refs):
    rows, w, outs, held, sems = refs[:4], refs[4], refs[5:9], refs[9], refs[10]
    width = w.shape[2]
    copies = []
    for n in range(16):
        k, c = n // 4, n % 4
        block = w.at[lax.rem(info[4] + k, 4) * 4 + c]
        copy = pltpu.make_async_copy(
            block, held.at[k, :, c * width : (c + 1) * width], sems.at[n]
        )
        copy.start()
        copies.append(copy)
    wide = jnp.concatenate([row[...] for row in rows], axis=1)
    for k in range(4):
        for c in range(4):
            copies[4 * k + c].wait()
        result = jnp.dot(wide, held[k], preferred_element_type=jnp.float32)
        outs[k][...] = result.astype(outs[k].dtype)


def output_projection(info, rows, w):
    count, depth = rows[0].shape
    cols = 4 * w.shape[2]
    return pl.pallas_call(
        output_kernel,
        out_shape=[jax.ShapeDtypeStruct((count, cols), jnp.bfloat16)] * 4,
        in_specs=specs(1, 4, 1),
        out_specs=specs(0, 4),
        scratch_shapes=[
            pltpu.VMEM((4, 4 * depth, cols), jnp.bfloat16),
            pltpu.SemaphoreType.DMA((16,)),
        ],
        compiler_params=params(50),
        cost_estimate=pl.CostEstimate(
            flops=32 * count * depth * cols, bytes_accessed=10 << 20, transcendentals=0
        ),
        name="output_projection",
    )(info, *rows, w)


def quarter(info, k, width):
    return pl.ds(pl.multiple_of(lax.rem(info[5] + k, 4) * width, width), width)


def sum_kernel(info, *refs):
    parts, outs, held = refs[:4], refs[4:8], refs[8]
    total = parts[0][...].astype(jnp.float32)
    for part in parts[1:]:
        total = total + part[...].astype(jnp.float32)
    held[...] = total
    for k in range(4):
        outs[k][...] = held[:, quarter(info, k, outs[k].shape[1])].astype(outs[k].dtype)


def sum_parts(info, parts):
    rows, cols = parts[0].shape
    return pl.pallas_call(
        sum_kernel,
        out_shape=[jax.ShapeDtypeStruct((rows, cols // 4), jnp.bfloat16)] * 4,
        in_specs=specs(1, 4),
        out_specs=specs(0, 4),
        scratch_shapes=[pltpu.VMEM((rows, cols), jnp.float32)],
        compiler_params=params(16),
        name="sum_parts",
    )(info, *parts)


def assemble_kernel(info, *refs):
    pieces, out = refs[:4], refs[4]
    for k in range(4):
        out[:, quarter(info, 4 - k, pieces[k].shape[1])] = pieces[k][...]


def assemble(info, pieces):
    rows, cols = pieces[0].shape
    return pl.pallas_call(
        assemble_kernel,
        out_shape=jax.ShapeDtypeStruct((rows, 4 * cols), jnp.bfloat16),
        in_specs=specs(1, 4),
        out_specs=specs(0, 1)[0],
        compiler_params=params(16),
        name="assemble",
    )(info, *pieces)


def along(values, dx, dy):
    sent = list(values)
    for k in (2, 1, 3):
        sent[k] = lax.ppermute(values[k], "tp", tp_perm(k * dx, k * dy))
    return sent


def on_device(
    x_prefill, x_decode, w_query, w_keyval, w_out, cache_pool, placement, page_table, cache_len
):
    tokens = x_prefill.shape[0]
    steps, requests, width = x_decode.shape
    section, tp, plane = lax.axis_index("section"), lax.axis_index("tp"), lax.axis_index("dp")
    x, y = lax.div(tp, 4), lax.rem(tp, 4)
    lane = lax.rem(tp, 2)
    group = section * 8 + plane
    info = jnp.stack([group, section, plane, lane, x, y, tp]).astype(jnp.int32)
    turn = jnp.where(section == 0, 1, -1)
    count = jnp.arange(16, dtype=jnp.int32)
    order = lax.rem(x - turn * (count // 4) + 4, 4) * 4 + lax.rem(y - turn * (count % 4) + 4, 4)

    q_cols = w_query.shape[1]
    kv_cols = w_keyval.shape[1]
    w_all = lax.all_gather(jnp.concatenate([w_query, w_keyval], axis=1), SD, axis=0, tiled=False)

    part = w_out.shape[1] // 4
    w_cut = along(
        [lax.dynamic_slice_in_dim(w_out, lax.rem(y + k, 4) * part, part, 1) for k in range(4)], 0, 1
    )
    rows = x_decode.reshape(steps * requests, width)
    half_p, half_d = tokens // 2, rows.shape[0] // 2
    blocks, w_cut = gather_tp(
        jnp.concatenate([x_prefill[:half_p], rows[:half_d]], axis=0),
        jnp.concatenate([x_prefill[half_p:], rows[half_d:]], axis=0),
        w_cut,
    )
    wo_all = lax.all_gather(jnp.concatenate(w_cut, axis=0), SD, axis=0, tiled=False)
    kv_mine = project_keys(order, blocks, w_all, kv_cols, tokens)
    kv_lane = lax.ppermute(kv_mine, "tp", LANE)
    kv_core = lax.ppermute(kv_mine, "section", SWAP)
    kv_both = lax.ppermute(kv_mine, ST, BOTH)
    mine, kv_lane, kv_core, kv_both = lax.optimization_barrier(
        (cache_pool[0], kv_lane, kv_core, kv_both)
    )
    is_key = lane == 0
    pair = jnp.stack(
        [
            jnp.stack([jnp.where(is_key, p, q), jnp.where(is_key, q, p)])
            for p, q in ((kv_mine, kv_lane), (kv_core, kv_both))
        ]
    )
    kv, (q_pre, q_dec, new_mine) = gather_planes(pair, project(order, blocks, w_all, q_cols, tokens))
    new_lane = lax.ppermute(new_mine, "tp", LANE)
    other = lax.ppermute(mine, "tp", LANE)
    keys = jnp.where(is_key, new_mine, new_lane)
    values = jnp.where(is_key, new_lane, new_mine)

    attention = decode_attention(
        info, placement, q_dec, keys, values, page_table, cache_len[:, None], mine, other, kv
    )
    attended = along([attention] * 4, 0, 1)
    parts = along(output_projection(info, attended, wo_all), 1, 0)
    prefill_out = prefill_attention(info, q_pre, kv)
    prefill_out, *parts = lax.optimization_barrier((prefill_out, *parts))
    pieces = along(sum_parts(info, parts), 0, 1)
    decode_out = assemble(info, pieces).reshape(steps, requests, -1)
    return (prefill_out, decode_out)


def solution(mesh):
    return jax.shard_map(
        on_device,
        mesh=mesh,
        in_specs=(
            P(("section", "dp"), "tp"),
            P(None, ("section", "dp"), "tp"),
            P(("section", "dp"), "tp"),
            P(("section", "dp"), "tp"),
            P("tp", ("section", "dp")),
            P("tp", ("section", "dp"), None, None),
            P(),
            P(("section", "dp"), None),
            P(("section", "dp")),
        ),
        out_specs=(P(("section", "dp"), "tp"), P(None, ("section", "dp"), "tp")),
        check_vma=False,
    )
```

```python
import functools
import math

import jax
import jax.numpy as jnp
from jax import lax
from jax.experimental import pallas as pl
from jax.experimental.pallas import tpu as pltpu
from jax.sharding import PartitionSpec as P

HD = 128
PAGE = 128
NEG = -1e30
SCALE = 1.0 / math.sqrt(HD)
LOG2E = math.log2(math.e)

ST = ("section", "tp")
SD = ("section", "dp")

SWAP = [(0, 1), (1, 0)]
LANE = [(t, t ^ 1) for t in range(16)]
BOTH = [(t, t ^ 17) for t in range(32)]
SPIN = [
    [(s * 8 + z, s * 8 + (z + r - 2 * r * s) % 8) for s in range(2) for z in range(8)]
    for r in range(3)
]


def tp_perm(dx, dy):
    return [
        (x * 4 + y, (x + dx) % 4 * 4 + (y + dy) % 4) for x in range(4) for y in range(4)
    ]


def ring_perm(dx, dy):
    pairs = []
    for s in range(2):
        d = 1 - 2 * s
        pairs += [(s * 16 + a, s * 16 + b) for a, b in tp_perm(d * dx, d * dy)]
    return pairs


RING_X = ring_perm(1, 0)
RING_Y = ring_perm(0, 1)


def gather_tp(first, second, beside):
    a, b = [first], [second]
    for r in range(1, 4):
        a.append(lax.ppermute(first, ST, ring_perm(0, r)))
        b.append(lax.ppermute(second, ST, ring_perm(r, 0)))
    a, b = [jnp.stack(a)], [jnp.stack(b)]
    for r in range(3):
        a.append(lax.ppermute(a[-1], ST, RING_X))
        b.append(lax.ppermute(b[-1], ST, RING_Y))
        if r == 0:
            a[1], b[1], *beside = lax.optimization_barrier((a[1], b[1], *beside))
    return a + b, beside


def gather_planes(pair, beside):
    mine = [pair, lax.ppermute(pair, SD, SPIN[1]), lax.ppermute(pair, SD, SPIN[2])]
    mine[1], mine[2], *beside = lax.optimization_barrier((mine[1], mine[2], *beside))
    mine += [lax.ppermute(mine[1], SD, SPIN[2]), lax.ppermute(mine[2], SD, SPIN[2])]
    return mine + [lax.ppermute(block, "section", SWAP) for block in mine[1:4]], beside


def placed(refs, section):
    for n, ref in enumerate(refs):
        r = n if n < 5 else n - 4
        up, down = (r, (8 - r) % 8) if n < 5 else (8 - r, r)
        below = jnp.where(section == 0, up, down)
        for e in range(2):
            yield ref.at[e], (e if n < 5 else 1 - e), below


def group_at(info, other, below):
    section = info[1] if other == 0 else 1 - info[1]
    return section * 8 + lax.rem(info[2] - below + 8, 8)


def specs(smem, vmem, anywhere=0):
    return (
        [pl.BlockSpec(memory_space=pltpu.SMEM)] * smem
        + [pl.BlockSpec(memory_space=pltpu.VMEM)] * vmem
        + [pl.BlockSpec(memory_space=pl.ANY)] * anywhere
    )


def params(mib):
    return pltpu.CompilerParams(vmem_limit_bytes=mib << 20)


def start_copies(w, held, sems, order=None):
    copies = []
    for n in range(16):
        copy = pltpu.make_async_copy(w.at[n if order is None else order[n]], held.at[n], sems.at[n])
        copy.start()
        copies.append(copy)
    return copies


def key_kernel(tokens, order, *refs):
    a, b, w, out, held, sems = refs[:4], refs[4:8], refs[8], *refs[9:]
    depth, cols = held.shape[1:]
    half = tokens // 2
    copies = start_copies(w.at[:, :, w.shape[2] - cols :], held, sems, order)
    total = None
    for i in range(4):
        rows = jnp.concatenate(
            [
                jnp.concatenate([a[i][j, :half, :] for j in range(4)], axis=1),
                jnp.concatenate([b[j][i, :half, :] for j in range(4)], axis=1),
            ],
            axis=0,
        )
        for j in range(4):
            copies[4 * i + j].wait()
        block = held[4 * i : 4 * i + 4].reshape(4 * depth, cols)
        part = jnp.dot(rows, block, preferred_element_type=jnp.float32)
        total = part if total is None else total + part
    out[...] = total.astype(out.dtype)


def project_keys(order, blocks, w, cols, tokens):
    depth = w.shape[1]
    return pl.pallas_call(
        functools.partial(key_kernel, tokens),
        out_shape=jax.ShapeDtypeStruct((tokens, cols), jnp.bfloat16),
        in_specs=specs(1, 8, 1),
        out_specs=specs(0, 1)[0],
        scratch_shapes=[
            pltpu.VMEM((16, depth, cols), jnp.bfloat16),
            pltpu.SemaphoreType.DMA((16,)),
        ],
        compiler_params=params(47),
        cost_estimate=pl.CostEstimate(
            flops=2 * tokens * 16 * depth * cols,
            bytes_accessed=2 * 16 * depth * (tokens + cols),
            transcendentals=0,
        ),
        name="project_keys",
    )(order, *blocks, w)


def project_kernel(tokens, order, *refs):
    a, b, w, pre, dec, kv, held, sems = refs[:4], refs[4:8], refs[8], *refs[9:]
    q_cols = pre.shape[1]
    half, each = tokens // 2, a[0].shape[1]
    late = each - half
    copies = start_copies(w, held, sems, order)
    total, total_kv = None, None
    for n in range(16):
        i, j = n // 4, n % 4
        rows = jnp.concatenate([a[i][j], b[j][i]], axis=0)
        rows_kv = jnp.concatenate([a[i][j, half:, :], b[j][i, half:, :]], axis=0)
        copies[n].wait()
        part = jnp.dot(rows, held[n, :, :q_cols], preferred_element_type=jnp.float32)
        part_kv = jnp.dot(rows_kv, held[n, :, q_cols:], preferred_element_type=jnp.float32)
        total = part if total is None else total + part
        total_kv = part_kv if total_kv is None else total_kv + part_kv
    kv[...] = total_kv.astype(kv.dtype)
    result = total.astype(pre.dtype)
    for first in range(2):
        start = first * each
        pre[first * half : (first + 1) * half, :] = result[start : start + half]
        dec[first * late : (first + 1) * late, :] = result[start + half : start + each]


def project(order, blocks, w, q_cols, tokens):
    rows = 2 * blocks[0].shape[1]
    depth, cols = w.shape[1:]
    return pl.pallas_call(
        functools.partial(project_kernel, tokens),
        out_shape=[
            jax.ShapeDtypeStruct((tokens, q_cols), jnp.bfloat16),
            jax.ShapeDtypeStruct((rows - tokens, q_cols), jnp.bfloat16),
            jax.ShapeDtypeStruct((rows - tokens, cols - q_cols), jnp.bfloat16),
        ],
        in_specs=specs(1, 8, 1),
        out_specs=specs(0, 3),
        scratch_shapes=[
            pltpu.VMEM((16, depth, cols), jnp.bfloat16),
            pltpu.SemaphoreType.DMA((16,)),
        ],
        compiler_params=params(47),
        cost_estimate=pl.CostEstimate(
            flops=2 * rows * 16 * depth * cols,
            bytes_accessed=2 * 16 * depth * (rows + cols),
            transcendentals=0,
        ),
        name="project",
    )(order, *blocks, w)


def dot_t(a, b):
    return lax.dot_general(a, b, (((1,), (1,)), ((), ())), preferred_element_type=jnp.float32)


def lanes_max(value, top):
    for n in range(0, value.shape[-1], HD):
        top = jnp.maximum(top, value[..., n : n + HD])
    return top


def lanes_sum(value, total):
    for n in range(0, value.shape[-1], HD):
        total = total + value[..., n : n + HD]
    return total


def prefill_kernel(info, q, *refs):
    kv, out, qs, kvs, sc, mx, ls, acc = refs[:8], *refs[8:]
    tokens = q.shape[0]
    wide = kvs.shape[2]
    heads = q.shape[1] // HD
    last, late = lax.div(info[0], 2), lax.rem(info[0], 2) * tokens
    for block, other, below in placed(kv, info[1]):
        group = group_at(info, other, below)
        at = pl.ds(pl.multiple_of(lax.rem(group, 2) * tokens, tokens), tokens)
        for c in range(2):
            kvs[lax.div(group, 2), c, at, :] = block[c]
    for h in range(heads):
        qs[h] = q[:, h * HD : (h + 1) * HD]

    row = lax.broadcasted_iota(jnp.int32, (tokens, wide), 0)
    col = lax.broadcasted_iota(jnp.int32, (tokens, wide), 1)
    for h in range(heads):
        scores = jnp.where(col <= row + late, dot_t(qs[h], kvs[last, 0]), NEG)
        sc[last, h] = scores
        mx[h] = lanes_max(scores[:, HD:], scores[:, :HD])

    @pl.loop(0, last)
    def _(n):
        for h in range(heads):
            scores = dot_t(qs[h], kvs[n, 0])
            sc[n, h] = scores
            mx[h] = lanes_max(scores, mx[h])

    for h in range(heads):
        top = jnp.max(mx[h], axis=-1, keepdims=True) * (SCALE * LOG2E)
        mx[h] = jnp.broadcast_to(top, (tokens, HD))
        ls[h] = jnp.zeros((tokens, HD), jnp.float32)
        acc[h] = jnp.zeros((tokens, HD), jnp.float32)

    @pl.loop(0, last + 1)
    def _(n):
        for h in range(heads):
            top = jnp.concatenate([mx[h]] * (wide // HD), axis=1)
            probs = jnp.exp2(sc[n, h] * (SCALE * LOG2E) - top)
            ls[h] = lanes_sum(probs, ls[h])
            acc[h] += jnp.dot(
                probs.astype(jnp.bfloat16), kvs[n, 1], preferred_element_type=jnp.float32
            )

    for h in range(heads):
        total = jnp.sum(ls[h], axis=-1, keepdims=True)
        out[:, h * HD : (h + 1) * HD] = (acc[h] / total).astype(out.dtype)


def prefill_attention(info, q, kv):
    tokens, cols = q.shape
    heads = cols // HD
    return pl.pallas_call(
        prefill_kernel,
        out_shape=jax.ShapeDtypeStruct(q.shape, jnp.bfloat16),
        in_specs=specs(1, 9),
        out_specs=specs(0, 1)[0],
        scratch_shapes=[
            pltpu.VMEM((heads, tokens, HD), jnp.bfloat16),
            pltpu.VMEM((8, 2, 2 * tokens, HD), jnp.bfloat16),
            pltpu.VMEM((8, heads, tokens, 2 * tokens), jnp.float32),
            pltpu.VMEM((heads, tokens, HD), jnp.float32),
            pltpu.VMEM((heads, tokens, HD), jnp.float32),
            pltpu.VMEM((heads, tokens, HD), jnp.float32),
        ],
        compiler_params=params(36),
        cost_estimate=pl.CostEstimate(
            flops=4 * 4096 * tokens * cols, bytes_accessed=3 << 20, transcendentals=4096 * 1024
        ),
        name="prefill_attention",
    )(info, q, *kv)


def decode_kernel(info, placement, q, keys, values, table, lens, mine, other, *refs):
    kv, res, ks, vs, bias, sc, sems = refs[:8], *refs[8:]
    slots = mine.shape[0]
    requests, pages = table.shape
    steps = q.shape[0] // requests
    heads = q.shape[1] // HD
    lane = info[3]
    pools = []
    for pool, first in ((mine, lane * slots), (other, (1 - lane) * slots)):
        for c, held in enumerate((ks, vs)):
            source, target = pool.at[:, :, c * HD : (c + 1) * HD], held.at[pl.ds(first, slots)]
            pools.append(pltpu.make_async_copy(source, target, sems.at[len(pools)]))
            pools[-1].start()

    offset = lax.broadcasted_iota(jnp.int32, (requests, PAGE), 1)
    length = jnp.broadcast_to(lens[...], (requests, PAGE))
    named = []
    for j in range(pages):
        slot = jnp.broadcast_to(table[:, j : j + 1], (requests, PAGE))
        named.append(jnp.where(offset + j * PAGE < length, slot, -1))
    for slot in range(2 * slots):
        count = jnp.zeros((requests, PAGE), jnp.float32)
        for j in range(slot // slots, pages, 2):
            count = count + jnp.where(named[j] == slot, 1.0, 0.0)
        bias[:, slot * PAGE : (slot + 1) * PAGE] = jnp.where(
            count > 0, jnp.log2(jnp.maximum(count, 1.0)), NEG
        )

    for copy in pools:
        copy.wait()
    landings = []
    for block, far, below in placed(kv, info[1]):
        number = 2 * group_at(info, far, below)
        for half in range(2):
            hit, target = placement[number + half, 0] == info[0], placement[number + half, 1]
            pair = []
            for c, held in enumerate((ks, vs)):
                source = block.at[c, half * PAGE : (half + 1) * PAGE, :]
                at = len(pools) + 2 * len(landings) + c
                pair.append(pltpu.make_async_copy(source, held.at[target], sems.at[at]))
            landings.append((hit, pair))
    for hit, pair in landings:

        @pl.when(hit)
        def _():
            for copy in pair:
                copy.start()

    for hit, pair in landings:

        @pl.when(hit)
        def _():
            for copy in pair:
                copy.wait()

    chunk = 8
    width = chunk * PAGE
    for step in range(steps):
        q_rows = q[step * requests : (step + 1) * requests, :]
        stacked = jnp.concatenate([q_rows[:, h * HD : (h + 1) * HD] for h in range(heads)], axis=0)
        wide = stacked.astype(jnp.float32).reshape(heads, requests, HD)
        fresh = []
        for t in range(step + 1):
            key = keys[t * requests : (t + 1) * requests, :].astype(jnp.float32)
            fresh.append(jnp.sum(wide * key[None], axis=-1, keepdims=True) * (SCALE * LOG2E))
        top = fresh[0]
        for score in fresh[1:]:
            top = jnp.maximum(top, score)
        lane_top = jnp.broadcast_to(top, (heads, requests, HD))
        for n in range(2 * slots // chunk):
            k = ks[n * chunk : (n + 1) * chunk].reshape(width, HD)
            scores = dot_t(stacked, k).reshape(heads, requests, width) * (SCALE * LOG2E)
            scores = scores + bias[:, n * width : (n + 1) * width][None]
            sc[n] = scores
            lane_top = lanes_max(scores, lane_top)
        top = jnp.max(lane_top, axis=-1, keepdims=True)
        total = jnp.zeros((heads, requests, 1), jnp.float32)
        weighted = jnp.zeros((heads, requests, HD), jnp.float32)
        for t, score in enumerate(fresh):
            prob = jnp.exp2(score - top)
            value = values[t * requests : (t + 1) * requests, :].astype(jnp.float32)
            total = total + prob
            weighted = weighted + prob * value[None]
        wide_top = jnp.broadcast_to(top, (heads, requests, HD))
        lane_sum = jnp.zeros((heads, requests, HD), jnp.float32)
        for n in range(2 * slots // chunk):
            v = vs[n * chunk : (n + 1) * chunk].reshape(width, HD)
            probs = jnp.exp2(sc[n] - jnp.concatenate([wide_top] * chunk, axis=-1))
            lane_sum = lanes_sum(probs, lane_sum)
            update = jnp.dot(
                probs.reshape(heads * requests, width).astype(jnp.bfloat16),
                v,
                preferred_element_type=jnp.float32,
            )
            weighted = weighted + update.reshape(heads, requests, HD)
        total = total + jnp.sum(lane_sum, axis=-1, keepdims=True)
        result = (weighted / total).astype(res.dtype)
        for h in range(heads):
            res[step * requests : (step + 1) * requests, h * HD : (h + 1) * HD] = result[h]


def decode_attention(info, placement, q, keys, values, table, lens, mine, other, kv):
    slots = mine.shape[0]
    requests = table.shape[0]
    cols = q.shape[1]
    return pl.pallas_call(
        decode_kernel,
        out_shape=jax.ShapeDtypeStruct(q.shape, jnp.bfloat16),
        in_specs=specs(2, 5, 10),
        out_specs=specs(0, 1)[0],
        scratch_shapes=[
            pltpu.VMEM((2 * slots, PAGE, HD), jnp.bfloat16),
            pltpu.VMEM((2 * slots, PAGE, HD), jnp.bfloat16),
            pltpu.VMEM((requests, 2 * slots * PAGE), jnp.float32),
            pltpu.VMEM((2 * slots // 8, cols // HD, requests, 8 * PAGE), jnp.float32),
            pltpu.SemaphoreType.DMA((68,)),
        ],
        compiler_params=params(32),
        cost_estimate=pl.CostEstimate(
            flops=4 * 768 * 4096 * HD, bytes_accessed=5 << 20, transcendentals=768 * 4096
        ),
        name="decode_attention",
    )(info, placement, q, keys, values, table, lens, mine, other, *kv)


def output_kernel(info, *refs):
    rows, w, outs, held, sems = refs[:4], refs[4], refs[5:9], refs[9], refs[10]
    width = w.shape[2]
    copies = []
    for n in range(16):
        k, c = n // 4, n % 4
        block = w.at[lax.rem(info[4] + k, 4) * 4 + c]
        copy = pltpu.make_async_copy(
            block, held.at[k, :, c * width : (c + 1) * width], sems.at[n]
        )
        copy.start()
        copies.append(copy)
    wide = jnp.concatenate([row[...] for row in rows], axis=1)
    for k in range(4):
        for c in range(4):
            copies[4 * k + c].wait()
        result = jnp.dot(wide, held[k], preferred_element_type=jnp.float32)
        outs[k][...] = result.astype(outs[k].dtype)


def output_projection(info, rows, w):
    count, depth = rows[0].shape
    cols = 4 * w.shape[2]
    return pl.pallas_call(
        output_kernel,
        out_shape=[jax.ShapeDtypeStruct((count, cols), jnp.bfloat16)] * 4,
        in_specs=specs(1, 4, 1),
        out_specs=specs(0, 4),
        scratch_shapes=[
            pltpu.VMEM((4, 4 * depth, cols), jnp.bfloat16),
            pltpu.SemaphoreType.DMA((16,)),
        ],
        compiler_params=params(50),
        cost_estimate=pl.CostEstimate(
            flops=32 * count * depth * cols, bytes_accessed=10 << 20, transcendentals=0
        ),
        name="output_projection",
    )(info, *rows, w)


def quarter(info, k, width):
    return pl.ds(pl.multiple_of(lax.rem(info[5] + k, 4) * width, width), width)


def sum_kernel(info, *refs):
    parts, outs, held = refs[:4], refs[4:8], refs[8]
    total = parts[0][...].astype(jnp.float32)
    for part in parts[1:]:
        total = total + part[...].astype(jnp.float32)
    held[...] = total
    for k in range(4):
        outs[k][...] = held[:, quarter(info, k, outs[k].shape[1])].astype(outs[k].dtype)


def sum_parts(info, parts):
    rows, cols = parts[0].shape
    return pl.pallas_call(
        sum_kernel,
        out_shape=[jax.ShapeDtypeStruct((rows, cols // 4), jnp.bfloat16)] * 4,
        in_specs=specs(1, 4),
        out_specs=specs(0, 4),
        scratch_shapes=[pltpu.VMEM((rows, cols), jnp.float32)],
        compiler_params=params(16),
        name="sum_parts",
    )(info, *parts)


def assemble_kernel(info, *refs):
    pieces, out = refs[:4], refs[4]
    for k in range(4):
        out[:, quarter(info, 4 - k, pieces[k].shape[1])] = pieces[k][...]


def assemble(info, pieces):
    rows, cols = pieces[0].shape
    return pl.pallas_call(
        assemble_kernel,
        out_shape=jax.ShapeDtypeStruct((rows, 4 * cols), jnp.bfloat16),
        in_specs=specs(1, 4),
        out_specs=specs(0, 1)[0],
        compiler_params=params(16),
        name="assemble",
    )(info, *pieces)


def along(values, dx, dy):
    sent = list(values)
    for k in (2, 1, 3):
        sent[k] = lax.ppermute(values[k], "tp", tp_perm(k * dx, k * dy))
    return sent


def on_device(
    x_prefill, x_decode, w_query, w_keyval, w_out, cache_pool, placement, page_table, cache_len
):
    tokens = x_prefill.shape[0]
    steps, requests, width = x_decode.shape
    section, tp, plane = lax.axis_index("section"), lax.axis_index("tp"), lax.axis_index("dp")
    x, y = lax.div(tp, 4), lax.rem(tp, 4)
    lane = lax.rem(tp, 2)
    group = section * 8 + plane
    info = jnp.stack([group, section, plane, lane, x, y, tp]).astype(jnp.int32)
    turn = jnp.where(section == 0, 1, -1)
    count = jnp.arange(16, dtype=jnp.int32)
    order = lax.rem(x - turn * (count // 4) + 4, 4) * 4 + lax.rem(y - turn * (count % 4) + 4, 4)

    q_cols = w_query.shape[1]
    kv_cols = w_keyval.shape[1]
    w_all = lax.all_gather(jnp.concatenate([w_query, w_keyval], axis=1), SD, axis=0, tiled=False)

    part = w_out.shape[1] // 4
    w_cut = along(
        [lax.dynamic_slice_in_dim(w_out, lax.rem(y + k, 4) * part, part, 1) for k in range(4)], 0, 1
    )
    rows = x_decode.reshape(steps * requests, width)
    half_p, half_d = tokens // 2, rows.shape[0] // 2
    blocks, w_cut = gather_tp(
        jnp.concatenate([x_prefill[:half_p], rows[:half_d]], axis=0),
        jnp.concatenate([x_prefill[half_p:], rows[half_d:]], axis=0),
        w_cut,
    )
    kv_mine = project_keys(order, blocks, w_all, kv_cols, tokens)
    kv_mine, w_cut = lax.optimization_barrier((kv_mine, jnp.concatenate(w_cut, axis=0)))
    wo_all = lax.all_gather(w_cut, SD, axis=0, tiled=False)
    kv_lane = lax.ppermute(kv_mine, "tp", LANE)
    kv_core = lax.ppermute(kv_mine, "section", SWAP)
    kv_both = lax.ppermute(kv_mine, ST, BOTH)
    mine, kv_lane, kv_core, kv_both = lax.optimization_barrier(
        (cache_pool[0], kv_lane, kv_core, kv_both)
    )
    is_key = lane == 0
    pair = jnp.stack(
        [
            jnp.stack([jnp.where(is_key, p, q), jnp.where(is_key, q, p)])
            for p, q in ((kv_mine, kv_lane), (kv_core, kv_both))
        ]
    )
    kv, (q_pre, q_dec, new_mine) = gather_planes(pair, project(order, blocks, w_all, q_cols, tokens))
    new_lane = lax.ppermute(new_mine, "tp", LANE)
    other = lax.ppermute(mine, "tp", LANE)
    keys = jnp.where(is_key, new_mine, new_lane)
    values = jnp.where(is_key, new_lane, new_mine)

    attention = decode_attention(
        info, placement, q_dec, keys, values, page_table, cache_len[:, None], mine, other, kv
    )
    attended = along([attention] * 4, 0, 1)
    parts = along(output_projection(info, attended, wo_all), 1, 0)
    prefill_out = prefill_attention(info, q_pre, kv)
    prefill_out, *parts = lax.optimization_barrier((prefill_out, *parts))
    pieces = along(sum_parts(info, parts), 0, 1)
    decode_out = assemble(info, pieces).reshape(steps, requests, -1)
    return (prefill_out, decode_out)


def solution(mesh):
    return jax.shard_map(
        on_device,
        mesh=mesh,
        in_specs=(
            P(("section", "dp"), "tp"),
            P(None, ("section", "dp"), "tp"),
            P(("section", "dp"), "tp"),
            P(("section", "dp"), "tp"),
            P("tp", ("section", "dp")),
            P("tp", ("section", "dp"), None, None),
            P(),
            P(("section", "dp"), None),
            P(("section", "dp")),
        ),
        out_specs=(P(("section", "dp"), "tp"), P(None, ("section", "dp"), "tp")),
        check_vma=False,
    )
```

```python
import functools
import math

import jax
import jax.numpy as jnp
from jax import lax
from jax.experimental import pallas as pl
from jax.experimental.pallas import tpu as pltpu
from jax.sharding import PartitionSpec as P

HD = 128
PAGE = 128
NEG = -1e30
SCALE = 1.0 / math.sqrt(HD)
LOG2E = math.log2(math.e)

ST = ("section", "tp")
SD = ("section", "dp")

SWAP = [(0, 1), (1, 0)]
LANE = [(t, t ^ 1) for t in range(16)]
BOTH = [(t, t ^ 17) for t in range(32)]
SPIN = [(s * 8 + z, s * 8 + (z + 1 - 2 * s) % 8) for s in range(2) for z in range(8)]


def tp_perm(dx, dy):
    return [
        (x * 4 + y, (x + dx) % 4 * 4 + (y + dy) % 4) for x in range(4) for y in range(4)
    ]


def ring_perm(dx, dy):
    pairs = []
    for s in range(2):
        d = 1 - 2 * s
        pairs += [(s * 16 + a, s * 16 + b) for a, b in tp_perm(d * dx, d * dy)]
    return pairs


RING_X = ring_perm(1, 0)
RING_Y = ring_perm(0, 1)


def gather_tp(first, second, beside):
    a, b = [first], [second]
    for r in range(1, 4):
        a.append(lax.ppermute(first, ST, ring_perm(0, r)))
        b.append(lax.ppermute(second, ST, ring_perm(r, 0)))
    a, b = [jnp.stack(a)], [jnp.stack(b)]
    for r in range(3):
        a.append(lax.ppermute(a[-1], ST, RING_X))
        b.append(lax.ppermute(b[-1], ST, RING_Y))
        if r == 0:
            a[1], b[1], *beside = lax.optimization_barrier((a[1], b[1], *beside))
    return a + b, beside


def gather_planes(pair, beside):
    mine, near, theirs, far = [pair], [lax.ppermute(pair, "tp", LANE)], [], []
    for r in range(1, 5):
        mine.append(lax.ppermute(mine[-1], SD, SPIN))
        if r == 1:
            mine[1], *beside = lax.optimization_barrier((mine[1], *beside))
        near.append(lax.ppermute(mine[r], "tp", LANE))
        if r < 4:
            theirs.append(lax.ppermute(mine[r], "section", SWAP))
            far.append(lax.ppermute(mine[r], ST, BOTH))
    return mine + theirs + near + far, beside


def placed(refs, section):
    for n, ref in enumerate(refs):
        r = n if n < 5 else n - 4
        up, down = (r, (8 - r) % 8) if n < 5 else (8 - r, r)
        below = jnp.where(section == 0, up, down)
        for e in range(2):
            yield ref.at[e], (e if n < 5 else 1 - e), below


def group_at(info, other, below):
    section = info[1] if other == 0 else 1 - info[1]
    return section * 8 + lax.rem(info[2] - below + 8, 8)


def specs(smem, vmem, anywhere=0):
    return (
        [pl.BlockSpec(memory_space=pltpu.SMEM)] * smem
        + [pl.BlockSpec(memory_space=pltpu.VMEM)] * vmem
        + [pl.BlockSpec(memory_space=pl.ANY)] * anywhere
    )


def params(mib):
    return pltpu.CompilerParams(vmem_limit_bytes=mib << 20)


def start_copies(w, held, sems, order=None):
    copies = []
    for n in range(16):
        copy = pltpu.make_async_copy(w.at[n if order is None else order[n]], held.at[n], sems.at[n])
        copy.start()
        copies.append(copy)
    return copies


def key_kernel(tokens, order, *refs):
    a, b, w, out, held, sems = refs[:4], refs[4:8], refs[8], *refs[9:]
    depth, cols = held.shape[1:]
    half = tokens // 2
    copies = start_copies(w.at[:, :, w.shape[2] - cols :], held, sems, order)
    total = None
    for i in range(4):
        rows = jnp.concatenate(
            [
                jnp.concatenate([a[i][j, :half, :] for j in range(4)], axis=1),
                jnp.concatenate([b[j][i, :half, :] for j in range(4)], axis=1),
            ],
            axis=0,
        )
        for j in range(4):
            copies[4 * i + j].wait()
        block = held[4 * i : 4 * i + 4].reshape(4 * depth, cols)
        part = jnp.dot(rows, block, preferred_element_type=jnp.float32)
        total = part if total is None else total + part
    out[...] = total.astype(out.dtype)


def project_keys(order, blocks, w, cols, tokens):
    depth = w.shape[1]
    return pl.pallas_call(
        functools.partial(key_kernel, tokens),
        out_shape=jax.ShapeDtypeStruct((tokens, cols), jnp.bfloat16),
        in_specs=specs(1, 8, 1),
        out_specs=specs(0, 1)[0],
        scratch_shapes=[
            pltpu.VMEM((16, depth, cols), jnp.bfloat16),
            pltpu.SemaphoreType.DMA((16,)),
        ],
        compiler_params=params(47),
        cost_estimate=pl.CostEstimate(
            flops=2 * tokens * 16 * depth * cols,
            bytes_accessed=2 * 16 * depth * (tokens + cols),
            transcendentals=0,
        ),
        name="project_keys",
    )(order, *blocks, w)


def project_kernel(tokens, order, *refs):
    a, b, w, pre, dec, kv, held, sems = refs[:4], refs[4:8], refs[8], *refs[9:]
    q_cols = pre.shape[1]
    half, each = tokens // 2, a[0].shape[1]
    late = each - half
    copies = start_copies(w, held, sems, order)
    total, total_kv = None, None
    for n in range(16):
        i, j = n // 4, n % 4
        rows = jnp.concatenate([a[i][j], b[j][i]], axis=0)
        rows_kv = jnp.concatenate([a[i][j, half:, :], b[j][i, half:, :]], axis=0)
        copies[n].wait()
        part = jnp.dot(rows, held[n, :, :q_cols], preferred_element_type=jnp.float32)
        part_kv = jnp.dot(rows_kv, held[n, :, q_cols:], preferred_element_type=jnp.float32)
        total = part if total is None else total + part
        total_kv = part_kv if total_kv is None else total_kv + part_kv
    kv[...] = total_kv.astype(kv.dtype)
    result = total.astype(pre.dtype)
    for first in range(2):
        start = first * each
        pre[first * half : (first + 1) * half, :] = result[start : start + half]
        dec[first * late : (first + 1) * late, :] = result[start + half : start + each]


def project(order, blocks, w, q_cols, tokens):
    rows = 2 * blocks[0].shape[1]
    depth, cols = w.shape[1:]
    return pl.pallas_call(
        functools.partial(project_kernel, tokens),
        out_shape=[
            jax.ShapeDtypeStruct((tokens, q_cols), jnp.bfloat16),
            jax.ShapeDtypeStruct((rows - tokens, q_cols), jnp.bfloat16),
            jax.ShapeDtypeStruct((rows - tokens, cols - q_cols), jnp.bfloat16),
        ],
        in_specs=specs(1, 8, 1),
        out_specs=specs(0, 3),
        scratch_shapes=[
            pltpu.VMEM((16, depth, cols), jnp.bfloat16),
            pltpu.SemaphoreType.DMA((16,)),
        ],
        compiler_params=params(47),
        cost_estimate=pl.CostEstimate(
            flops=2 * rows * 16 * depth * cols,
            bytes_accessed=2 * 16 * depth * (rows + cols),
            transcendentals=0,
        ),
        name="project",
    )(order, *blocks, w)


def dot_t(a, b):
    return lax.dot_general(a, b, (((1,), (1,)), ((), ())), preferred_element_type=jnp.float32)


def lanes_max(value, top):
    for n in range(0, value.shape[-1], HD):
        top = jnp.maximum(top, value[..., n : n + HD])
    return top


def lanes_sum(value, total):
    for n in range(0, value.shape[-1], HD):
        total = total + value[..., n : n + HD]
    return total


def prefill_kernel(info, q, *refs):
    kv, out, qs, kvs, sc, mx, ls, acc, sems = refs[:16], *refs[16:]
    tokens = q.shape[0]
    wide = kvs.shape[2]
    heads = q.shape[1] // HD
    last, late = lax.div(info[0], 2), lax.rem(info[0], 2) * tokens
    copies = []
    for kind, blocks in ((info[3], kv[:8]), (1 - info[3], kv[8:])):
        for block, other, below in placed(blocks, info[1]):
            group = group_at(info, other, below)
            at = pl.ds(pl.multiple_of(lax.rem(group, 2) * tokens, tokens), tokens)
            target = kvs.at[lax.div(group, 2), kind, at, :]
            copies.append(pltpu.make_async_copy(block, target, sems.at[len(copies)]))
            copies[-1].start()
    for h in range(heads):
        qs[h] = q[:, h * HD : (h + 1) * HD]
    for copy in copies:
        copy.wait()

    row = lax.broadcasted_iota(jnp.int32, (tokens, wide), 0)
    col = lax.broadcasted_iota(jnp.int32, (tokens, wide), 1)
    for h in range(heads):
        scores = jnp.where(col <= row + late, dot_t(qs[h], kvs[last, 0]), NEG)
        sc[last, h] = scores
        mx[h] = lanes_max(scores[:, HD:], scores[:, :HD])

    @pl.loop(0, last)
    def _(n):
        for h in range(heads):
            scores = dot_t(qs[h], kvs[n, 0])
            sc[n, h] = scores
            mx[h] = lanes_max(scores, mx[h])

    for h in range(heads):
        top = jnp.max(mx[h], axis=-1, keepdims=True) * (SCALE * LOG2E)
        mx[h] = jnp.broadcast_to(top, (tokens, HD))
        ls[h] = jnp.zeros((tokens, HD), jnp.float32)
        acc[h] = jnp.zeros((tokens, HD), jnp.float32)

    @pl.loop(0, last + 1)
    def _(n):
        for h in range(heads):
            top = jnp.concatenate([mx[h]] * (wide // HD), axis=1)
            probs = jnp.exp2(sc[n, h] * (SCALE * LOG2E) - top)
            ls[h] = lanes_sum(probs, ls[h])
            acc[h] += jnp.dot(
                probs.astype(jnp.bfloat16), kvs[n, 1], preferred_element_type=jnp.float32
            )

    for h in range(heads):
        total = jnp.sum(ls[h], axis=-1, keepdims=True)
        out[:, h * HD : (h + 1) * HD] = (acc[h] / total).astype(out.dtype)


def prefill_attention(info, q, kv):
    tokens, cols = q.shape
    heads = cols // HD
    return pl.pallas_call(
        prefill_kernel,
        out_shape=jax.ShapeDtypeStruct(q.shape, jnp.bfloat16),
        in_specs=specs(1, 1, 16),
        out_specs=specs(0, 1)[0],
        scratch_shapes=[
            pltpu.VMEM((heads, tokens, HD), jnp.bfloat16),
            pltpu.VMEM((8, 2, 2 * tokens, HD), jnp.bfloat16),
            pltpu.VMEM((8, heads, tokens, 2 * tokens), jnp.float32),
            pltpu.VMEM((heads, tokens, HD), jnp.float32),
            pltpu.VMEM((heads, tokens, HD), jnp.float32),
            pltpu.VMEM((heads, tokens, HD), jnp.float32),
            pltpu.SemaphoreType.DMA((32,)),
        ],
        compiler_params=params(36),
        cost_estimate=pl.CostEstimate(
            flops=4 * 4096 * tokens * cols, bytes_accessed=3 << 20, transcendentals=4096 * 1024
        ),
        name="prefill_attention",
    )(info, q, *kv)


def decode_kernel(info, placement, q, keys, values, table, lens, mine, low, high, *refs):
    kv, res, held, bias, sc, sems = refs[:16], *refs[16:]
    slots = mine.shape[0]
    requests, pages = table.shape
    steps = q.shape[0] // requests
    heads = q.shape[1] // HD
    lane = info[3]
    pools = []
    starts = (lane * slots, (1 - lane) * slots, (1 - lane) * slots + slots // 2)
    for pool, first in zip((mine, low, high), starts):
        for c in range(2):
            source = pool.at[:, :, c * HD : (c + 1) * HD]
            target = held.at[c, pl.ds(first, pool.shape[0])]
            pools.append(pltpu.make_async_copy(source, target, sems.at[len(pools)]))
            pools[-1].start()

    offset = lax.broadcasted_iota(jnp.int32, (requests, PAGE), 1)
    length = jnp.broadcast_to(lens[...], (requests, PAGE))
    named = []
    for j in range(pages):
        slot = jnp.broadcast_to(table[:, j : j + 1], (requests, PAGE))
        named.append(jnp.where(offset + j * PAGE < length, slot, -1))
    for slot in range(2 * slots):
        count = jnp.zeros((requests, PAGE), jnp.float32)
        for j in range(slot // slots, pages, 2):
            count = count + jnp.where(named[j] == slot, 1.0, 0.0)
        bias[:, slot * PAGE : (slot + 1) * PAGE] = jnp.where(
            count > 0, jnp.log2(jnp.maximum(count, 1.0)), NEG
        )

    for copy in pools:
        copy.wait()
    landings = []
    for (block, far, below), (swapped, _, _) in zip(placed(kv[:8], info[1]), placed(kv[8:], info[1])):
        number = 2 * group_at(info, far, below)
        for half in range(2):
            hit, target = placement[number + half, 0] == info[0], placement[number + half, 1]
            pair = []
            for kind, source in ((lane, block), (1 - lane, swapped)):
                source = source.at[half * PAGE : (half + 1) * PAGE, :]
                at = len(pools) + 2 * len(landings) + len(pair)
                pair.append(pltpu.make_async_copy(source, held.at[kind, target], sems.at[at]))
            landings.append((hit, pair))
    for hit, pair in landings:

        @pl.when(hit)
        def _():
            for copy in pair:
                copy.start()

    for hit, pair in landings:

        @pl.when(hit)
        def _():
            for copy in pair:
                copy.wait()

    chunk = 8
    width = chunk * PAGE
    for step in range(steps):
        q_rows = q[step * requests : (step + 1) * requests, :]
        stacked = jnp.concatenate([q_rows[:, h * HD : (h + 1) * HD] for h in range(heads)], axis=0)
        wide = stacked.astype(jnp.float32).reshape(heads, requests, HD)
        fresh = []
        for t in range(step + 1):
            key = keys[t * requests : (t + 1) * requests, :].astype(jnp.float32)
            fresh.append(jnp.sum(wide * key[None], axis=-1, keepdims=True) * (SCALE * LOG2E))
        top = fresh[0]
        for score in fresh[1:]:
            top = jnp.maximum(top, score)
        lane_top = jnp.broadcast_to(top, (heads, requests, HD))
        for n in range(2 * slots // chunk):
            k = held[0, n * chunk : (n + 1) * chunk].reshape(width, HD)
            scores = dot_t(stacked, k).reshape(heads, requests, width) * (SCALE * LOG2E)
            scores = scores + bias[:, n * width : (n + 1) * width][None]
            sc[n] = scores
            lane_top = lanes_max(scores, lane_top)
        top = jnp.max(lane_top, axis=-1, keepdims=True)
        total = jnp.zeros((heads, requests, 1), jnp.float32)
        weighted = jnp.zeros((heads, requests, HD), jnp.float32)
        for t, score in enumerate(fresh):
            prob = jnp.exp2(score - top)
            value = values[t * requests : (t + 1) * requests, :].astype(jnp.float32)
            total = total + prob
            weighted = weighted + prob * value[None]
        wide_top = jnp.broadcast_to(top, (heads, requests, HD))
        lane_sum = jnp.zeros((heads, requests, HD), jnp.float32)
        for n in range(2 * slots // chunk):
            v = held[1, n * chunk : (n + 1) * chunk].reshape(width, HD)
            probs = jnp.exp2(sc[n] - jnp.concatenate([wide_top] * chunk, axis=-1))
            lane_sum = lanes_sum(probs, lane_sum)
            update = jnp.dot(
                probs.reshape(heads * requests, width).astype(jnp.bfloat16),
                v,
                preferred_element_type=jnp.float32,
            )
            weighted = weighted + update.reshape(heads, requests, HD)
        total = total + jnp.sum(lane_sum, axis=-1, keepdims=True)
        result = (weighted / total).astype(res.dtype)
        for h in range(heads):
            res[step * requests : (step + 1) * requests, h * HD : (h + 1) * HD] = result[h]


def decode_attention(info, placement, q, keys, values, table, lens, mine, low, high, kv):
    slots = mine.shape[0]
    requests = table.shape[0]
    cols = q.shape[1]
    return pl.pallas_call(
        decode_kernel,
        out_shape=jax.ShapeDtypeStruct(q.shape, jnp.bfloat16),
        in_specs=specs(2, 5, 19),
        out_specs=specs(0, 1)[0],
        scratch_shapes=[
            pltpu.VMEM((2, 2 * slots, PAGE, HD), jnp.bfloat16),
            pltpu.VMEM((requests, 2 * slots * PAGE), jnp.float32),
            pltpu.VMEM((2 * slots // 8, cols // HD, requests, 8 * PAGE), jnp.float32),
            pltpu.SemaphoreType.DMA((70,)),
        ],
        compiler_params=params(32),
        cost_estimate=pl.CostEstimate(
            flops=4 * 768 * 4096 * HD, bytes_accessed=5 << 20, transcendentals=768 * 4096
        ),
        name="decode_attention",
    )(info, placement, q, keys, values, table, lens, mine, low, high, *kv)


def output_kernel(info, *refs):
    rows, w, outs, held, sems = refs[:4], refs[4], refs[5:9], refs[9], refs[10]
    width = w.shape[2]
    copies = []
    for n in range(16):
        k, c = n // 4, n % 4
        block = w.at[lax.rem(info[4] + k, 4) * 4 + c]
        copy = pltpu.make_async_copy(
            block, held.at[k, :, c * width : (c + 1) * width], sems.at[n]
        )
        copy.start()
        copies.append(copy)
    wide = jnp.concatenate([row[...] for row in rows], axis=1)
    for k in range(4):
        for c in range(4):
            copies[4 * k + c].wait()
        result = jnp.dot(wide, held[k], preferred_element_type=jnp.float32)
        outs[k][...] = result.astype(outs[k].dtype)


def output_projection(info, rows, w):
    count, depth = rows[0].shape
    cols = 4 * w.shape[2]
    return pl.pallas_call(
        output_kernel,
        out_shape=[jax.ShapeDtypeStruct((count, cols), jnp.bfloat16)] * 4,
        in_specs=specs(1, 4, 1),
        out_specs=specs(0, 4),
        scratch_shapes=[
            pltpu.VMEM((4, 4 * depth, cols), jnp.bfloat16),
            pltpu.SemaphoreType.DMA((16,)),
        ],
        compiler_params=params(50),
        cost_estimate=pl.CostEstimate(
            flops=32 * count * depth * cols, bytes_accessed=10 << 20, transcendentals=0
        ),
        name="output_projection",
    )(info, *rows, w)


def quarter(info, k, width):
    return pl.ds(pl.multiple_of(lax.rem(info[5] + k, 4) * width, width), width)


def sum_kernel(info, *refs):
    parts, outs, held = refs[:4], refs[4:8], refs[8]
    total = parts[0][...].astype(jnp.float32)
    for part in parts[1:]:
        total = total + part[...].astype(jnp.float32)
    held[...] = total
    for k in range(4):
        outs[k][...] = held[:, quarter(info, k, outs[k].shape[1])].astype(outs[k].dtype)


def sum_parts(info, parts):
    rows, cols = parts[0].shape
    return pl.pallas_call(
        sum_kernel,
        out_shape=[jax.ShapeDtypeStruct((rows, cols // 4), jnp.bfloat16)] * 4,
        in_specs=specs(1, 4),
        out_specs=specs(0, 4),
        scratch_shapes=[pltpu.VMEM((rows, cols), jnp.float32)],
        compiler_params=params(16),
        name="sum_parts",
    )(info, *parts)


def assemble_kernel(info, *refs):
    pieces, out = refs[:4], refs[4]
    for k in range(4):
        out[:, quarter(info, 4 - k, pieces[k].shape[1])] = pieces[k][...]


def assemble(info, pieces):
    rows, cols = pieces[0].shape
    return pl.pallas_call(
        assemble_kernel,
        out_shape=jax.ShapeDtypeStruct((rows, 4 * cols), jnp.bfloat16),
        in_specs=specs(1, 4),
        out_specs=specs(0, 1)[0],
        compiler_params=params(16),
        name="assemble",
    )(info, *pieces)


def along(values, dx, dy):
    sent = list(values)
    for k in (2, 1, 3):
        sent[k] = lax.ppermute(values[k], "tp", tp_perm(k * dx, k * dy))
    return sent


def on_device(
    x_prefill, x_decode, w_query, w_keyval, w_out, cache_pool, placement, page_table, cache_len
):
    tokens = x_prefill.shape[0]
    steps, requests, width = x_decode.shape
    section, tp, plane = lax.axis_index("section"), lax.axis_index("tp"), lax.axis_index("dp")
    x, y = lax.div(tp, 4), lax.rem(tp, 4)
    lane = lax.rem(tp, 2)
    group = section * 8 + plane
    info = jnp.stack([group, section, plane, lane, x, y, tp]).astype(jnp.int32)
    turn = jnp.where(section == 0, 1, -1)
    count = jnp.arange(16, dtype=jnp.int32)
    order = lax.rem(x - turn * (count // 4) + 4, 4) * 4 + lax.rem(y - turn * (count % 4) + 4, 4)

    q_cols = w_query.shape[1]
    kv_cols = w_keyval.shape[1]
    w_all = lax.all_gather(jnp.concatenate([w_query, w_keyval], axis=1), SD, axis=0, tiled=False)

    part = w_out.shape[1] // 4
    w_cut = along(
        [lax.dynamic_slice_in_dim(w_out, lax.rem(y + k, 4) * part, part, 1) for k in range(4)], 0, 1
    )
    rows = x_decode.reshape(steps * requests, width)
    half_p, half_d = tokens // 2, rows.shape[0] // 2
    mine = cache_pool[0]
    pool_half = mine.shape[0] // 2
    low = lax.ppermute(mine[:pool_half], "tp", LANE)
    blocks, (low, *w_cut) = gather_tp(
        jnp.concatenate([x_prefill[:half_p], rows[:half_d]], axis=0),
        jnp.concatenate([x_prefill[half_p:], rows[half_d:]], axis=0),
        [low, *w_cut],
    )
    wo_all = lax.all_gather(jnp.concatenate(w_cut, axis=0), SD, axis=0, tiled=False)
    kv_mine = project_keys(order, blocks, w_all, kv_cols, tokens)
    pair = jnp.stack([kv_mine, lax.ppermute(kv_mine, "section", SWAP)])
    high, pair = lax.optimization_barrier((mine[pool_half:], pair))
    kv, (q_pre, q_dec, new_mine) = gather_planes(pair, project(order, blocks, w_all, q_cols, tokens))
    new_lane = lax.ppermute(new_mine, "tp", LANE)
    high = lax.ppermute(high, "tp", LANE)
    is_key = lane == 0
    keys = jnp.where(is_key, new_mine, new_lane)
    values = jnp.where(is_key, new_lane, new_mine)

    attention = decode_attention(
        info, placement, q_dec, keys, values, page_table, cache_len[:, None], mine, low, high, kv
    )
    attended = along([attention] * 4, 0, 1)
    parts = along(output_projection(info, attended, wo_all), 1, 0)
    prefill_out = prefill_attention(info, q_pre, kv)
    prefill_out, *parts = lax.optimization_barrier((prefill_out, *parts))
    pieces = along(sum_parts(info, parts), 0, 1)
    decode_out = assemble(info, pieces).reshape(steps, requests, -1)
    return (prefill_out, decode_out)


def solution(mesh):
    return jax.shard_map(
        on_device,
        mesh=mesh,
        in_specs=(
            P(("section", "dp"), "tp"),
            P(None, ("section", "dp"), "tp"),
            P(("section", "dp"), "tp"),
            P(("section", "dp"), "tp"),
            P("tp", ("section", "dp")),
            P("tp", ("section", "dp"), None, None),
            P(),
            P(("section", "dp"), None),
            P(("section", "dp")),
        ),
        out_specs=(P(("section", "dp"), "tp"), P(None, ("section", "dp"), "tp")),
        check_vma=False,
    )
```

```python
import functools
import math

import jax
import jax.numpy as jnp
from jax import lax
from jax.experimental import pallas as pl
from jax.experimental.pallas import tpu as pltpu
from jax.sharding import PartitionSpec as P

HD = 128
PAGE = 128
NEG = -1e30
SCALE = 1.0 / math.sqrt(HD)
LOG2E = math.log2(math.e)

ST = ("section", "tp")
SD = ("section", "dp")

SWAP = [(0, 1), (1, 0)]
LANE = [(t, t ^ 1) for t in range(16)]
BOTH = [(t, t ^ 17) for t in range(32)]
SPIN = [(s * 8 + z, s * 8 + (z + 1 - 2 * s) % 8) for s in range(2) for z in range(8)]


def tp_perm(dx, dy):
    return [
        (x * 4 + y, (x + dx) % 4 * 4 + (y + dy) % 4) for x in range(4) for y in range(4)
    ]


def ring_perm(dx, dy):
    pairs = []
    for s in range(2):
        d = 1 - 2 * s
        pairs += [(s * 16 + a, s * 16 + b) for a, b in tp_perm(d * dx, d * dy)]
    return pairs


RING_X = ring_perm(1, 0)
RING_Y = ring_perm(0, 1)


def gather_tp(first, second, beside):
    a, b = [first], [second]
    for r in range(1, 4):
        a.append(lax.ppermute(first, ST, ring_perm(0, r)))
        b.append(lax.ppermute(second, ST, ring_perm(r, 0)))
    a, b = [jnp.stack(a)], [jnp.stack(b)]
    for r in range(3):
        a.append(lax.ppermute(a[-1], ST, RING_X))
        b.append(lax.ppermute(b[-1], ST, RING_Y))
        if r == 0:
            a[1], b[1], *beside = lax.optimization_barrier((a[1], b[1], *beside))
    return a + b, beside


def gather_planes(pair, beside):
    mine, theirs = [pair], []
    for r in range(1, 5):
        mine.append(lax.ppermute(mine[-1], SD, SPIN))
        if r == 1:
            mine[1], *beside = lax.optimization_barrier((mine[1], *beside))
        if r < 4:
            theirs.append(lax.ppermute(mine[r], "section", SWAP))
    return mine + theirs, beside


def placed(refs, section):
    for n, ref in enumerate(refs):
        r = n if n < 5 else n - 4
        up, down = (r, (8 - r) % 8) if n < 5 else (8 - r, r)
        below = jnp.where(section == 0, up, down)
        for e in range(2):
            yield ref.at[e], (e if n < 5 else 1 - e), below


def group_at(info, other, below):
    section = info[1] if other == 0 else 1 - info[1]
    return section * 8 + lax.rem(info[2] - below + 8, 8)


def specs(smem, vmem, anywhere=0):
    return (
        [pl.BlockSpec(memory_space=pltpu.SMEM)] * smem
        + [pl.BlockSpec(memory_space=pltpu.VMEM)] * vmem
        + [pl.BlockSpec(memory_space=pl.ANY)] * anywhere
    )


def params(mib):
    return pltpu.CompilerParams(vmem_limit_bytes=mib << 20)


def start_copies(w, held, sems, order=None):
    copies = []
    for n in range(16):
        copy = pltpu.make_async_copy(w.at[n if order is None else order[n]], held.at[n], sems.at[n])
        copy.start()
        copies.append(copy)
    return copies


def key_kernel(tokens, order, *refs):
    a, b, w, out, held, sems = refs[:4], refs[4:8], refs[8], *refs[9:]
    depth, cols = held.shape[1:]
    half = tokens // 2
    copies = start_copies(w.at[:, :, w.shape[2] - cols :], held, sems, order)
    total = None
    for i in range(4):
        rows = jnp.concatenate(
            [
                jnp.concatenate([a[i][j, :half, :] for j in range(4)], axis=1),
                jnp.concatenate([b[j][i, :half, :] for j in range(4)], axis=1),
            ],
            axis=0,
        )
        for j in range(4):
            copies[4 * i + j].wait()
        block = held[4 * i : 4 * i + 4].reshape(4 * depth, cols)
        part = jnp.dot(rows, block, preferred_element_type=jnp.float32)
        total = part if total is None else total + part
    out[...] = total.astype(out.dtype)


def project_keys(order, blocks, w, cols, tokens):
    depth = w.shape[1]
    return pl.pallas_call(
        functools.partial(key_kernel, tokens),
        out_shape=jax.ShapeDtypeStruct((tokens, cols), jnp.bfloat16),
        in_specs=specs(1, 8, 1),
        out_specs=specs(0, 1)[0],
        scratch_shapes=[
            pltpu.VMEM((16, depth, cols), jnp.bfloat16),
            pltpu.SemaphoreType.DMA((16,)),
        ],
        compiler_params=params(47),
        cost_estimate=pl.CostEstimate(
            flops=2 * tokens * 16 * depth * cols,
            bytes_accessed=2 * 16 * depth * (tokens + cols),
            transcendentals=0,
        ),
        name="project_keys",
    )(order, *blocks, w)


def project_kernel(tokens, order, *refs):
    a, b, w, pre, dec, kv, held, sems = refs[:4], refs[4:8], refs[8], *refs[9:]
    q_cols = pre.shape[1]
    half, each = tokens // 2, a[0].shape[1]
    late = each - half
    copies = start_copies(w, held, sems, order)
    total, total_kv = None, None
    for n in range(16):
        i, j = n // 4, n % 4
        rows = jnp.concatenate([a[i][j], b[j][i]], axis=0)
        rows_kv = jnp.concatenate([a[i][j, half:, :], b[j][i, half:, :]], axis=0)
        copies[n].wait()
        part = jnp.dot(rows, held[n, :, :q_cols], preferred_element_type=jnp.float32)
        part_kv = jnp.dot(rows_kv, held[n, :, q_cols:], preferred_element_type=jnp.float32)
        total = part if total is None else total + part
        total_kv = part_kv if total_kv is None else total_kv + part_kv
    kv[...] = total_kv.astype(kv.dtype)
    result = total.astype(pre.dtype)
    for first in range(2):
        start = first * each
        pre[first * half : (first + 1) * half, :] = result[start : start + half]
        dec[first * late : (first + 1) * late, :] = result[start + half : start + each]


def project(order, blocks, w, q_cols, tokens):
    rows = 2 * blocks[0].shape[1]
    depth, cols = w.shape[1:]
    return pl.pallas_call(
        functools.partial(project_kernel, tokens),
        out_shape=[
            jax.ShapeDtypeStruct((tokens, q_cols), jnp.bfloat16),
            jax.ShapeDtypeStruct((rows - tokens, q_cols), jnp.bfloat16),
            jax.ShapeDtypeStruct((rows - tokens, cols - q_cols), jnp.bfloat16),
        ],
        in_specs=specs(1, 8, 1),
        out_specs=specs(0, 3),
        scratch_shapes=[
            pltpu.VMEM((16, depth, cols), jnp.bfloat16),
            pltpu.SemaphoreType.DMA((16,)),
        ],
        compiler_params=params(47),
        cost_estimate=pl.CostEstimate(
            flops=2 * rows * 16 * depth * cols,
            bytes_accessed=2 * 16 * depth * (rows + cols),
            transcendentals=0,
        ),
        name="project",
    )(order, *blocks, w)


def dot_t(a, b):
    return lax.dot_general(a, b, (((1,), (1,)), ((), ())), preferred_element_type=jnp.float32)


def lanes_max(value, top):
    for n in range(0, value.shape[-1], HD):
        top = jnp.maximum(top, value[..., n : n + HD])
    return top


def lanes_sum(value, total):
    for n in range(0, value.shape[-1], HD):
        total = total + value[..., n : n + HD]
    return total


def prefill_kernel(info, q, *refs):
    kv, out, qs, kvs, sc, mx, ls, acc, sems = refs[:8], *refs[8:]
    tokens = q.shape[0]
    wide = kvs.shape[2]
    heads = q.shape[1] // HD
    last, late = lax.div(info[0], 2), lax.rem(info[0], 2) * tokens
    copies = []
    for block, other, below in placed(kv, info[1]):
        group = group_at(info, other, below)
        at = pl.ds(pl.multiple_of(lax.rem(group, 2) * tokens, tokens), tokens)
        target = kvs.at[lax.div(group, 2), :, at, :]
        copies.append(pltpu.make_async_copy(block, target, sems.at[len(copies)]))
        copies[-1].start()
    for h in range(heads):
        qs[h] = q[:, h * HD : (h + 1) * HD]
    for copy in copies:
        copy.wait()

    row = lax.broadcasted_iota(jnp.int32, (tokens, wide), 0)
    col = lax.broadcasted_iota(jnp.int32, (tokens, wide), 1)
    for h in range(heads):
        scores = jnp.where(col <= row + late, dot_t(qs[h], kvs[last, 0]), NEG)
        sc[last, h] = scores
        mx[h] = lanes_max(scores[:, HD:], scores[:, :HD])

    @pl.loop(0, last)
    def _(n):
        for h in range(heads):
            scores = dot_t(qs[h], kvs[n, 0])
            sc[n, h] = scores
            mx[h] = lanes_max(scores, mx[h])

    for h in range(heads):
        top = jnp.max(mx[h], axis=-1, keepdims=True) * (SCALE * LOG2E)
        mx[h] = jnp.broadcast_to(top, (tokens, HD))
        ls[h] = jnp.zeros((tokens, HD), jnp.float32)
        acc[h] = jnp.zeros((tokens, HD), jnp.float32)

    @pl.loop(0, last + 1)
    def _(n):
        for h in range(heads):
            top = jnp.concatenate([mx[h]] * (wide // HD), axis=1)
            probs = jnp.exp2(sc[n, h] * (SCALE * LOG2E) - top)
            ls[h] = lanes_sum(probs, ls[h])
            acc[h] += jnp.dot(
                probs.astype(jnp.bfloat16), kvs[n, 1], preferred_element_type=jnp.float32
            )

    for h in range(heads):
        total = jnp.sum(ls[h], axis=-1, keepdims=True)
        out[:, h * HD : (h + 1) * HD] = (acc[h] / total).astype(out.dtype)


def prefill_attention(info, q, kv):
    tokens, cols = q.shape
    heads = cols // HD
    return pl.pallas_call(
        prefill_kernel,
        out_shape=jax.ShapeDtypeStruct(q.shape, jnp.bfloat16),
        in_specs=specs(1, 1, 8),
        out_specs=specs(0, 1)[0],
        scratch_shapes=[
            pltpu.VMEM((heads, tokens, HD), jnp.bfloat16),
            pltpu.VMEM((8, 2, 2 * tokens, HD), jnp.bfloat16),
            pltpu.VMEM((8, heads, tokens, 2 * tokens), jnp.float32),
            pltpu.VMEM((heads, tokens, HD), jnp.float32),
            pltpu.VMEM((heads, tokens, HD), jnp.float32),
            pltpu.VMEM((heads, tokens, HD), jnp.float32),
            pltpu.SemaphoreType.DMA((16,)),
        ],
        compiler_params=params(36),
        cost_estimate=pl.CostEstimate(
            flops=4 * 4096 * tokens * cols, bytes_accessed=3 << 20, transcendentals=4096 * 1024
        ),
        name="prefill_attention",
    )(info, q, *kv)


def mask_kernel(table, lens, bias):
    requests, pages = table.shape
    slots = bias.shape[1] // PAGE // 2
    offset = lax.broadcasted_iota(jnp.int32, (requests, PAGE), 1)
    length = jnp.broadcast_to(lens[...], (requests, PAGE))
    named = []
    for j in range(pages):
        slot = jnp.broadcast_to(table[:, j : j + 1], (requests, PAGE))
        named.append(jnp.where(offset + j * PAGE < length, slot, -1))
    for slot in range(2 * slots):
        count = jnp.zeros((requests, PAGE), jnp.float32)
        for j in range(slot // slots, pages, 2):
            count = count + jnp.where(named[j] == slot, 1.0, 0.0)
        bias[:, slot * PAGE : (slot + 1) * PAGE] = jnp.where(
            count > 0, jnp.log2(jnp.maximum(count, 1.0)), NEG
        )


def cache_mask(table, lens, slots):
    return pl.pallas_call(
        mask_kernel,
        out_shape=jax.ShapeDtypeStruct((table.shape[0], 2 * slots * PAGE), jnp.float32),
        in_specs=specs(0, 2),
        out_specs=specs(0, 1)[0],
        compiler_params=params(16),
        name="cache_mask",
    )(table, lens)


def decode_kernel(info, placement, q, keys, values, bias, mine, other, *refs):
    kv, res, ks, vs, sc, sems = refs[:8], *refs[8:]
    slots = mine.shape[0]
    requests = bias.shape[0]
    steps = q.shape[0] // requests
    heads = q.shape[1] // HD
    lane = info[3]
    pools = []
    for pool, first in ((mine, lane * slots), (other, (1 - lane) * slots)):
        for c, held in enumerate((ks, vs)):
            source, target = pool.at[:, :, c * HD : (c + 1) * HD], held.at[pl.ds(first, slots)]
            pools.append(pltpu.make_async_copy(source, target, sems.at[len(pools)]))
            pools[-1].start()

    for copy in pools:
        copy.wait()
    landings = []
    for block, far, below in placed(kv, info[1]):
        number = 2 * group_at(info, far, below)
        for half in range(2):
            hit, target = placement[number + half, 0] == info[0], placement[number + half, 1]
            pair = []
            for c, held in enumerate((ks, vs)):
                source = block.at[c, half * PAGE : (half + 1) * PAGE, :]
                at = len(pools) + 2 * len(landings) + c
                pair.append(pltpu.make_async_copy(source, held.at[target], sems.at[at]))
            landings.append((hit, pair))
    for hit, pair in landings:

        @pl.when(hit)
        def _():
            for copy in pair:
                copy.start()

    for hit, pair in landings:

        @pl.when(hit)
        def _():
            for copy in pair:
                copy.wait()

    chunk = 8
    width = chunk * PAGE
    for step in range(steps):
        q_rows = q[step * requests : (step + 1) * requests, :]
        stacked = jnp.concatenate([q_rows[:, h * HD : (h + 1) * HD] for h in range(heads)], axis=0)
        wide = stacked.astype(jnp.float32).reshape(heads, requests, HD)
        fresh = []
        for t in range(step + 1):
            key = keys[t * requests : (t + 1) * requests, :].astype(jnp.float32)
            fresh.append(jnp.sum(wide * key[None], axis=-1, keepdims=True) * (SCALE * LOG2E))
        top = fresh[0]
        for score in fresh[1:]:
            top = jnp.maximum(top, score)
        lane_top = jnp.broadcast_to(top, (heads, requests, HD))
        for n in range(2 * slots // chunk):
            k = ks[n * chunk : (n + 1) * chunk].reshape(width, HD)
            scores = dot_t(stacked, k).reshape(heads, requests, width) * (SCALE * LOG2E)
            scores = scores + bias[:, n * width : (n + 1) * width][None]
            sc[n] = scores
            lane_top = lanes_max(scores, lane_top)
        top = jnp.max(lane_top, axis=-1, keepdims=True)
        total = jnp.zeros((heads, requests, 1), jnp.float32)
        weighted = jnp.zeros((heads, requests, HD), jnp.float32)
        for t, score in enumerate(fresh):
            prob = jnp.exp2(score - top)
            value = values[t * requests : (t + 1) * requests, :].astype(jnp.float32)
            total = total + prob
            weighted = weighted + prob * value[None]
        wide_top = jnp.broadcast_to(top, (heads, requests, HD))
        lane_sum = jnp.zeros((heads, requests, HD), jnp.float32)
        for n in range(2 * slots // chunk):
            v = vs[n * chunk : (n + 1) * chunk].reshape(width, HD)
            probs = jnp.exp2(sc[n] - jnp.concatenate([wide_top] * chunk, axis=-1))
            lane_sum = lanes_sum(probs, lane_sum)
            update = jnp.dot(
                probs.reshape(heads * requests, width).astype(jnp.bfloat16),
                v,
                preferred_element_type=jnp.float32,
            )
            weighted = weighted + update.reshape(heads, requests, HD)
        total = total + jnp.sum(lane_sum, axis=-1, keepdims=True)
        result = (weighted / total).astype(res.dtype)
        for h in range(heads):
            res[step * requests : (step + 1) * requests, h * HD : (h + 1) * HD] = result[h]


def decode_attention(info, placement, q, keys, values, bias, mine, other, kv):
    slots = mine.shape[0]
    requests = bias.shape[0]
    cols = q.shape[1]
    return pl.pallas_call(
        decode_kernel,
        out_shape=jax.ShapeDtypeStruct(q.shape, jnp.bfloat16),
        in_specs=specs(2, 4, 10),
        out_specs=specs(0, 1)[0],
        scratch_shapes=[
            pltpu.VMEM((2 * slots, PAGE, HD), jnp.bfloat16),
            pltpu.VMEM((2 * slots, PAGE, HD), jnp.bfloat16),
            pltpu.VMEM((2 * slots // 8, cols // HD, requests, 8 * PAGE), jnp.float32),
            pltpu.SemaphoreType.DMA((68,)),
        ],
        compiler_params=params(32),
        cost_estimate=pl.CostEstimate(
            flops=4 * 768 * 4096 * HD, bytes_accessed=5 << 20, transcendentals=768 * 4096
        ),
        name="decode_attention",
    )(info, placement, q, keys, values, bias, mine, other, *kv)


def output_kernel(info, *refs):
    rows, w, outs, held, sems = refs[:4], refs[4], refs[5:9], refs[9], refs[10]
    width = w.shape[2]
    copies = []
    for n in range(16):
        k, c = n // 4, n % 4
        block = w.at[lax.rem(info[4] + k, 4) * 4 + c]
        copy = pltpu.make_async_copy(
            block, held.at[k, :, c * width : (c + 1) * width], sems.at[n]
        )
        copy.start()
        copies.append(copy)
    wide = jnp.concatenate([row[...] for row in rows], axis=1)
    for k in range(4):
        for c in range(4):
            copies[4 * k + c].wait()
        result = jnp.dot(wide, held[k], preferred_element_type=jnp.float32)
        outs[k][...] = result.astype(outs[k].dtype)


def output_projection(info, rows, w):
    count, depth = rows[0].shape
    cols = 4 * w.shape[2]
    return pl.pallas_call(
        output_kernel,
        out_shape=[jax.ShapeDtypeStruct((count, cols), jnp.bfloat16)] * 4,
        in_specs=specs(1, 4, 1),
        out_specs=specs(0, 4),
        scratch_shapes=[
            pltpu.VMEM((4, 4 * depth, cols), jnp.bfloat16),
            pltpu.SemaphoreType.DMA((16,)),
        ],
        compiler_params=params(50),
        cost_estimate=pl.CostEstimate(
            flops=32 * count * depth * cols, bytes_accessed=10 << 20, transcendentals=0
        ),
        name="output_projection",
    )(info, *rows, w)


def quarter(info, k, width):
    return pl.ds(pl.multiple_of(lax.rem(info[5] + k, 4) * width, width), width)


def sum_kernel(info, *refs):
    parts, outs, held = refs[:4], refs[4:8], refs[8]
    total = parts[0][...].astype(jnp.float32)
    for part in parts[1:]:
        total = total + part[...].astype(jnp.float32)
    held[...] = total
    for k in range(4):
        outs[k][...] = held[:, quarter(info, k, outs[k].shape[1])].astype(outs[k].dtype)


def sum_parts(info, parts):
    rows, cols = parts[0].shape
    return pl.pallas_call(
        sum_kernel,
        out_shape=[jax.ShapeDtypeStruct((rows, cols // 4), jnp.bfloat16)] * 4,
        in_specs=specs(1, 4),
        out_specs=specs(0, 4),
        scratch_shapes=[pltpu.VMEM((rows, cols), jnp.float32)],
        compiler_params=params(16),
        name="sum_parts",
    )(info, *parts)


def assemble_kernel(info, *refs):
    pieces, out = refs[:4], refs[4]
    for k in range(4):
        out[:, quarter(info, 4 - k, pieces[k].shape[1])] = pieces[k][...]


def assemble(info, pieces):
    rows, cols = pieces[0].shape
    return pl.pallas_call(
        assemble_kernel,
        out_shape=jax.ShapeDtypeStruct((rows, 4 * cols), jnp.bfloat16),
        in_specs=specs(1, 4),
        out_specs=specs(0, 1)[0],
        compiler_params=params(16),
        name="assemble",
    )(info, *pieces)


def along(values, dx, dy):
    sent = list(values)
    for k in (2, 1, 3):
        sent[k] = lax.ppermute(values[k], "tp", tp_perm(k * dx, k * dy))
    return sent


def on_device(
    x_prefill, x_decode, w_query, w_keyval, w_out, cache_pool, placement, page_table, cache_len
):
    tokens = x_prefill.shape[0]
    steps, requests, width = x_decode.shape
    section, tp, plane = lax.axis_index("section"), lax.axis_index("tp"), lax.axis_index("dp")
    x, y = lax.div(tp, 4), lax.rem(tp, 4)
    lane = lax.rem(tp, 2)
    group = section * 8 + plane
    info = jnp.stack([group, section, plane, lane, x, y, tp]).astype(jnp.int32)
    turn = jnp.where(section == 0, 1, -1)
    count = jnp.arange(16, dtype=jnp.int32)
    order = lax.rem(x - turn * (count // 4) + 4, 4) * 4 + lax.rem(y - turn * (count % 4) + 4, 4)

    q_cols = w_query.shape[1]
    kv_cols = w_keyval.shape[1]
    w_all = lax.all_gather(jnp.concatenate([w_query, w_keyval], axis=1), SD, axis=0, tiled=False)

    part = w_out.shape[1] // 4
    w_cut = along(
        [lax.dynamic_slice_in_dim(w_out, lax.rem(y + k, 4) * part, part, 1) for k in range(4)], 0, 1
    )
    rows = x_decode.reshape(steps * requests, width)
    half_p, half_d = tokens // 2, rows.shape[0] // 2
    bias = cache_mask(page_table, cache_len[:, None], cache_pool.shape[1])
    blocks, (bias, *w_cut) = gather_tp(
        jnp.concatenate([x_prefill[:half_p], rows[:half_d]], axis=0),
        jnp.concatenate([x_prefill[half_p:], rows[half_d:]], axis=0),
        [bias, *w_cut],
    )
    wo_all = lax.all_gather(jnp.concatenate(w_cut, axis=0), SD, axis=0, tiled=False)
    kv_mine = project_keys(order, blocks, w_all, kv_cols, tokens)
    kv_lane = lax.ppermute(kv_mine, "tp", LANE)
    kv_core = lax.ppermute(kv_mine, "section", SWAP)
    kv_both = lax.ppermute(kv_mine, ST, BOTH)
    mine, kv_lane, kv_core, kv_both = lax.optimization_barrier(
        (cache_pool[0], kv_lane, kv_core, kv_both)
    )
    is_key = lane == 0
    pair = jnp.stack(
        [
            jnp.stack([jnp.where(is_key, p, q), jnp.where(is_key, q, p)])
            for p, q in ((kv_mine, kv_lane), (kv_core, kv_both))
        ]
    )
    kv, (q_pre, q_dec, new_mine) = gather_planes(pair, project(order, blocks, w_all, q_cols, tokens))
    new_lane = lax.ppermute(new_mine, "tp", LANE)
    other = lax.ppermute(mine, "tp", LANE)
    keys = jnp.where(is_key, new_mine, new_lane)
    values = jnp.where(is_key, new_lane, new_mine)

    attention = decode_attention(
        info, placement, q_dec, keys, values, bias, mine, other, kv
    )
    attended = along([attention] * 4, 0, 1)
    parts = along(output_projection(info, attended, wo_all), 1, 0)
    prefill_out = prefill_attention(info, q_pre, kv)
    prefill_out, *parts = lax.optimization_barrier((prefill_out, *parts))
    pieces = along(sum_parts(info, parts), 0, 1)
    decode_out = assemble(info, pieces).reshape(steps, requests, -1)
    return (prefill_out, decode_out)


def solution(mesh):
    return jax.shard_map(
        on_device,
        mesh=mesh,
        in_specs=(
            P(("section", "dp"), "tp"),
            P(None, ("section", "dp"), "tp"),
            P(("section", "dp"), "tp"),
            P(("section", "dp"), "tp"),
            P("tp", ("section", "dp")),
            P("tp", ("section", "dp"), None, None),
            P(),
            P(("section", "dp"), None),
            P(("section", "dp")),
        ),
        out_specs=(P(("section", "dp"), "tp"), P(None, ("section", "dp"), "tp")),
        check_vma=False,
    )
```

```python
import functools
import math

import jax
import jax.numpy as jnp
from jax import lax
from jax.experimental import pallas as pl
from jax.experimental.pallas import tpu as pltpu
from jax.sharding import PartitionSpec as P

HD = 128
PAGE = 128
NEG = -1e30
SCALE = 1.0 / math.sqrt(HD)
LOG2E = math.log2(math.e)

ST = ("section", "tp")
SD = ("section", "dp")

SWAP = [(0, 1), (1, 0)]
LANE = [(t, t ^ 1) for t in range(16)]
BOTH = [(t, t ^ 17) for t in range(32)]
SPIN = [(s * 8 + z, s * 8 + (z + 1 - 2 * s) % 8) for s in range(2) for z in range(8)]


def tp_perm(dx, dy):
    return [
        (x * 4 + y, (x + dx) % 4 * 4 + (y + dy) % 4) for x in range(4) for y in range(4)
    ]


def ring_perm(dx, dy):
    pairs = []
    for s in range(2):
        d = 1 - 2 * s
        pairs += [(s * 16 + a, s * 16 + b) for a, b in tp_perm(d * dx, d * dy)]
    return pairs


RING_X = ring_perm(1, 0)
RING_Y = ring_perm(0, 1)


def gather_tp(first, second, beside):
    a, b = [first], [second]
    for r in range(1, 4):
        a.append(lax.ppermute(first, ST, ring_perm(0, r)))
        b.append(lax.ppermute(second, ST, ring_perm(r, 0)))
    a, b = [jnp.stack(a)], [jnp.stack(b)]
    for r in range(3):
        a.append(lax.ppermute(a[-1], ST, RING_X))
        b.append(lax.ppermute(b[-1], ST, RING_Y))
        if r == 0:
            a[1], b[1], *beside = lax.optimization_barrier((a[1], b[1], *beside))
    return a + b, beside


def gather_planes(pair, beside):
    mine, theirs = [pair], []
    for r in range(1, 5):
        mine.append(lax.ppermute(mine[-1], SD, SPIN))
        if r == 3:
            mine[3], *beside = lax.optimization_barrier((mine[3], *beside))
        if r < 4:
            theirs.append(lax.ppermute(mine[r], "section", SWAP))
    return mine + theirs, beside


def placed(refs, section):
    for n, ref in enumerate(refs):
        r = n if n < 5 else n - 4
        up, down = (r, (8 - r) % 8) if n < 5 else (8 - r, r)
        below = jnp.where(section == 0, up, down)
        for e in range(2):
            yield ref.at[e], (e if n < 5 else 1 - e), below


def group_at(info, other, below):
    section = info[1] if other == 0 else 1 - info[1]
    return section * 8 + lax.rem(info[2] - below + 8, 8)


def specs(smem, vmem, anywhere=0):
    return (
        [pl.BlockSpec(memory_space=pltpu.SMEM)] * smem
        + [pl.BlockSpec(memory_space=pltpu.VMEM)] * vmem
        + [pl.BlockSpec(memory_space=pl.ANY)] * anywhere
    )


def params(mib):
    return pltpu.CompilerParams(vmem_limit_bytes=mib << 20)


def start_copies(w, held, sems, order=None):
    copies = []
    for n in range(16):
        copy = pltpu.make_async_copy(w.at[n if order is None else order[n]], held.at[n], sems.at[n])
        copy.start()
        copies.append(copy)
    return copies


def key_kernel(tokens, order, *refs):
    a, b, w, out, held, sems = refs[:4], refs[4:8], refs[8], *refs[9:]
    depth, cols = held.shape[1:]
    half = tokens // 2
    copies = start_copies(w.at[:, :, w.shape[2] - cols :], held, sems, order)
    total = None
    for i in range(4):
        rows = jnp.concatenate(
            [
                jnp.concatenate([a[i][j, :half, :] for j in range(4)], axis=1),
                jnp.concatenate([b[j][i, :half, :] for j in range(4)], axis=1),
            ],
            axis=0,
        )
        for j in range(4):
            copies[4 * i + j].wait()
        block = held[4 * i : 4 * i + 4].reshape(4 * depth, cols)
        part = jnp.dot(rows, block, preferred_element_type=jnp.float32)
        total = part if total is None else total + part
    out[...] = total.astype(out.dtype)


def project_keys(order, blocks, w, cols, tokens):
    depth = w.shape[1]
    return pl.pallas_call(
        functools.partial(key_kernel, tokens),
        out_shape=jax.ShapeDtypeStruct((tokens, cols), jnp.bfloat16),
        in_specs=specs(1, 8, 1),
        out_specs=specs(0, 1)[0],
        scratch_shapes=[
            pltpu.VMEM((16, depth, cols), jnp.bfloat16),
            pltpu.SemaphoreType.DMA((16,)),
        ],
        compiler_params=params(47),
        cost_estimate=pl.CostEstimate(
            flops=2 * tokens * 16 * depth * cols,
            bytes_accessed=2 * 16 * depth * (tokens + cols),
            transcendentals=0,
        ),
        name="project_keys",
    )(order, *blocks, w)


def project_kernel(tokens, order, *refs):
    a, b, w, pre, dec, kv, held, sems = refs[:4], refs[4:8], refs[8], *refs[9:]
    q_cols = pre.shape[1]
    half, each = tokens // 2, a[0].shape[1]
    late = each - half
    copies = start_copies(w, held, sems, order)
    total, total_kv = None, None
    for n in range(16):
        i, j = n // 4, n % 4
        rows = jnp.concatenate([a[i][j], b[j][i]], axis=0)
        rows_kv = jnp.concatenate([a[i][j, half:, :], b[j][i, half:, :]], axis=0)
        copies[n].wait()
        part = jnp.dot(rows, held[n, :, :q_cols], preferred_element_type=jnp.float32)
        part_kv = jnp.dot(rows_kv, held[n, :, q_cols:], preferred_element_type=jnp.float32)
        total = part if total is None else total + part
        total_kv = part_kv if total_kv is None else total_kv + part_kv
    kv[...] = total_kv.astype(kv.dtype)
    result = total.astype(pre.dtype)
    for first in range(2):
        start = first * each
        pre[first * half : (first + 1) * half, :] = result[start : start + half]
        dec[first * late : (first + 1) * late, :] = result[start + half : start + each]


def project(order, blocks, w, q_cols, tokens):
    rows = 2 * blocks[0].shape[1]
    depth, cols = w.shape[1:]
    return pl.pallas_call(
        functools.partial(project_kernel, tokens),
        out_shape=[
            jax.ShapeDtypeStruct((tokens, q_cols), jnp.bfloat16),
            jax.ShapeDtypeStruct((rows - tokens, q_cols), jnp.bfloat16),
            jax.ShapeDtypeStruct((rows - tokens, cols - q_cols), jnp.bfloat16),
        ],
        in_specs=specs(1, 8, 1),
        out_specs=specs(0, 3),
        scratch_shapes=[
            pltpu.VMEM((16, depth, cols), jnp.bfloat16),
            pltpu.SemaphoreType.DMA((16,)),
        ],
        compiler_params=params(47),
        cost_estimate=pl.CostEstimate(
            flops=2 * rows * 16 * depth * cols,
            bytes_accessed=2 * 16 * depth * (rows + cols),
            transcendentals=0,
        ),
        name="project",
    )(order, *blocks, w)


def dot_t(a, b):
    return lax.dot_general(a, b, (((1,), (1,)), ((), ())), preferred_element_type=jnp.float32)


def lanes_max(value, top):
    for n in range(0, value.shape[-1], HD):
        top = jnp.maximum(top, value[..., n : n + HD])
    return top


def lanes_sum(value, total):
    for n in range(0, value.shape[-1], HD):
        total = total + value[..., n : n + HD]
    return total


def prefill_kernel(info, q, *refs):
    kv, out, qs, kvs, sc, mx, ls, acc, sems = refs[:8], *refs[8:]
    tokens = q.shape[0]
    wide = kvs.shape[2]
    heads = q.shape[1] // HD
    last, late = lax.div(info[0], 2), lax.rem(info[0], 2) * tokens
    copies = []
    for block, other, below in placed(kv, info[1]):
        group = group_at(info, other, below)
        at = pl.ds(pl.multiple_of(lax.rem(group, 2) * tokens, tokens), tokens)
        target = kvs.at[lax.div(group, 2), :, at, :]
        copies.append(pltpu.make_async_copy(block, target, sems.at[len(copies)]))
        copies[-1].start()
    for h in range(heads):
        qs[h] = q[:, h * HD : (h + 1) * HD]
    for copy in copies:
        copy.wait()

    row = lax.broadcasted_iota(jnp.int32, (tokens, wide), 0)
    col = lax.broadcasted_iota(jnp.int32, (tokens, wide), 1)
    for h in range(heads):
        scores = jnp.where(col <= row + late, dot_t(qs[h], kvs[last, 0]), NEG)
        sc[last, h] = scores
        mx[h] = lanes_max(scores[:, HD:], scores[:, :HD])

    @pl.loop(0, last)
    def _(n):
        for h in range(heads):
            scores = dot_t(qs[h], kvs[n, 0])
            sc[n, h] = scores
            mx[h] = lanes_max(scores, mx[h])

    for h in range(heads):
        top = jnp.max(mx[h], axis=-1, keepdims=True) * (SCALE * LOG2E)
        mx[h] = jnp.broadcast_to(top, (tokens, HD))
        ls[h] = jnp.zeros((tokens, HD), jnp.float32)
        acc[h] = jnp.zeros((tokens, HD), jnp.float32)

    @pl.loop(0, last + 1)
    def _(n):
        for h in range(heads):
            top = jnp.concatenate([mx[h]] * (wide // HD), axis=1)
            probs = jnp.exp2(sc[n, h] * (SCALE * LOG2E) - top)
            ls[h] = lanes_sum(probs, ls[h])
            acc[h] += jnp.dot(
                probs.astype(jnp.bfloat16), kvs[n, 1], preferred_element_type=jnp.float32
            )

    for h in range(heads):
        total = jnp.sum(ls[h], axis=-1, keepdims=True)
        out[:, h * HD : (h + 1) * HD] = (acc[h] / total).astype(out.dtype)


def prefill_attention(info, q, kv):
    tokens, cols = q.shape
    heads = cols // HD
    return pl.pallas_call(
        prefill_kernel,
        out_shape=jax.ShapeDtypeStruct(q.shape, jnp.bfloat16),
        in_specs=specs(1, 1, 8),
        out_specs=specs(0, 1)[0],
        scratch_shapes=[
            pltpu.VMEM((heads, tokens, HD), jnp.bfloat16),
            pltpu.VMEM((8, 2, 2 * tokens, HD), jnp.bfloat16),
            pltpu.VMEM((8, heads, tokens, 2 * tokens), jnp.float32),
            pltpu.VMEM((heads, tokens, HD), jnp.float32),
            pltpu.VMEM((heads, tokens, HD), jnp.float32),
            pltpu.VMEM((heads, tokens, HD), jnp.float32),
            pltpu.SemaphoreType.DMA((16,)),
        ],
        compiler_params=params(36),
        cost_estimate=pl.CostEstimate(
            flops=4 * 4096 * tokens * cols, bytes_accessed=3 << 20, transcendentals=4096 * 1024
        ),
        name="prefill_attention",
    )(info, q, *kv)


def mask_kernel(table, lens, bias):
    requests, pages = table.shape
    slots = bias.shape[1] // PAGE // 2
    offset = lax.broadcasted_iota(jnp.int32, (requests, PAGE), 1)
    length = jnp.broadcast_to(lens[...], (requests, PAGE))
    named = []
    for j in range(pages):
        slot = jnp.broadcast_to(table[:, j : j + 1], (requests, PAGE))
        named.append(jnp.where(offset + j * PAGE < length, slot, -1))
    for slot in range(2 * slots):
        count = jnp.zeros((requests, PAGE), jnp.float32)
        for j in range(slot // slots, pages, 2):
            count = count + jnp.where(named[j] == slot, 1.0, 0.0)
        bias[:, slot * PAGE : (slot + 1) * PAGE] = jnp.where(
            count > 0, jnp.log2(jnp.maximum(count, 1.0)), NEG
        )


def cache_mask(table, lens, slots):
    return pl.pallas_call(
        mask_kernel,
        out_shape=jax.ShapeDtypeStruct((table.shape[0], 2 * slots * PAGE), jnp.float32),
        in_specs=specs(0, 2),
        out_specs=specs(0, 1)[0],
        compiler_params=params(16),
        name="cache_mask",
    )(table, lens)


def decode_kernel(info, placement, q, keys, values, bias, mine, other, *refs):
    kv, res, ks, vs, sc, sems = refs[:8], *refs[8:]
    slots = mine.shape[0]
    requests = bias.shape[0]
    steps = q.shape[0] // requests
    heads = q.shape[1] // HD
    lane = info[3]
    pools = []
    for pool, first in ((mine, lane * slots), (other, (1 - lane) * slots)):
        for c, held in enumerate((ks, vs)):
            source, target = pool.at[:, :, c * HD : (c + 1) * HD], held.at[pl.ds(first, slots)]
            pools.append(pltpu.make_async_copy(source, target, sems.at[len(pools)]))
            pools[-1].start()

    for copy in pools:
        copy.wait()
    landings = []
    for block, far, below in placed(kv, info[1]):
        number = 2 * group_at(info, far, below)
        for half in range(2):
            hit, target = placement[number + half, 0] == info[0], placement[number + half, 1]
            pair = []
            for c, held in enumerate((ks, vs)):
                source = block.at[c, half * PAGE : (half + 1) * PAGE, :]
                at = len(pools) + 2 * len(landings) + c
                pair.append(pltpu.make_async_copy(source, held.at[target], sems.at[at]))
            landings.append((hit, pair))
    for hit, pair in landings:

        @pl.when(hit)
        def _():
            for copy in pair:
                copy.start()

    for hit, pair in landings:

        @pl.when(hit)
        def _():
            for copy in pair:
                copy.wait()

    chunk = 8
    width = chunk * PAGE
    for step in range(steps):
        q_rows = q[step * requests : (step + 1) * requests, :]
        stacked = jnp.concatenate([q_rows[:, h * HD : (h + 1) * HD] for h in range(heads)], axis=0)
        wide = stacked.astype(jnp.float32).reshape(heads, requests, HD)
        fresh = []
        for t in range(step + 1):
            key = keys[t * requests : (t + 1) * requests, :].astype(jnp.float32)
            fresh.append(jnp.sum(wide * key[None], axis=-1, keepdims=True) * (SCALE * LOG2E))
        top = fresh[0]
        for score in fresh[1:]:
            top = jnp.maximum(top, score)
        lane_top = jnp.broadcast_to(top, (heads, requests, HD))
        for n in range(2 * slots // chunk):
            k = ks[n * chunk : (n + 1) * chunk].reshape(width, HD)
            scores = dot_t(stacked, k).reshape(heads, requests, width) * (SCALE * LOG2E)
            scores = scores + bias[:, n * width : (n + 1) * width][None]
            sc[n] = scores
            lane_top = lanes_max(scores, lane_top)
        top = jnp.max(lane_top, axis=-1, keepdims=True)
        total = jnp.zeros((heads, requests, 1), jnp.float32)
        weighted = jnp.zeros((heads, requests, HD), jnp.float32)
        for t, score in enumerate(fresh):
            prob = jnp.exp2(score - top)
            value = values[t * requests : (t + 1) * requests, :].astype(jnp.float32)
            total = total + prob
            weighted = weighted + prob * value[None]
        wide_top = jnp.broadcast_to(top, (heads, requests, HD))
        lane_sum = jnp.zeros((heads, requests, HD), jnp.float32)
        for n in range(2 * slots // chunk):
            v = vs[n * chunk : (n + 1) * chunk].reshape(width, HD)
            probs = jnp.exp2(sc[n] - jnp.concatenate([wide_top] * chunk, axis=-1))
            lane_sum = lanes_sum(probs, lane_sum)
            update = jnp.dot(
                probs.reshape(heads * requests, width).astype(jnp.bfloat16),
                v,
                preferred_element_type=jnp.float32,
            )
            weighted = weighted + update.reshape(heads, requests, HD)
        total = total + jnp.sum(lane_sum, axis=-1, keepdims=True)
        result = (weighted / total).astype(res.dtype)
        for h in range(heads):
            res[step * requests : (step + 1) * requests, h * HD : (h + 1) * HD] = result[h]


def decode_attention(info, placement, q, keys, values, bias, mine, other, kv):
    slots = mine.shape[0]
    requests = bias.shape[0]
    cols = q.shape[1]
    return pl.pallas_call(
        decode_kernel,
        out_shape=jax.ShapeDtypeStruct(q.shape, jnp.bfloat16),
        in_specs=specs(2, 4, 10),
        out_specs=specs(0, 1)[0],
        scratch_shapes=[
            pltpu.VMEM((2 * slots, PAGE, HD), jnp.bfloat16),
            pltpu.VMEM((2 * slots, PAGE, HD), jnp.bfloat16),
            pltpu.VMEM((2 * slots // 8, cols // HD, requests, 8 * PAGE), jnp.float32),
            pltpu.SemaphoreType.DMA((68,)),
        ],
        compiler_params=params(32),
        cost_estimate=pl.CostEstimate(
            flops=4 * 768 * 4096 * HD, bytes_accessed=5 << 20, transcendentals=768 * 4096
        ),
        name="decode_attention",
    )(info, placement, q, keys, values, bias, mine, other, *kv)


def output_kernel(info, *refs):
    rows, w, outs, held, sems = refs[:4], refs[4], refs[5:9], refs[9], refs[10]
    width = w.shape[2]
    copies = []
    for n in range(16):
        k, c = n // 4, n % 4
        block = w.at[lax.rem(info[4] + k, 4) * 4 + c]
        copy = pltpu.make_async_copy(
            block, held.at[k, :, c * width : (c + 1) * width], sems.at[n]
        )
        copy.start()
        copies.append(copy)
    wide = jnp.concatenate([row[...] for row in rows], axis=1)
    for k in range(4):
        for c in range(4):
            copies[4 * k + c].wait()
        result = jnp.dot(wide, held[k], preferred_element_type=jnp.float32)
        outs[k][...] = result.astype(outs[k].dtype)


def output_projection(info, rows, w):
    count, depth = rows[0].shape
    cols = 4 * w.shape[2]
    return pl.pallas_call(
        output_kernel,
        out_shape=[jax.ShapeDtypeStruct((count, cols), jnp.bfloat16)] * 4,
        in_specs=specs(1, 4, 1),
        out_specs=specs(0, 4),
        scratch_shapes=[
            pltpu.VMEM((4, 4 * depth, cols), jnp.bfloat16),
            pltpu.SemaphoreType.DMA((16,)),
        ],
        compiler_params=params(50),
        cost_estimate=pl.CostEstimate(
            flops=32 * count * depth * cols, bytes_accessed=10 << 20, transcendentals=0
        ),
        name="output_projection",
    )(info, *rows, w)


def quarter(info, k, width):
    return pl.ds(pl.multiple_of(lax.rem(info[5] + k, 4) * width, width), width)


def sum_kernel(info, *refs):
    parts, outs, held = refs[:4], refs[4:8], refs[8]
    total = parts[0][...].astype(jnp.float32)
    for part in parts[1:]:
        total = total + part[...].astype(jnp.float32)
    held[...] = total
    for k in range(4):
        outs[k][...] = held[:, quarter(info, k, outs[k].shape[1])].astype(outs[k].dtype)


def sum_parts(info, parts):
    rows, cols = parts[0].shape
    return pl.pallas_call(
        sum_kernel,
        out_shape=[jax.ShapeDtypeStruct((rows, cols // 4), jnp.bfloat16)] * 4,
        in_specs=specs(1, 4),
        out_specs=specs(0, 4),
        scratch_shapes=[pltpu.VMEM((rows, cols), jnp.float32)],
        compiler_params=params(16),
        name="sum_parts",
    )(info, *parts)


def assemble_kernel(info, *refs):
    pieces, out = refs[:4], refs[4]
    for k in range(4):
        out[:, quarter(info, 4 - k, pieces[k].shape[1])] = pieces[k][...]


def assemble(info, pieces):
    rows, cols = pieces[0].shape
    return pl.pallas_call(
        assemble_kernel,
        out_shape=jax.ShapeDtypeStruct((rows, 4 * cols), jnp.bfloat16),
        in_specs=specs(1, 4),
        out_specs=specs(0, 1)[0],
        compiler_params=params(16),
        name="assemble",
    )(info, *pieces)


def along(values, dx, dy):
    sent = list(values)
    for k in (2, 1, 3):
        sent[k] = lax.ppermute(values[k], "tp", tp_perm(k * dx, k * dy))
    return sent


def on_device(
    x_prefill, x_decode, w_query, w_keyval, w_out, cache_pool, placement, page_table, cache_len
):
    tokens = x_prefill.shape[0]
    steps, requests, width = x_decode.shape
    section, tp, plane = lax.axis_index("section"), lax.axis_index("tp"), lax.axis_index("dp")
    x, y = lax.div(tp, 4), lax.rem(tp, 4)
    lane = lax.rem(tp, 2)
    group = section * 8 + plane
    info = jnp.stack([group, section, plane, lane, x, y, tp]).astype(jnp.int32)
    turn = jnp.where(section == 0, 1, -1)
    count = jnp.arange(16, dtype=jnp.int32)
    order = lax.rem(x - turn * (count // 4) + 4, 4) * 4 + lax.rem(y - turn * (count % 4) + 4, 4)

    q_cols = w_query.shape[1]
    kv_cols = w_keyval.shape[1]
    w_all = lax.all_gather(jnp.concatenate([w_query, w_keyval], axis=1), SD, axis=0, tiled=False)

    part = w_out.shape[1] // 4
    w_cut = along(
        [lax.dynamic_slice_in_dim(w_out, lax.rem(y + k, 4) * part, part, 1) for k in range(4)], 0, 1
    )
    rows = x_decode.reshape(steps * requests, width)
    half_p, half_d = tokens // 2, rows.shape[0] // 2
    bias = cache_mask(page_table, cache_len[:, None], cache_pool.shape[1])
    blocks, (bias, *w_cut) = gather_tp(
        jnp.concatenate([x_prefill[:half_p], rows[:half_d]], axis=0),
        jnp.concatenate([x_prefill[half_p:], rows[half_d:]], axis=0),
        [bias, *w_cut],
    )
    kv_mine = project_keys(order, blocks, w_all, kv_cols, tokens)
    kv_lane = lax.ppermute(kv_mine, "tp", LANE)
    kv_core = lax.ppermute(kv_mine, "section", SWAP)
    kv_both = lax.ppermute(kv_mine, ST, BOTH)
    mine, w_cut, kv_lane, kv_core, kv_both = lax.optimization_barrier(
        (cache_pool[0], jnp.concatenate(w_cut, axis=0), kv_lane, kv_core, kv_both)
    )
    wo_all = lax.all_gather(w_cut, SD, axis=0, tiled=False)
    is_key = lane == 0
    pair = jnp.stack(
        [
            jnp.stack([jnp.where(is_key, p, q), jnp.where(is_key, q, p)])
            for p, q in ((kv_mine, kv_lane), (kv_core, kv_both))
        ]
    )
    kv, (q_pre, q_dec, new_mine) = gather_planes(pair, project(order, blocks, w_all, q_cols, tokens))
    new_lane = lax.ppermute(new_mine, "tp", LANE)
    other = lax.ppermute(mine, "tp", LANE)
    keys = jnp.where(is_key, new_mine, new_lane)
    values = jnp.where(is_key, new_lane, new_mine)

    attention = decode_attention(
        info, placement, q_dec, keys, values, bias, mine, other, kv
    )
    attended = along([attention] * 4, 0, 1)
    parts = along(output_projection(info, attended, wo_all), 1, 0)
    prefill_out = prefill_attention(info, q_pre, kv)
    prefill_out, *parts = lax.optimization_barrier((prefill_out, *parts))
    pieces = along(sum_parts(info, parts), 0, 1)
    decode_out = assemble(info, pieces).reshape(steps, requests, -1)
    return (prefill_out, decode_out)


def solution(mesh):
    return jax.shard_map(
        on_device,
        mesh=mesh,
        in_specs=(
            P(("section", "dp"), "tp"),
            P(None, ("section", "dp"), "tp"),
            P(("section", "dp"), "tp"),
            P(("section", "dp"), "tp"),
            P("tp", ("section", "dp")),
            P("tp", ("section", "dp"), None, None),
            P(),
            P(("section", "dp"), None),
            P(("section", "dp")),
        ),
        out_specs=(P(("section", "dp"), "tp"), P(None, ("section", "dp"), "tp")),
        check_vma=False,
    )
```

```python
import functools
import math

import jax
import jax.numpy as jnp
from jax import lax
from jax.experimental import pallas as pl
from jax.experimental.pallas import tpu as pltpu
from jax.sharding import PartitionSpec as P

HD = 128
PAGE = 128
NEG = -1e30
SCALE = 1.0 / math.sqrt(HD)
LOG2E = math.log2(math.e)

ST = ("section", "tp")
SD = ("section", "dp")

SWAP = [(0, 1), (1, 0)]
LANE = [(t, t ^ 1) for t in range(16)]
BOTH = [(t, t ^ 17) for t in range(32)]
SPIN = [(s * 8 + z, s * 8 + (z + 1 - 2 * s) % 8) for s in range(2) for z in range(8)]


def tp_perm(dx, dy):
    return [
        (x * 4 + y, (x + dx) % 4 * 4 + (y + dy) % 4) for x in range(4) for y in range(4)
    ]


def ring_perm(dx, dy):
    pairs = []
    for s in range(2):
        d = 1 - 2 * s
        pairs += [(s * 16 + a, s * 16 + b) for a, b in tp_perm(d * dx, d * dy)]
    return pairs


RING_X = ring_perm(1, 0)
RING_Y = ring_perm(0, 1)


def gather_tp(first, second, beside):
    a, b = [first], [second]
    for r in range(1, 4):
        a.append(lax.ppermute(first, ST, ring_perm(0, r)))
        b.append(lax.ppermute(second, ST, ring_perm(r, 0)))
    a, b = [jnp.stack(a)], [jnp.stack(b)]
    for r in range(3):
        a.append(lax.ppermute(a[-1], ST, RING_X))
        b.append(lax.ppermute(b[-1], ST, RING_Y))
        if r == 0:
            a[1], b[1], *beside = lax.optimization_barrier((a[1], b[1], *beside))
    return a + b, beside


def gather_planes(own, other, beside):
    mine, theirs = ([own], [other]), ([], [])
    for r in range(1, 5):
        for e in range(2 if r < 4 else 1):
            mine[e].append(lax.ppermute(mine[e][-1], SD, SPIN))
        if r == 1:
            mine[0][1], mine[1][1], *beside = lax.optimization_barrier(
                (mine[0][1], mine[1][1], *beside)
            )
        for e in range(2 if r < 4 else 1):
            theirs[e].append(lax.ppermute(mine[e][r], "section", SWAP))
    return mine[0] + mine[1] + theirs[0] + theirs[1], beside


PLACES = (
    [(0, r, True) for r in range(5)]
    + [(1, r, True) for r in range(4)]
    + [(1, r, False) for r in range(1, 5)]
    + [(0, r, False) for r in range(1, 4)]
)


def placed(refs, section):
    for ref, (other, r, here) in zip(refs, PLACES):
        up, down = (r, (8 - r) % 8) if here else (8 - r, r)
        yield ref, other, jnp.where(section == 0, up, down)


def group_at(info, other, below):
    section = info[1] if other == 0 else 1 - info[1]
    return section * 8 + lax.rem(info[2] - below + 8, 8)


def specs(smem, vmem, anywhere=0):
    return (
        [pl.BlockSpec(memory_space=pltpu.SMEM)] * smem
        + [pl.BlockSpec(memory_space=pltpu.VMEM)] * vmem
        + [pl.BlockSpec(memory_space=pl.ANY)] * anywhere
    )


def params(mib):
    return pltpu.CompilerParams(vmem_limit_bytes=mib << 20)


def start_copies(w, held, sems, order=None):
    copies = []
    for n in range(16):
        copy = pltpu.make_async_copy(w.at[n if order is None else order[n]], held.at[n], sems.at[n])
        copy.start()
        copies.append(copy)
    return copies


def key_kernel(tokens, order, *refs):
    a, b, w, out, held, sems = refs[:4], refs[4:8], refs[8], *refs[9:]
    depth, cols = held.shape[1:]
    half = tokens // 2
    copies = start_copies(w.at[:, :, w.shape[2] - cols :], held, sems, order)
    total = None
    for i in range(4):
        rows = jnp.concatenate(
            [
                jnp.concatenate([a[i][j, :half, :] for j in range(4)], axis=1),
                jnp.concatenate([b[j][i, :half, :] for j in range(4)], axis=1),
            ],
            axis=0,
        )
        for j in range(4):
            copies[4 * i + j].wait()
        block = held[4 * i : 4 * i + 4].reshape(4 * depth, cols)
        part = jnp.dot(rows, block, preferred_element_type=jnp.float32)
        total = part if total is None else total + part
    out[...] = total.astype(out.dtype)


def project_keys(order, blocks, w, cols, tokens):
    depth = w.shape[1]
    return pl.pallas_call(
        functools.partial(key_kernel, tokens),
        out_shape=jax.ShapeDtypeStruct((tokens, cols), jnp.bfloat16),
        in_specs=specs(1, 8, 1),
        out_specs=specs(0, 1)[0],
        scratch_shapes=[
            pltpu.VMEM((16, depth, cols), jnp.bfloat16),
            pltpu.SemaphoreType.DMA((16,)),
        ],
        compiler_params=params(47),
        cost_estimate=pl.CostEstimate(
            flops=2 * tokens * 16 * depth * cols,
            bytes_accessed=2 * 16 * depth * (tokens + cols),
            transcendentals=0,
        ),
        name="project_keys",
    )(order, *blocks, w)


def project_kernel(tokens, order, *refs):
    a, b, w, pre, dec, kv, held, sems = refs[:4], refs[4:8], refs[8], *refs[9:]
    q_cols = pre.shape[1]
    half, each = tokens // 2, a[0].shape[1]
    late = each - half
    copies = start_copies(w, held, sems, order)
    total, total_kv = None, None
    for n in range(16):
        i, j = n // 4, n % 4
        rows = jnp.concatenate([a[i][j], b[j][i]], axis=0)
        rows_kv = jnp.concatenate([a[i][j, half:, :], b[j][i, half:, :]], axis=0)
        copies[n].wait()
        part = jnp.dot(rows, held[n, :, :q_cols], preferred_element_type=jnp.float32)
        part_kv = jnp.dot(rows_kv, held[n, :, q_cols:], preferred_element_type=jnp.float32)
        total = part if total is None else total + part
        total_kv = part_kv if total_kv is None else total_kv + part_kv
    kv[...] = total_kv.astype(kv.dtype)
    result = total.astype(pre.dtype)
    for first in range(2):
        start = first * each
        pre[first * half : (first + 1) * half, :] = result[start : start + half]
        dec[first * late : (first + 1) * late, :] = result[start + half : start + each]


def project(order, blocks, w, q_cols, tokens):
    rows = 2 * blocks[0].shape[1]
    depth, cols = w.shape[1:]
    return pl.pallas_call(
        functools.partial(project_kernel, tokens),
        out_shape=[
            jax.ShapeDtypeStruct((tokens, q_cols), jnp.bfloat16),
            jax.ShapeDtypeStruct((rows - tokens, q_cols), jnp.bfloat16),
            jax.ShapeDtypeStruct((rows - tokens, cols - q_cols), jnp.bfloat16),
        ],
        in_specs=specs(1, 8, 1),
        out_specs=specs(0, 3),
        scratch_shapes=[
            pltpu.VMEM((16, depth, cols), jnp.bfloat16),
            pltpu.SemaphoreType.DMA((16,)),
        ],
        compiler_params=params(47),
        cost_estimate=pl.CostEstimate(
            flops=2 * rows * 16 * depth * cols,
            bytes_accessed=2 * 16 * depth * (rows + cols),
            transcendentals=0,
        ),
        name="project",
    )(order, *blocks, w)


def dot_t(a, b):
    return lax.dot_general(a, b, (((1,), (1,)), ((), ())), preferred_element_type=jnp.float32)


def lanes_max(value, top):
    for n in range(0, value.shape[-1], HD):
        top = jnp.maximum(top, value[..., n : n + HD])
    return top


def lanes_sum(value, total):
    for n in range(0, value.shape[-1], HD):
        total = total + value[..., n : n + HD]
    return total


def prefill_kernel(info, q, *refs):
    kv, out, qs, kvs, sc, mx, ls, acc, sems = refs[:16], *refs[16:]
    tokens = q.shape[0]
    wide = kvs.shape[2]
    heads = q.shape[1] // HD
    last, late = lax.div(info[0], 2), lax.rem(info[0], 2) * tokens
    copies = []
    for block, other, below in placed(kv, info[1]):
        group = group_at(info, other, below)
        at = pl.ds(pl.multiple_of(lax.rem(group, 2) * tokens, tokens), tokens)
        target = kvs.at[lax.div(group, 2), :, at, :]
        copies.append(pltpu.make_async_copy(block, target, sems.at[len(copies)]))
        copies[-1].start()
    for h in range(heads):
        qs[h] = q[:, h * HD : (h + 1) * HD]
    for copy in copies:
        copy.wait()

    row = lax.broadcasted_iota(jnp.int32, (tokens, wide), 0)
    col = lax.broadcasted_iota(jnp.int32, (tokens, wide), 1)
    for h in range(heads):
        scores = jnp.where(col <= row + late, dot_t(qs[h], kvs[last, 0]), NEG)
        sc[last, h] = scores
        mx[h] = lanes_max(scores[:, HD:], scores[:, :HD])

    @pl.loop(0, last)
    def _(n):
        for h in range(heads):
            scores = dot_t(qs[h], kvs[n, 0])
            sc[n, h] = scores
            mx[h] = lanes_max(scores, mx[h])

    for h in range(heads):
        top = jnp.max(mx[h], axis=-1, keepdims=True) * (SCALE * LOG2E)
        mx[h] = jnp.broadcast_to(top, (tokens, HD))
        ls[h] = jnp.zeros((tokens, HD), jnp.float32)
        acc[h] = jnp.zeros((tokens, HD), jnp.float32)

    @pl.loop(0, last + 1)
    def _(n):
        for h in range(heads):
            top = jnp.concatenate([mx[h]] * (wide // HD), axis=1)
            probs = jnp.exp2(sc[n, h] * (SCALE * LOG2E) - top)
            ls[h] = lanes_sum(probs, ls[h])
            acc[h] += jnp.dot(
                probs.astype(jnp.bfloat16), kvs[n, 1], preferred_element_type=jnp.float32
            )

    for h in range(heads):
        total = jnp.sum(ls[h], axis=-1, keepdims=True)
        out[:, h * HD : (h + 1) * HD] = (acc[h] / total).astype(out.dtype)


def prefill_attention(info, q, kv):
    tokens, cols = q.shape
    heads = cols // HD
    return pl.pallas_call(
        prefill_kernel,
        out_shape=jax.ShapeDtypeStruct(q.shape, jnp.bfloat16),
        in_specs=specs(1, 1, 16),
        out_specs=specs(0, 1)[0],
        scratch_shapes=[
            pltpu.VMEM((heads, tokens, HD), jnp.bfloat16),
            pltpu.VMEM((8, 2, 2 * tokens, HD), jnp.bfloat16),
            pltpu.VMEM((8, heads, tokens, 2 * tokens), jnp.float32),
            pltpu.VMEM((heads, tokens, HD), jnp.float32),
            pltpu.VMEM((heads, tokens, HD), jnp.float32),
            pltpu.VMEM((heads, tokens, HD), jnp.float32),
            pltpu.SemaphoreType.DMA((16,)),
        ],
        compiler_params=params(36),
        cost_estimate=pl.CostEstimate(
            flops=4 * 4096 * tokens * cols, bytes_accessed=3 << 20, transcendentals=4096 * 1024
        ),
        name="prefill_attention",
    )(info, q, *kv)


def mask_kernel(table, lens, bias):
    requests, pages = table.shape
    slots = bias.shape[1] // PAGE // 2
    offset = lax.broadcasted_iota(jnp.int32, (requests, PAGE), 1)
    length = jnp.broadcast_to(lens[...], (requests, PAGE))
    named = []
    for j in range(pages):
        slot = jnp.broadcast_to(table[:, j : j + 1], (requests, PAGE))
        named.append(jnp.where(offset + j * PAGE < length, slot, -1))
    for slot in range(2 * slots):
        count = jnp.zeros((requests, PAGE), jnp.float32)
        for j in range(slot // slots, pages, 2):
            count = count + jnp.where(named[j] == slot, 1.0, 0.0)
        bias[:, slot * PAGE : (slot + 1) * PAGE] = jnp.where(
            count > 0, jnp.log2(jnp.maximum(count, 1.0)), NEG
        )


def cache_mask(table, lens, slots):
    return pl.pallas_call(
        mask_kernel,
        out_shape=jax.ShapeDtypeStruct((table.shape[0], 2 * slots * PAGE), jnp.float32),
        in_specs=specs(0, 2),
        out_specs=specs(0, 1)[0],
        compiler_params=params(16),
        name="cache_mask",
    )(table, lens)


def decode_kernel(info, placement, q, keys, values, bias, mine, other, *refs):
    kv, res, ks, vs, sc, sems = refs[:16], *refs[16:]
    slots = mine.shape[0]
    requests = bias.shape[0]
    steps = q.shape[0] // requests
    heads = q.shape[1] // HD
    lane = info[3]
    pools = []
    for pool, first in ((mine, lane * slots), (other, (1 - lane) * slots)):
        for c, held in enumerate((ks, vs)):
            source, target = pool.at[:, :, c * HD : (c + 1) * HD], held.at[pl.ds(first, slots)]
            pools.append(pltpu.make_async_copy(source, target, sems.at[len(pools)]))
            pools[-1].start()

    for copy in pools:
        copy.wait()
    landings = []
    for block, far, below in placed(kv, info[1]):
        number = 2 * group_at(info, far, below)
        for half in range(2):
            hit, target = placement[number + half, 0] == info[0], placement[number + half, 1]
            pair = []
            for c, held in enumerate((ks, vs)):
                source = block.at[c, half * PAGE : (half + 1) * PAGE, :]
                at = len(pools) + 2 * len(landings) + c
                pair.append(pltpu.make_async_copy(source, held.at[target], sems.at[at]))
            landings.append((hit, pair))
    for hit, pair in landings:

        @pl.when(hit)
        def _():
            for copy in pair:
                copy.start()

    for hit, pair in landings:

        @pl.when(hit)
        def _():
            for copy in pair:
                copy.wait()

    chunk = 8
    width = chunk * PAGE
    for step in range(steps):
        q_rows = q[step * requests : (step + 1) * requests, :]
        stacked = jnp.concatenate([q_rows[:, h * HD : (h + 1) * HD] for h in range(heads)], axis=0)
        wide = stacked.astype(jnp.float32).reshape(heads, requests, HD)
        fresh = []
        for t in range(step + 1):
            key = keys[t * requests : (t + 1) * requests, :].astype(jnp.float32)
            fresh.append(jnp.sum(wide * key[None], axis=-1, keepdims=True) * (SCALE * LOG2E))
        top = fresh[0]
        for score in fresh[1:]:
            top = jnp.maximum(top, score)
        lane_top = jnp.broadcast_to(top, (heads, requests, HD))
        for n in range(2 * slots // chunk):
            k = ks[n * chunk : (n + 1) * chunk].reshape(width, HD)
            scores = dot_t(stacked, k).reshape(heads, requests, width) * (SCALE * LOG2E)
            scores = scores + bias[:, n * width : (n + 1) * width][None]
            sc[n] = scores
            lane_top = lanes_max(scores, lane_top)
        top = jnp.max(lane_top, axis=-1, keepdims=True)
        total = jnp.zeros((heads, requests, 1), jnp.float32)
        weighted = jnp.zeros((heads, requests, HD), jnp.float32)
        for t, score in enumerate(fresh):
            prob = jnp.exp2(score - top)
            value = values[t * requests : (t + 1) * requests, :].astype(jnp.float32)
            total = total + prob
            weighted = weighted + prob * value[None]
        wide_top = jnp.broadcast_to(top, (heads, requests, HD))
        lane_sum = jnp.zeros((heads, requests, HD), jnp.float32)
        for n in range(2 * slots // chunk):
            v = vs[n * chunk : (n + 1) * chunk].reshape(width, HD)
            probs = jnp.exp2(sc[n] - jnp.concatenate([wide_top] * chunk, axis=-1))
            lane_sum = lanes_sum(probs, lane_sum)
            update = jnp.dot(
                probs.reshape(heads * requests, width).astype(jnp.bfloat16),
                v,
                preferred_element_type=jnp.float32,
            )
            weighted = weighted + update.reshape(heads, requests, HD)
        total = total + jnp.sum(lane_sum, axis=-1, keepdims=True)
        result = (weighted / total).astype(res.dtype)
        for h in range(heads):
            res[step * requests : (step + 1) * requests, h * HD : (h + 1) * HD] = result[h]


def decode_attention(info, placement, q, keys, values, bias, mine, other, kv):
    slots = mine.shape[0]
    requests = bias.shape[0]
    cols = q.shape[1]
    return pl.pallas_call(
        decode_kernel,
        out_shape=jax.ShapeDtypeStruct(q.shape, jnp.bfloat16),
        in_specs=specs(2, 4, 18),
        out_specs=specs(0, 1)[0],
        scratch_shapes=[
            pltpu.VMEM((2 * slots, PAGE, HD), jnp.bfloat16),
            pltpu.VMEM((2 * slots, PAGE, HD), jnp.bfloat16),
            pltpu.VMEM((2 * slots // 8, cols // HD, requests, 8 * PAGE), jnp.float32),
            pltpu.SemaphoreType.DMA((68,)),
        ],
        compiler_params=params(32),
        cost_estimate=pl.CostEstimate(
            flops=4 * 768 * 4096 * HD, bytes_accessed=5 << 20, transcendentals=768 * 4096
        ),
        name="decode_attention",
    )(info, placement, q, keys, values, bias, mine, other, *kv)


def output_kernel(info, *refs):
    rows, w, outs, held, sems = refs[:4], refs[4], refs[5:9], refs[9], refs[10]
    width = w.shape[2]
    copies = []
    for n in range(16):
        k, c = n // 4, n % 4
        block = w.at[lax.rem(info[4] + k, 4) * 4 + c]
        copy = pltpu.make_async_copy(
            block, held.at[k, :, c * width : (c + 1) * width], sems.at[n]
        )
        copy.start()
        copies.append(copy)
    wide = jnp.concatenate([row[...] for row in rows], axis=1)
    for k in range(4):
        for c in range(4):
            copies[4 * k + c].wait()
        result = jnp.dot(wide, held[k], preferred_element_type=jnp.float32)
        outs[k][...] = result.astype(outs[k].dtype)


def output_projection(info, rows, w):
    count, depth = rows[0].shape
    cols = 4 * w.shape[2]
    return pl.pallas_call(
        output_kernel,
        out_shape=[jax.ShapeDtypeStruct((count, cols), jnp.bfloat16)] * 4,
        in_specs=specs(1, 4, 1),
        out_specs=specs(0, 4),
        scratch_shapes=[
            pltpu.VMEM((4, 4 * depth, cols), jnp.bfloat16),
            pltpu.SemaphoreType.DMA((16,)),
        ],
        compiler_params=params(50),
        cost_estimate=pl.CostEstimate(
            flops=32 * count * depth * cols, bytes_accessed=10 << 20, transcendentals=0
        ),
        name="output_projection",
    )(info, *rows, w)


def quarter(info, k, width):
    return pl.ds(pl.multiple_of(lax.rem(info[5] + k, 4) * width, width), width)


def sum_kernel(info, *refs):
    parts, outs, held = refs[:4], refs[4:8], refs[8]
    total = parts[0][...].astype(jnp.float32)
    for part in parts[1:]:
        total = total + part[...].astype(jnp.float32)
    held[...] = total
    for k in range(4):
        outs[k][...] = held[:, quarter(info, k, outs[k].shape[1])].astype(outs[k].dtype)


def sum_parts(info, parts):
    rows, cols = parts[0].shape
    return pl.pallas_call(
        sum_kernel,
        out_shape=[jax.ShapeDtypeStruct((rows, cols // 4), jnp.bfloat16)] * 4,
        in_specs=specs(1, 4),
        out_specs=specs(0, 4),
        scratch_shapes=[pltpu.VMEM((rows, cols), jnp.float32)],
        compiler_params=params(16),
        name="sum_parts",
    )(info, *parts)


def assemble_kernel(info, *refs):
    pieces, out = refs[:4], refs[4]
    for k in range(4):
        out[:, quarter(info, 4 - k, pieces[k].shape[1])] = pieces[k][...]


def assemble(info, pieces):
    rows, cols = pieces[0].shape
    return pl.pallas_call(
        assemble_kernel,
        out_shape=jax.ShapeDtypeStruct((rows, 4 * cols), jnp.bfloat16),
        in_specs=specs(1, 4),
        out_specs=specs(0, 1)[0],
        compiler_params=params(16),
        name="assemble",
    )(info, *pieces)


def along(values, dx, dy):
    sent = list(values)
    for k in (2, 1, 3):
        sent[k] = lax.ppermute(values[k], "tp", tp_perm(k * dx, k * dy))
    return sent


def on_device(
    x_prefill, x_decode, w_query, w_keyval, w_out, cache_pool, placement, page_table, cache_len
):
    tokens = x_prefill.shape[0]
    steps, requests, width = x_decode.shape
    section, tp, plane = lax.axis_index("section"), lax.axis_index("tp"), lax.axis_index("dp")
    x, y = lax.div(tp, 4), lax.rem(tp, 4)
    lane = lax.rem(tp, 2)
    group = section * 8 + plane
    info = jnp.stack([group, section, plane, lane, x, y, tp]).astype(jnp.int32)
    turn = jnp.where(section == 0, 1, -1)
    count = jnp.arange(16, dtype=jnp.int32)
    order = lax.rem(x - turn * (count // 4) + 4, 4) * 4 + lax.rem(y - turn * (count % 4) + 4, 4)

    q_cols = w_query.shape[1]
    kv_cols = w_keyval.shape[1]
    w_all = lax.all_gather(jnp.concatenate([w_query, w_keyval], axis=1), SD, axis=0, tiled=False)

    part = w_out.shape[1] // 4
    w_cut = along(
        [lax.dynamic_slice_in_dim(w_out, lax.rem(y + k, 4) * part, part, 1) for k in range(4)], 0, 1
    )
    rows = x_decode.reshape(steps * requests, width)
    half_p, half_d = tokens // 2, rows.shape[0] // 2
    bias = cache_mask(page_table, cache_len[:, None], cache_pool.shape[1])
    blocks, (bias, *w_cut) = gather_tp(
        jnp.concatenate([x_prefill[:half_p], rows[:half_d]], axis=0),
        jnp.concatenate([x_prefill[half_p:], rows[half_d:]], axis=0),
        [bias, *w_cut],
    )
    wo_all = lax.all_gather(jnp.concatenate(w_cut, axis=0), SD, axis=0, tiled=False)
    kv_mine = project_keys(order, blocks, w_all, kv_cols, tokens)
    kv_lane = lax.ppermute(kv_mine, "tp", LANE)
    kv_core = lax.ppermute(kv_mine, "section", SWAP)
    kv_both = lax.ppermute(kv_mine, ST, BOTH)
    mine, kv_lane = lax.optimization_barrier((cache_pool[0], kv_lane))
    is_key = lane == 0
    own, other_core = (
        jnp.stack([jnp.where(is_key, p, q), jnp.where(is_key, q, p)])
        for p, q in ((kv_mine, kv_lane), (kv_core, kv_both))
    )
    kv, (q_pre, q_dec, new_mine) = gather_planes(
        own, other_core, project(order, blocks, w_all, q_cols, tokens)
    )
    new_lane = lax.ppermute(new_mine, "tp", LANE)
    other = lax.ppermute(mine, "tp", LANE)
    keys = jnp.where(is_key, new_mine, new_lane)
    values = jnp.where(is_key, new_lane, new_mine)

    attention = decode_attention(
        info, placement, q_dec, keys, values, bias, mine, other, kv
    )
    attended = along([attention] * 4, 0, 1)
    parts = along(output_projection(info, attended, wo_all), 1, 0)
    prefill_out = prefill_attention(info, q_pre, kv)
    prefill_out, *parts = lax.optimization_barrier((prefill_out, *parts))
    pieces = along(sum_parts(info, parts), 0, 1)
    decode_out = assemble(info, pieces).reshape(steps, requests, -1)
    return (prefill_out, decode_out)


def solution(mesh):
    return jax.shard_map(
        on_device,
        mesh=mesh,
        in_specs=(
            P(("section", "dp"), "tp"),
            P(None, ("section", "dp"), "tp"),
            P(("section", "dp"), "tp"),
            P(("section", "dp"), "tp"),
            P("tp", ("section", "dp")),
            P("tp", ("section", "dp"), None, None),
            P(),
            P(("section", "dp"), None),
            P(("section", "dp")),
        ),
        out_specs=(P(("section", "dp"), "tp"), P(None, ("section", "dp"), "tp")),
        check_vma=False,
    )
```

```python
import functools
import math

import jax
import jax.numpy as jnp
from jax import lax
from jax.experimental import pallas as pl
from jax.experimental.pallas import tpu as pltpu
from jax.sharding import PartitionSpec as P

HD = 128
PAGE = 128
NEG = -1e30
SCALE = 1.0 / math.sqrt(HD)
LOG2E = math.log2(math.e)

ST = ("section", "tp")
SD = ("section", "dp")

SWAP = [(0, 1), (1, 0)]
LANE = [(t, t ^ 1) for t in range(16)]
BOTH = [(t, t ^ 17) for t in range(32)]
SPIN = [(s * 8 + z, s * 8 + (z + 1 - 2 * s) % 8) for s in range(2) for z in range(8)]


def tp_perm(dx, dy):
    return [
        (x * 4 + y, (x + dx) % 4 * 4 + (y + dy) % 4) for x in range(4) for y in range(4)
    ]


def ring_perm(dx, dy):
    pairs = []
    for s in range(2):
        d = 1 - 2 * s
        pairs += [(s * 16 + a, s * 16 + b) for a, b in tp_perm(d * dx, d * dy)]
    return pairs


RING_X = ring_perm(1, 0)
RING_Y = ring_perm(0, 1)


def gather_tp(first, second, beside):
    a, b = [first], [second]
    for r in range(1, 4):
        a.append(lax.ppermute(first, ST, ring_perm(0, r)))
        b.append(lax.ppermute(second, ST, ring_perm(r, 0)))
    a, b = [jnp.stack(a)], [jnp.stack(b)]
    for r in range(3):
        a.append(lax.ppermute(a[-1], ST, RING_X))
        b.append(lax.ppermute(b[-1], ST, RING_Y))
        if r == 0:
            a[1], b[1], *beside = lax.optimization_barrier((a[1], b[1], *beside))
    return a + b, beside


def gather_planes(own, other, beside):
    mine, theirs = ([own], [other]), ([], [])
    for r in range(1, 5):
        for e in range(2 if r < 4 else 1):
            mine[e].append(lax.ppermute(mine[e][-1], SD, SPIN))
        if r == 1:
            mine[0][1], mine[1][1], *beside = lax.optimization_barrier(
                (mine[0][1], mine[1][1], *beside)
            )
        for e in range(2 if r < 4 else 1):
            theirs[e].append(lax.ppermute(mine[e][r], "section", SWAP))
    return mine[0] + mine[1] + theirs[0] + theirs[1], beside


PLACES = (
    [(0, r, True) for r in range(5)]
    + [(1, r, True) for r in range(4)]
    + [(1, r, False) for r in range(1, 5)]
    + [(0, r, False) for r in range(1, 4)]
)


def placed(refs, section):
    for ref, (other, r, here) in zip(refs, PLACES):
        up, down = (r, (8 - r) % 8) if here else (8 - r, r)
        yield ref, other, jnp.where(section == 0, up, down)


def group_at(info, other, below):
    section = info[1] if other == 0 else 1 - info[1]
    return section * 8 + lax.rem(info[2] - below + 8, 8)


def specs(smem, vmem, anywhere=0):
    return (
        [pl.BlockSpec(memory_space=pltpu.SMEM)] * smem
        + [pl.BlockSpec(memory_space=pltpu.VMEM)] * vmem
        + [pl.BlockSpec(memory_space=pl.ANY)] * anywhere
    )


def params(mib):
    return pltpu.CompilerParams(vmem_limit_bytes=mib << 20)


def start_copies(w, held, sems, order=None):
    copies = []
    for n in range(16):
        copy = pltpu.make_async_copy(w.at[n if order is None else order[n]], held.at[n], sems.at[n])
        copy.start()
        copies.append(copy)
    return copies


def key_kernel(tokens, order, *refs):
    a, b, w, out, held, sems = refs[:4], refs[4:8], refs[8], *refs[9:]
    depth, cols = held.shape[1:]
    half = tokens // 2
    copies = start_copies(w.at[:, :, w.shape[2] - cols :], held, sems, order)
    total = None
    for i in range(4):
        rows = jnp.concatenate(
            [
                jnp.concatenate([a[i][j, :half, :] for j in range(4)], axis=1),
                jnp.concatenate([b[j][i, :half, :] for j in range(4)], axis=1),
            ],
            axis=0,
        )
        for j in range(4):
            copies[4 * i + j].wait()
        block = held[4 * i : 4 * i + 4].reshape(4 * depth, cols)
        part = jnp.dot(rows, block, preferred_element_type=jnp.float32)
        total = part if total is None else total + part
    out[...] = total.astype(out.dtype)


def project_keys(order, blocks, w, cols, tokens):
    depth = w.shape[1]
    return pl.pallas_call(
        functools.partial(key_kernel, tokens),
        out_shape=jax.ShapeDtypeStruct((tokens, cols), jnp.bfloat16),
        in_specs=specs(1, 8, 1),
        out_specs=specs(0, 1)[0],
        scratch_shapes=[
            pltpu.VMEM((16, depth, cols), jnp.bfloat16),
            pltpu.SemaphoreType.DMA((16,)),
        ],
        compiler_params=params(47),
        cost_estimate=pl.CostEstimate(
            flops=2 * tokens * 16 * depth * cols,
            bytes_accessed=2 * 16 * depth * (tokens + cols),
            transcendentals=0,
        ),
        name="project_keys",
    )(order, *blocks, w)


def project_kernel(tokens, order, *refs):
    a, b, w, pre, dec, kv, held, sems = refs[:4], refs[4:8], refs[8], *refs[9:]
    q_cols = pre.shape[1]
    half, each = tokens // 2, a[0].shape[1]
    late = each - half
    copies = start_copies(w, held, sems, order)
    total, total_kv = None, None
    for n in range(16):
        i, j = n // 4, n % 4
        rows = jnp.concatenate([a[i][j], b[j][i]], axis=0)
        rows_kv = jnp.concatenate([a[i][j, half:, :], b[j][i, half:, :]], axis=0)
        copies[n].wait()
        part = jnp.dot(rows, held[n, :, :q_cols], preferred_element_type=jnp.float32)
        part_kv = jnp.dot(rows_kv, held[n, :, q_cols:], preferred_element_type=jnp.float32)
        total = part if total is None else total + part
        total_kv = part_kv if total_kv is None else total_kv + part_kv
    kv[...] = total_kv.astype(kv.dtype)
    result = total.astype(pre.dtype)
    for first in range(2):
        start = first * each
        pre[first * half : (first + 1) * half, :] = result[start : start + half]
        dec[first * late : (first + 1) * late, :] = result[start + half : start + each]


def project(order, blocks, w, q_cols, tokens):
    rows = 2 * blocks[0].shape[1]
    depth, cols = w.shape[1:]
    return pl.pallas_call(
        functools.partial(project_kernel, tokens),
        out_shape=[
            jax.ShapeDtypeStruct((tokens, q_cols), jnp.bfloat16),
            jax.ShapeDtypeStruct((rows - tokens, q_cols), jnp.bfloat16),
            jax.ShapeDtypeStruct((rows - tokens, cols - q_cols), jnp.bfloat16),
        ],
        in_specs=specs(1, 8, 1),
        out_specs=specs(0, 3),
        scratch_shapes=[
            pltpu.VMEM((16, depth, cols), jnp.bfloat16),
            pltpu.SemaphoreType.DMA((16,)),
        ],
        compiler_params=params(47),
        cost_estimate=pl.CostEstimate(
            flops=2 * rows * 16 * depth * cols,
            bytes_accessed=2 * 16 * depth * (rows + cols),
            transcendentals=0,
        ),
        name="project",
    )(order, *blocks, w)


def dot_t(a, b):
    return lax.dot_general(a, b, (((1,), (1,)), ((), ())), preferred_element_type=jnp.float32)


def lanes_max(value, top):
    for n in range(0, value.shape[-1], HD):
        top = jnp.maximum(top, value[..., n : n + HD])
    return top


def lanes_sum(value, total):
    for n in range(0, value.shape[-1], HD):
        total = total + value[..., n : n + HD]
    return total


def collect_kernel(info, *refs):
    kv, out, sems = refs[:16], refs[16], refs[17]
    tokens = out.shape[2] // 2
    copies = []
    for block, other, below in placed(kv, info[1]):
        group = group_at(info, other, below)
        at = pl.ds(pl.multiple_of(lax.rem(group, 2) * tokens, tokens), tokens)
        target = out.at[lax.div(group, 2), :, at, :]
        copies.append(pltpu.make_async_copy(block, target, sems.at[len(copies)]))
        copies[-1].start()
    for copy in copies:
        copy.wait()


def collect(info, kv):
    _, tokens, cols = kv[0].shape
    return pl.pallas_call(
        collect_kernel,
        out_shape=jax.ShapeDtypeStruct((8, 2, 2 * tokens, cols), jnp.bfloat16),
        in_specs=specs(1, 0, 16),
        out_specs=specs(0, 1)[0],
        scratch_shapes=[pltpu.SemaphoreType.DMA((16,))],
        compiler_params=params(16),
        name="collect",
    )(info, *kv)


def prefill_kernel(info, q, kvs, out, qs, sc, mx, ls, acc):
    tokens = q.shape[0]
    wide = kvs.shape[2]
    heads = q.shape[1] // HD
    last, late = lax.div(info[0], 2), lax.rem(info[0], 2) * tokens
    for h in range(heads):
        qs[h] = q[:, h * HD : (h + 1) * HD]

    row = lax.broadcasted_iota(jnp.int32, (tokens, wide), 0)
    col = lax.broadcasted_iota(jnp.int32, (tokens, wide), 1)
    for h in range(heads):
        scores = jnp.where(col <= row + late, dot_t(qs[h], kvs[last, 0]), NEG)
        sc[last, h] = scores
        mx[h] = lanes_max(scores[:, HD:], scores[:, :HD])

    @pl.loop(0, last)
    def _(n):
        for h in range(heads):
            scores = dot_t(qs[h], kvs[n, 0])
            sc[n, h] = scores
            mx[h] = lanes_max(scores, mx[h])

    for h in range(heads):
        top = jnp.max(mx[h], axis=-1, keepdims=True) * (SCALE * LOG2E)
        mx[h] = jnp.broadcast_to(top, (tokens, HD))
        ls[h] = jnp.zeros((tokens, HD), jnp.float32)
        acc[h] = jnp.zeros((tokens, HD), jnp.float32)

    @pl.loop(0, last + 1)
    def _(n):
        for h in range(heads):
            top = jnp.concatenate([mx[h]] * (wide // HD), axis=1)
            probs = jnp.exp2(sc[n, h] * (SCALE * LOG2E) - top)
            ls[h] = lanes_sum(probs, ls[h])
            acc[h] += jnp.dot(
                probs.astype(jnp.bfloat16), kvs[n, 1], preferred_element_type=jnp.float32
            )

    for h in range(heads):
        total = jnp.sum(ls[h], axis=-1, keepdims=True)
        out[:, h * HD : (h + 1) * HD] = (acc[h] / total).astype(out.dtype)


def prefill_attention(info, q, kvs):
    tokens, cols = q.shape
    heads = cols // HD
    return pl.pallas_call(
        prefill_kernel,
        out_shape=jax.ShapeDtypeStruct(q.shape, jnp.bfloat16),
        in_specs=specs(1, 2),
        out_specs=specs(0, 1)[0],
        scratch_shapes=[
            pltpu.VMEM((heads, tokens, HD), jnp.bfloat16),
            pltpu.VMEM((8, heads, tokens, 2 * tokens), jnp.float32),
            pltpu.VMEM((heads, tokens, HD), jnp.float32),
            pltpu.VMEM((heads, tokens, HD), jnp.float32),
            pltpu.VMEM((heads, tokens, HD), jnp.float32),
        ],
        compiler_params=params(36),
        cost_estimate=pl.CostEstimate(
            flops=4 * 4096 * tokens * cols, bytes_accessed=3 << 20, transcendentals=4096 * 1024
        ),
        name="prefill_attention",
    )(info, q, kvs)


def mask_kernel(table, lens, bias):
    requests, pages = table.shape
    slots = bias.shape[1] // PAGE // 2
    offset = lax.broadcasted_iota(jnp.int32, (requests, PAGE), 1)
    length = jnp.broadcast_to(lens[...], (requests, PAGE))
    named = []
    for j in range(pages):
        slot = jnp.broadcast_to(table[:, j : j + 1], (requests, PAGE))
        named.append(jnp.where(offset + j * PAGE < length, slot, -1))
    for slot in range(2 * slots):
        count = jnp.zeros((requests, PAGE), jnp.float32)
        for j in range(slot // slots, pages, 2):
            count = count + jnp.where(named[j] == slot, 1.0, 0.0)
        bias[:, slot * PAGE : (slot + 1) * PAGE] = jnp.where(
            count > 0, jnp.log2(jnp.maximum(count, 1.0)), NEG
        )


def cache_mask(table, lens, slots):
    return pl.pallas_call(
        mask_kernel,
        out_shape=jax.ShapeDtypeStruct((table.shape[0], 2 * slots * PAGE), jnp.float32),
        in_specs=specs(0, 2),
        out_specs=specs(0, 1)[0],
        compiler_params=params(16),
        name="cache_mask",
    )(table, lens)


def decode_kernel(info, placement, q, keys, values, bias, mine, other, kvs, res, ks, vs, sc, sems):
    slots = mine.shape[0]
    requests = bias.shape[0]
    steps = q.shape[0] // requests
    heads = q.shape[1] // HD
    lane = info[3]
    pools = []
    for pool, first in ((mine, lane * slots), (other, (1 - lane) * slots)):
        for c, held in enumerate((ks, vs)):
            source, target = pool.at[:, :, c * HD : (c + 1) * HD], held.at[pl.ds(first, slots)]
            pools.append(pltpu.make_async_copy(source, target, sems.at[len(pools)]))
            pools[-1].start()

    for copy in pools:
        copy.wait()
    landings = []
    each = kvs.shape[2] // PAGE
    for number in range(placement.shape[0]):
        hit, target = placement[number, 0] == info[0], placement[number, 1]
        row, start = number // each, number % each * PAGE
        pair = []
        for c, held in enumerate((ks, vs)):
            source = kvs.at[row, c, start : start + PAGE, :]
            at = len(pools) + 2 * number + c
            pair.append(pltpu.make_async_copy(source, held.at[target], sems.at[at]))
        landings.append((hit, pair))
    for hit, pair in landings:

        @pl.when(hit)
        def _():
            for copy in pair:
                copy.start()

    for hit, pair in landings:

        @pl.when(hit)
        def _():
            for copy in pair:
                copy.wait()

    chunk = 8
    width = chunk * PAGE
    for step in range(steps):
        q_rows = q[step * requests : (step + 1) * requests, :]
        stacked = jnp.concatenate([q_rows[:, h * HD : (h + 1) * HD] for h in range(heads)], axis=0)
        wide = stacked.astype(jnp.float32).reshape(heads, requests, HD)
        fresh = []
        for t in range(step + 1):
            key = keys[t * requests : (t + 1) * requests, :].astype(jnp.float32)
            fresh.append(jnp.sum(wide * key[None], axis=-1, keepdims=True) * (SCALE * LOG2E))
        top = fresh[0]
        for score in fresh[1:]:
            top = jnp.maximum(top, score)
        lane_top = jnp.broadcast_to(top, (heads, requests, HD))
        for n in range(2 * slots // chunk):
            k = ks[n * chunk : (n + 1) * chunk].reshape(width, HD)
            scores = dot_t(stacked, k).reshape(heads, requests, width) * (SCALE * LOG2E)
            scores = scores + bias[:, n * width : (n + 1) * width][None]
            sc[n] = scores
            lane_top = lanes_max(scores, lane_top)
        top = jnp.max(lane_top, axis=-1, keepdims=True)
        total = jnp.zeros((heads, requests, 1), jnp.float32)
        weighted = jnp.zeros((heads, requests, HD), jnp.float32)
        for t, score in enumerate(fresh):
            prob = jnp.exp2(score - top)
            value = values[t * requests : (t + 1) * requests, :].astype(jnp.float32)
            total = total + prob
            weighted = weighted + prob * value[None]
        wide_top = jnp.broadcast_to(top, (heads, requests, HD))
        lane_sum = jnp.zeros((heads, requests, HD), jnp.float32)
        for n in range(2 * slots // chunk):
            v = vs[n * chunk : (n + 1) * chunk].reshape(width, HD)
            probs = jnp.exp2(sc[n] - jnp.concatenate([wide_top] * chunk, axis=-1))
            lane_sum = lanes_sum(probs, lane_sum)
            update = jnp.dot(
                probs.reshape(heads * requests, width).astype(jnp.bfloat16),
                v,
                preferred_element_type=jnp.float32,
            )
            weighted = weighted + update.reshape(heads, requests, HD)
        total = total + jnp.sum(lane_sum, axis=-1, keepdims=True)
        result = (weighted / total).astype(res.dtype)
        for h in range(heads):
            res[step * requests : (step + 1) * requests, h * HD : (h + 1) * HD] = result[h]


def decode_attention(info, placement, q, keys, values, bias, mine, other, kvs):
    slots = mine.shape[0]
    requests = bias.shape[0]
    cols = q.shape[1]
    return pl.pallas_call(
        decode_kernel,
        out_shape=jax.ShapeDtypeStruct(q.shape, jnp.bfloat16),
        in_specs=specs(2, 4, 3),
        out_specs=specs(0, 1)[0],
        scratch_shapes=[
            pltpu.VMEM((2 * slots, PAGE, HD), jnp.bfloat16),
            pltpu.VMEM((2 * slots, PAGE, HD), jnp.bfloat16),
            pltpu.VMEM((2 * slots // 8, cols // HD, requests, 8 * PAGE), jnp.float32),
            pltpu.SemaphoreType.DMA((68,)),
        ],
        compiler_params=params(32),
        cost_estimate=pl.CostEstimate(
            flops=4 * 768 * 4096 * HD, bytes_accessed=5 << 20, transcendentals=768 * 4096
        ),
        name="decode_attention",
    )(info, placement, q, keys, values, bias, mine, other, kvs)


def output_kernel(info, *refs):
    rows, w, outs, held, sems = refs[:4], refs[4], refs[5:9], refs[9], refs[10]
    width = w.shape[2]
    copies = []
    for n in range(16):
        k, c = n // 4, n % 4
        block = w.at[lax.rem(info[4] + k, 4) * 4 + c]
        copy = pltpu.make_async_copy(
            block, held.at[k, :, c * width : (c + 1) * width], sems.at[n]
        )
        copy.start()
        copies.append(copy)
    wide = jnp.concatenate([row[...] for row in rows], axis=1)
    for k in range(4):
        for c in range(4):
            copies[4 * k + c].wait()
        result = jnp.dot(wide, held[k], preferred_element_type=jnp.float32)
        outs[k][...] = result.astype(outs[k].dtype)


def output_projection(info, rows, w):
    count, depth = rows[0].shape
    cols = 4 * w.shape[2]
    return pl.pallas_call(
        output_kernel,
        out_shape=[jax.ShapeDtypeStruct((count, cols), jnp.bfloat16)] * 4,
        in_specs=specs(1, 4, 1),
        out_specs=specs(0, 4),
        scratch_shapes=[
            pltpu.VMEM((4, 4 * depth, cols), jnp.bfloat16),
            pltpu.SemaphoreType.DMA((16,)),
        ],
        compiler_params=params(50),
        cost_estimate=pl.CostEstimate(
            flops=32 * count * depth * cols, bytes_accessed=10 << 20, transcendentals=0
        ),
        name="output_projection",
    )(info, *rows, w)


def quarter(info, k, width):
    return pl.ds(pl.multiple_of(lax.rem(info[5] + k, 4) * width, width), width)


def sum_kernel(info, *refs):
    parts, outs, held = refs[:4], refs[4:8], refs[8]
    total = parts[0][...].astype(jnp.float32)
    for part in parts[1:]:
        total = total + part[...].astype(jnp.float32)
    held[...] = total
    for k in range(4):
        outs[k][...] = held[:, quarter(info, k, outs[k].shape[1])].astype(outs[k].dtype)


def sum_parts(info, parts):
    rows, cols = parts[0].shape
    return pl.pallas_call(
        sum_kernel,
        out_shape=[jax.ShapeDtypeStruct((rows, cols // 4), jnp.bfloat16)] * 4,
        in_specs=specs(1, 4),
        out_specs=specs(0, 4),
        scratch_shapes=[pltpu.VMEM((rows, cols), jnp.float32)],
        compiler_params=params(16),
        name="sum_parts",
    )(info, *parts)


def assemble_kernel(info, *refs):
    pieces, out = refs[:4], refs[4]
    for k in range(4):
        out[:, quarter(info, 4 - k, pieces[k].shape[1])] = pieces[k][...]


def assemble(info, pieces):
    rows, cols = pieces[0].shape
    return pl.pallas_call(
        assemble_kernel,
        out_shape=jax.ShapeDtypeStruct((rows, 4 * cols), jnp.bfloat16),
        in_specs=specs(1, 4),
        out_specs=specs(0, 1)[0],
        compiler_params=params(16),
        name="assemble",
    )(info, *pieces)


def along(values, dx, dy):
    sent = list(values)
    for k in (2, 1, 3):
        sent[k] = lax.ppermute(values[k], "tp", tp_perm(k * dx, k * dy))
    return sent


def on_device(
    x_prefill, x_decode, w_query, w_keyval, w_out, cache_pool, placement, page_table, cache_len
):
    tokens = x_prefill.shape[0]
    steps, requests, width = x_decode.shape
    section, tp, plane = lax.axis_index("section"), lax.axis_index("tp"), lax.axis_index("dp")
    x, y = lax.div(tp, 4), lax.rem(tp, 4)
    lane = lax.rem(tp, 2)
    group = section * 8 + plane
    info = jnp.stack([group, section, plane, lane, x, y, tp]).astype(jnp.int32)
    turn = jnp.where(section == 0, 1, -1)
    count = jnp.arange(16, dtype=jnp.int32)
    order = lax.rem(x - turn * (count // 4) + 4, 4) * 4 + lax.rem(y - turn * (count % 4) + 4, 4)

    q_cols = w_query.shape[1]
    kv_cols = w_keyval.shape[1]
    w_all = lax.all_gather(jnp.concatenate([w_query, w_keyval], axis=1), SD, axis=0, tiled=False)

    part = w_out.shape[1] // 4
    w_cut = along(
        [lax.dynamic_slice_in_dim(w_out, lax.rem(y + k, 4) * part, part, 1) for k in range(4)], 0, 1
    )
    rows = x_decode.reshape(steps * requests, width)
    half_p, half_d = tokens // 2, rows.shape[0] // 2
    bias = cache_mask(page_table, cache_len[:, None], cache_pool.shape[1])
    blocks, (bias, *w_cut) = gather_tp(
        jnp.concatenate([x_prefill[:half_p], rows[:half_d]], axis=0),
        jnp.concatenate([x_prefill[half_p:], rows[half_d:]], axis=0),
        [bias, *w_cut],
    )
    wo_all = lax.all_gather(jnp.concatenate(w_cut, axis=0), SD, axis=0, tiled=False)
    kv_mine = project_keys(order, blocks, w_all, kv_cols, tokens)
    kv_lane = lax.ppermute(kv_mine, "tp", LANE)
    kv_core = lax.ppermute(kv_mine, "section", SWAP)
    kv_both = lax.ppermute(kv_mine, ST, BOTH)
    mine, kv_lane = lax.optimization_barrier((cache_pool[0], kv_lane))
    is_key = lane == 0
    own, other_core = (
        jnp.stack([jnp.where(is_key, p, q), jnp.where(is_key, q, p)])
        for p, q in ((kv_mine, kv_lane), (kv_core, kv_both))
    )
    kv, (q_pre, q_dec, new_mine) = gather_planes(
        own, other_core, project(order, blocks, w_all, q_cols, tokens)
    )
    new_lane = lax.ppermute(new_mine, "tp", LANE)
    other = lax.ppermute(mine, "tp", LANE)
    keys = jnp.where(is_key, new_mine, new_lane)
    values = jnp.where(is_key, new_lane, new_mine)

    kvs = collect(info, kv)
    attention = decode_attention(
        info, placement, q_dec, keys, values, bias, mine, other, kvs
    )
    attended = along([attention] * 4, 0, 1)
    parts = along(output_projection(info, attended, wo_all), 1, 0)
    prefill_out = prefill_attention(info, q_pre, kvs)
    prefill_out, *parts = lax.optimization_barrier((prefill_out, *parts))
    pieces = along(sum_parts(info, parts), 0, 1)
    decode_out = assemble(info, pieces).reshape(steps, requests, -1)
    return (prefill_out, decode_out)


def solution(mesh):
    return jax.shard_map(
        on_device,
        mesh=mesh,
        in_specs=(
            P(("section", "dp"), "tp"),
            P(None, ("section", "dp"), "tp"),
            P(("section", "dp"), "tp"),
            P(("section", "dp"), "tp"),
            P("tp", ("section", "dp")),
            P("tp", ("section", "dp"), None, None),
            P(),
            P(("section", "dp"), None),
            P(("section", "dp")),
        ),
        out_specs=(P(("section", "dp"), "tp"), P(None, ("section", "dp"), "tp")),
        check_vma=False,
    )
```
